256 devices in a mesh: gx: 8 (over x, core), gy: 4 (over y), gz: 8 (over z).
Axes of the slice: x: 4, y: 4, z: 8, core: 2. Of those that a mesh axis runs over, the one named last changes fastest.
Arguments:
- velocity: float32 [3, 128, 64, 1024], P(None, 'gx', 'gy', 'gz'), may hold values from -6 to 6
- gradients: bfloat16 [2, 3, 128, 64, 1024], P(None, None, 'gx', 'gy', 'gz'), may hold values from -6 to 6
- shift_x: int32 [2, 16, 8, 8], P(None, 'gx', 'gy', 'gz'), may hold values from -6 to 6
- shift_y: int32 [2, 16, 8, 8], P(None, 'gx', 'gy', 'gz'), may hold values from -6 to 6
- shift_z: int32 [2, 16, 8, 8], P(None, 'gx', 'gy', 'gz'), may hold values from -14 to 14
- fractions: int32 [2, 3, 16, 8, 8], P(None, None, 'gx', 'gy', 'gz'), may hold values from 0 to 7
Outputs:
- hess_vec: float32 [3, 128, 64, 1024], P(None, 'gx', 'gy', 'gz')
The draws below stay inside these ranges and needn't reach their ends.
All inputs are finite; a program needn't handle non-finite values.
Results may differ from the reference program's by a relative error of at most 0.0003.
Values sent between devices are 32-bit elements; how exact they have to be, the bound alone decides.
No kernel may reach another device: no remote copies, remote signals or barrier semaphores. Data moves between devices by JAX's collectives and lax.ppermute only.
A program may use at most 64 MiB of HBM per device.

```python
import jax
import jax.numpy as jnp
from jax import lax

BX = 8
BY = 8
BZ = 128
RX = 6
RY = 6
RZ = 14
STEPS = 2
NX = 128
NY = 64
NZ = 1024
NBX = 16
NBY = 8
NBZ = 8


def set_ends(array, rng, smallest, largest):
    place = [jax.random.randint(jax.random.fold_in(rng, axis), (), 0, length) for axis, length in enumerate(array.shape)]
    main_axis = array.shape.index(max(array.shape))
    neighbour = place[:main_axis] + [(place[main_axis] + 1) % array.shape[main_axis]] + place[main_axis + 1:]
    return array.at[tuple(place)].set(smallest).at[tuple(neighbour)].set(largest)


def level_of(rng, dims, pieces, least, high):
    loudness = 1.0
    for axis_at, blocks in pieces:
        heights = jax.random.uniform(jax.random.fold_in(jax.random.fold_in(rng, 6), axis_at), (blocks,), jnp.float32, least / len(pieces), high / len(pieces))
        loudness = loudness * jnp.repeat(jnp.exp(heights), dims[axis_at] // blocks).reshape((-1,) + (1,) * (len(dims) - 1 - axis_at))
    return loudness


def gaussian(own_key, shape, spread, bound, cuts=(), kind=jnp.bfloat16):
    array = jax.random.normal(own_key, shape, jnp.float32) * spread
    if len(cuts) > 0:
        array = level_of(own_key, shape, cuts, -0.22, 0.18) * array
    return jnp.clip(array, min=-bound, max=bound).astype(kind)


def setup_inputs(seed: int = 0) -> dict:
    seeds = jax.random.split(jax.random.key(seed), 7)
    velocity = gaussian(seeds[0], (3, NX, NY, NZ), 1.0, 6.0, ((1, 8), (2, 4), (3, 8)), jnp.float32)
    gradients = gaussian(seeds[1], (STEPS, 3, NX, NY, NZ), 1.0, 6.0, ((2, 8), (3, 4), (4, 8)))
    shift_x = set_ends(jax.random.randint(seeds[2], (STEPS, NBX, NBY, NBZ), 0 - RX, RX + 1), jax.random.fold_in(seeds[2], 1), 0 - RX, RX).astype(jnp.int32)
    shift_y = set_ends(jax.random.randint(seeds[3], (STEPS, NBX, NBY, NBZ), 0 - RY, RY + 1), jax.random.fold_in(seeds[3], 1), 0 - RY, RY).astype(jnp.int32)
    shift_z = set_ends(jax.random.randint(seeds[4], (STEPS, NBX, NBY, NBZ), 0 - RZ, RZ + 1), jax.random.fold_in(seeds[4], 1), 0 - RZ, RZ).astype(jnp.int32)
    fractions = set_ends(jax.random.randint(seeds[5], (STEPS, 3, NBX, NBY, NBZ), 0, 8), jax.random.fold_in(seeds[5], 1), 0, 7).astype(jnp.int32)
    return {"velocity": velocity, "gradients": gradients, "shift_x": shift_x, "shift_y": shift_y, "shift_z": shift_z, "fractions": fractions}


STEP_SIZE = 0.5
REG_WEIGHT = 0.1
LAPLACE_TAPS = (-205.0 / 72.0, 8.0 / 5.0, -1.0 / 5.0, 8.0 / 315.0, -1.0 / 560.0)


def cubic_weights(fractions):
    fraction = fractions.astype(jnp.float32) / 8.0
    squared = fraction * fraction
    cubed = squared * fraction
    taps = jnp.stack([0.5 * (2.0 * squared - cubed - fraction), 0.5 * (3.0 * cubed - 5.0 * squared + 2.0), 0.5 * (4.0 * squared - 3.0 * cubed + fraction), 0.5 * (cubed - squared)], axis=-1)
    return taps.reshape(3, -1, 4)


def block_starts(shift_x, shift_y, shift_z):
    count_x, count_y, count_z = shift_x.shape
    base_x = jnp.arange(count_x, dtype=jnp.int32)[:, None, None] * BX
    base_y = jnp.arange(count_y, dtype=jnp.int32)[None, :, None] * BY
    base_z = jnp.arange(count_z, dtype=jnp.int32)[None, None, :] * BZ
    start_x = (base_x + shift_x + (RX + 1)).astype(jnp.int32).reshape(-1)
    start_y = (base_y + shift_y + (RY + 1)).astype(jnp.int32).reshape(-1)
    start_z = (base_z + shift_z + (RZ + 1)).astype(jnp.int32).reshape(-1)
    return start_x, start_y, start_z


def apply_cubic(window, weight_x, weight_y, weight_z):
    span_z = window.shape[2] - 3
    along_z = sum(weight_z[a] * window[:, :, a:a + span_z] for a in range(4))
    span_y = window.shape[1] - 3
    along_y = sum(weight_y[a] * along_z[:, a:a + span_y, :] for a in range(4))
    span_x = window.shape[0] - 3
    return sum(weight_x[a] * along_y[a:a + span_x] for a in range(4))


def transpose_cubic(values, weight_x, weight_y, weight_z):
    along_x = sum(weight_x[a] * jnp.pad(values, ((a, 3 - a), (0, 0), (0, 0))) for a in range(4))
    along_y = sum(weight_y[a] * jnp.pad(along_x, ((0, 0), (a, 3 - a), (0, 0))) for a in range(4))
    return sum(weight_z[a] * jnp.pad(along_y, ((0, 0), (0, 0), (a, 3 - a))) for a in range(4))


def to_blocks(field):
    tile_x, tile_y, tile_z = field.shape
    split = field.reshape(tile_x // BX, BX, tile_y // BY, BY, tile_z // BZ, BZ)
    return split.transpose(0, 2, 4, 1, 3, 5).reshape(-1, BX, BY, BZ)


def from_blocks(blocks, tile_x, tile_y, tile_z):
    split = blocks.reshape(tile_x // BX, tile_y // BY, tile_z // BZ, BX, BY, BZ)
    return split.transpose(0, 3, 1, 4, 2, 5).reshape(tile_x, tile_y, tile_z)


def spread_blocks(field, start_x, start_y, start_z, weights):
    values = to_blocks(field)
    accumulated = jnp.zeros((field.shape[0] + 2 * (RX + 2), field.shape[1] + 2 * (RY + 2), field.shape[2] + 2 * (RZ + 2)), jnp.float32)

    def add_block(b, accumulated):
        window = transpose_cubic(values[b], weights[0, b], weights[1, b], weights[2, b])
        corner = (start_x[b], start_y[b], start_z[b])
        current = lax.dynamic_slice(accumulated, corner, window.shape)
        return lax.dynamic_update_slice(accumulated, current + window, corner)

    return lax.fori_loop(0, values.shape[0], add_block, accumulated)


def neg_laplacian(padded):
    tile_x = padded.shape[1] - 8
    tile_y = padded.shape[2] - 8
    tile_z = padded.shape[3] - 8

    def shifted(off_x, off_y, off_z):
        return padded[:, 4 + off_x:4 + off_x + tile_x, 4 + off_y:4 + off_y + tile_y, 4 + off_z:4 + off_z + tile_z]

    result = (3.0 * LAPLACE_TAPS[0]) * shifted(0, 0, 0)
    for k in range(1, 5):
        result = result + LAPLACE_TAPS[k] * (shifted(k, 0, 0) + shifted(-k, 0, 0) + shifted(0, k, 0) + shifted(0, -k, 0) + shifted(0, 0, k) + shifted(0, 0, -k))
    return -result


def advect(field, shift_x, shift_y, shift_z, fractions):
    padded = jnp.pad(field, ((RX + 2, RX + 2), (RY + 2, RY + 2), (RZ + 2, RZ + 2)))
    start_x, start_y, start_z = block_starts(shift_x, shift_y, shift_z)
    weights = cubic_weights(fractions)

    def one_block(block_items):
        corner_x, corner_y, corner_z, weight_x, weight_y, weight_z = block_items
        window = lax.dynamic_slice(padded, (corner_x, corner_y, corner_z), (BX + 3, BY + 3, BZ + 3))
        return apply_cubic(window, weight_x, weight_y, weight_z)

    blocks = lax.map(one_block, (start_x, start_y, start_z, weights[0], weights[1], weights[2]))
    return from_blocks(blocks, field.shape[0], field.shape[1], field.shape[2])


def advect_transposed(field, shift_x, shift_y, shift_z, fractions):
    start_x, start_y, start_z = block_starts(shift_x, shift_y, shift_z)
    weights = cubic_weights(fractions)
    accumulated = spread_blocks(field, start_x, start_y, start_z, weights)
    return accumulated[RX + 2:RX + 2 + field.shape[0], RY + 2:RY + 2 + field.shape[1], RZ + 2:RZ + 2 + field.shape[2]]


def reference(velocity, gradients, shift_x, shift_y, shift_z, fractions):
    state = jnp.zeros(velocity.shape[1:], jnp.float32)
    for k in range(STEPS):
        source = state + STEP_SIZE * jnp.sum(gradients[k].astype(jnp.float32) * velocity, axis=0)
        state = advect(source, shift_x[k], shift_y[k], shift_z[k], fractions[k])
    adjoint = state
    gauss_term = jnp.zeros_like(velocity)
    for k in reversed(range(STEPS)):
        adjoint = advect_transposed(adjoint, shift_x[k], shift_y[k], shift_z[k], fractions[k])
        gauss_term = gauss_term + STEP_SIZE * gradients[k].astype(jnp.float32) * adjoint[None]
    faces = jnp.pad(velocity, ((0, 0), (4, 4), (4, 4), (4, 4)))
    regular = REG_WEIGHT * neg_laplacian(faces)
    return regular + gauss_term
```

```python
import jax
import jax.numpy as jnp
from jax import lax
from jax.experimental import pallas as pl
from jax.experimental.pallas import tpu as pltpu
from jax.sharding import PartitionSpec as P

F32 = jnp.float32
LAPLACE_TAPS = (-205.0 / 72.0, 8.0 / 5.0, -1.0 / 5.0, 8.0 / 315.0, -1.0 / 560.0)
STEP_SIZE = 0.5
REG_WEIGHT = 0.1
T = 16
L = 128
META = 48

Z_S0, Z_S1, Z_V, Z_META, Z_ROWS = 0, 64, 96, 144, 152
Y_S0, Y_M0, Y_S1, Y_M1, Y_V, Y_META, Y_ROWS = 0, 256, 384, 512, 544, 736, 744
X_S0, X_M0, X_S1, X_M1, X_V, X_META, X_ROWS = 0, 768, 1152, 1408, 1472, 1664, 1688
R_E, R_ROWS = 512, 640


def lanes(rows=8):
    return lax.broadcasted_iota(jnp.int32, (rows, L), 1)


def subs():
    return lax.broadcasted_iota(jnp.int32, (8, L), 0)


def roll(x, amount):
    amount = amount % L
    return x if amount == 0 else pltpu.roll(x, amount, 1)


def tap_weights(f):
    e = f * 0.125
    e2 = e * e
    e3 = e2 * e
    return [
        0.5 * (2.0 * e2 - e3 - e),
        0.5 * (3.0 * e3 - 5.0 * e2 + 2.0),
        0.5 * (4.0 * e2 - 3.0 * e3 + e),
        0.5 * (e3 - e2),
    ]


def block_numbers(meta, row, step, ix, iy):
    at = ((step * 2 + ix) * 2 + iy) * 6
    shift = [meta[row, at + d].astype(jnp.int32) for d in range(3)]
    weights = [tap_weights(meta[row, at + 3 + d]) for d in range(3)]
    return shift, weights


def sources_kernel(v, g, sx, sy, sz, fr, s0, s1, up, down):
    lane = lanes(T)
    for x in range(T):
        vel = [v[c, x] for c in range(3)]
        for k, s in ((0, s0), (1, s1)):
            total = g[k, 0, x].astype(F32) * vel[0]
            for c in (1, 2):
                total = total + g[k, c, x].astype(F32) * vel[c]
            s[x] = STEP_SIZE * total
    quarter = lane // 32
    for j in range(4):
        a, b, c, d = s0[j], roll(s0[j + 4], 32), roll(s0[j + 8], 64), roll(s0[j + 12], 96)
        rows = pl.ds(Z_S0 + j * T, T)
        up[rows] = jnp.where(quarter == 3, a, jnp.where(quarter == 1, c, jnp.where(quarter == 0, b, d)))
        down[rows] = jnp.where(quarter == 0, a, jnp.where(quarter == 2, c, jnp.where(quarter == 1, b, d)))
    eighth = lane // 16
    for h in range(2):
        u, d = s1[8 * h], s1[8 * h]
        for i in range(1, 8):
            r = roll(s1[8 * h + i], 16 * i)
            u = jnp.where(eighth == (7 + i) % 8, r, u)
            d = jnp.where(eighth == i, r, d)
        up[pl.ds(Z_S1 + h * T, T)] = u
        down[pl.ds(Z_S1 + h * T, T)] = d
    piece = lane // 8
    for c in range(3):
        u, d = v[c, 0], v[c, 0]
        for x in range(1, T):
            r = roll(v[c, x], 8 * x)
            u = jnp.where(piece == (15 + x) % 16, r, u)
            d = jnp.where(piece == x, r, d)
        up[pl.ds(Z_V + c * T, T)] = u
        down[pl.ds(Z_V + c * T, T)] = d
    lane = lanes()
    row = jnp.zeros((8, L), jnp.int32)
    for k in range(2):
        for ix in range(2):
            for iy in range(2):
                at = ((k * 2 + ix) * 2 + iy) * 6
                numbers = [sx[k, ix, iy, 0], sy[k, ix, iy, 0], sz[k, ix, iy, 0]]
                numbers += [fr[k, d, ix, iy, 0] for d in range(3)]
                for n, number in enumerate(numbers):
                    row = jnp.where(lane == at + n, number, row)
    up[pl.ds(Z_META, 8)] = row.astype(F32)
    down[pl.ds(Z_META, 8)] = row.astype(F32)


def y_message_kernel(s0, s1, v, own, low, high, up, down):
    lane = lanes(T)
    even = (lane // 32) % 2 == 0
    for x in range(T):
        for out in (up, down):
            out[pl.ds(Y_S0 + x * T, T)] = s0[x]
        up[pl.ds(Y_S1 + x * 8, 8)] = s1[x, 8:16]
        down[pl.ds(Y_S1 + x * 8, 8)] = s1[x, 0:8]
    for j in range(4):
        a, b = low[pl.ds(Z_S0 + j * T, T)], high[pl.ds(Z_S0 + j * T, T)]
        first = jnp.where(even, b, a)
        second = roll(jnp.where(even, a, b), -32)
        for out in (up, down):
            out[pl.ds(Y_M0 + j * T, T)] = first
            out[pl.ds(Y_M0 + (j + 4) * T, T)] = second
    even = (lane // 16) % 2 == 0
    for h in range(2):
        a, b = low[pl.ds(Z_S1 + h * T, T)], high[pl.ds(Z_S1 + h * T, T)]
        for j, value in enumerate((jnp.where(even, b, a), roll(jnp.where(even, a, b), -16))):
            up[pl.ds(Y_M1 + (h * 2 + j) * 8, 8)] = value[8:16]
            down[pl.ds(Y_M1 + (h * 2 + j) * 8, 8)] = value[0:8]
    first_half = subs() < 4
    for c in range(3):
        for x in range(8):
            rows = pl.ds(Y_V + (c * 8 + x) * 8, 8)
            up[rows] = jnp.where(first_half, pltpu.roll(v[c, x + 8, 8:16], 4, 0), v[c, x, 8:16])
            down[rows] = jnp.where(first_half, v[c, x, 0:8], pltpu.roll(v[c, x + 8, 0:8], 4, 0))
    sub = subs()
    meta = [ref[pl.ds(Z_META, 8)] for ref in (low, own, high)]
    row = jnp.where(sub == 0, meta[0], jnp.where(sub == 1, meta[1], meta[2]))
    up[pl.ds(Y_META, 8)] = row
    down[pl.ds(Y_META, 8)] = row


def x_message_kernel(own_up, own_down, low, high, v, up, down):
    for n, (start, planes, to) in enumerate(((Y_S0, T, X_S0), (Y_M0, 8, X_M0))):
        for x in range(planes):
            for at, ref in enumerate((low, own_up, high)):
                value = ref[pl.ds(start + x * T, T)]
                for out in (up, down):
                    out[pl.ds(to + x * 48 + at * T, T)] = value
    for h, out in ((1, up), (0, down)):
        for x in range(8):
            for at, ref in enumerate((low, own_down, own_up, high)):
                out[pl.ds(X_S1 + x * 32 + at * 8, 8)] = ref[pl.ds(Y_S1 + (8 * h + x) * 8, 8)]
        for j in range(2):
            for at, ref in enumerate((low, own_down, own_up, high)):
                out[pl.ds(X_M1 + j * 32 + at * 8, 8)] = ref[pl.ds(Y_M1 + (h * 2 + j) * 8, 8)]
        for c in range(3):
            for i in range(4):
                out[pl.ds(X_V + (c * 4 + i) * T, T)] = v[c, 12 * h + i]
        for at, ref in enumerate((low, own_up, high)):
            out[pl.ds(X_META + at * 8, 8)] = ref[pl.ds(Y_META, 8)]


def gather_xy(ref, x0, y0, wx, wy):
    planes = []
    for i in range(11):
        plane = wy[0] * ref[x0 + i, pl.ds(y0, 8), :]
        for t in range(1, 4):
            plane = plane + wy[t] * ref[x0 + i, pl.ds(y0 + t, 8), :]
        planes.append(plane)
    out = []
    for i in range(8):
        value = wx[0] * planes[i]
        for t in range(1, 4):
            value = value + wx[t] * planes[i + t]
        out.append(value)
    return out


def scatter_xy(ref, vals, x0, y0, wx, wy):
    sub = subs()
    low_w = [jnp.where(sub >= t, wy[t], 0.0) for t in range(4)]
    high_w = [jnp.where(sub < t, wy[t], 0.0) for t in range(4)]
    pairs = []
    for value in vals:
        first, second = wy[0] * value, None
        for t in range(1, 4):
            turned = pltpu.roll(value, t, 0)
            first = first + low_w[t] * turned
            second = high_w[t] * turned if second is None else second + high_w[t] * turned
        pairs.append((first, second))
    for p in range(11):
        for half in range(2):
            total = None
            for t in range(4):
                if 0 <= p - t < 8:
                    term = wx[t] * pairs[p - t][half]
                    total = term if total is None else total + term
            rows = pl.ds(y0 + 8 * half, 8)
            ref[x0 + p, rows, :] = ref[x0 + p, rows, :] + total


def block_of(b):
    return (b + 1) // 2, (b + 1) % 2


def steps_kernel(own_up, own_down, low, high, ra, up, down, clo, chi, a1, e1, re, meta, sem):
    lane = lanes()
    upper = lane >= 64
    copies = []
    for n, ref in enumerate((low, own_up, high)):
        copy = pltpu.make_async_copy(ref.at[pl.ds(X_META, 24)], meta.at[pl.ds(n * 24, 24)], sem.at[n])
        copy.start()
        copies.append(copy)
    upper48 = lanes(48) >= 64
    for n, ref in enumerate((low, own_up, high)):

        def assemble(x, _, n=n, ref=ref):
            m = ref[pl.ds(pl.multiple_of(X_M0 + x * 48, 8), 48)]
            for half, e in ((0, m), (1, roll(m, 64))):
                a = ref[pl.ds(pl.multiple_of(X_S0 + (x + 8 * half) * 48, 8), 48)]
                clo[n * T + 8 * half + x] = jnp.where(upper48, e, a)
                chi[n * T + 8 * half + x] = jnp.where(upper48, a, e)
            return 0

        lax.fori_loop(0, 8, assemble, 0)
    for n, ref in enumerate((low, own_down, own_up, high)):
        for x in range(8):
            a1[n * 8 + x] = ref[pl.ds(X_S1 + x * 32, 32)]
            e1[n * 8 + x] = roll(ref[pl.ds(X_M1 + (x % 2) * 32, 32)], -32 * (x // 2))
    ra[...] = jnp.zeros(ra.shape, F32)
    re[...] = jnp.zeros(re.shape, F32)
    for copy in copies:
        copy.wait()

    def first_step(i, _):
        bx, by = i // 4, i % 4
        (slot_x, ix), (slot_y, iy) = block_of(bx), block_of(by)
        row = slot_x * 24 + slot_y * 8
        edges = []
        for n, ref in ((0, clo), (2, chi)):
            (a, b, c), (wx, wy, wz) = block_numbers(meta, row + n, 0, ix, iy)
            values = gather_xy(ref, bx * 8 + 7 + a, by * 8 + 7 + b, wx, wy)
            turns = [(1 - c - t) & 127 for t in range(4)]
            edges.append([sum(wz[t] * pltpu.roll(value, turns[t], 1) for t in range(4)) for value in values])
        (a, b, c), (wx, wy, wz) = block_numbers(meta, row + 1, 0, ix, iy)
        x0, y0 = bx * 8 + 7 + a, by * 8 + 7 + b
        lows = gather_xy(clo, x0, y0, wx, wy)
        highs = gather_xy(chi, x0, y0, wx, wy)
        masks = [jnp.logical_xor(((lane - (c + t - 1)) & -128) == 0, upper) for t in range(4)]
        turns = [(1 - c - t) & 127 for t in range(4)]
        rows = pl.ds(pl.multiple_of(by * 8, 8), 8)
        for p in range(8):
            value = sum(wz[t] * pltpu.roll(jnp.where(masks[t], lows[p], highs[p]), turns[t], 1) for t in range(4))
            x = bx * 8 + p
            a1[x, rows, :] = a1[x, rows, :] + value
            e1[x, rows, :] = e1[x, rows, :] + jnp.where(upper, edges[0][p], edges[1][p])
        return 0

    lax.fori_loop(0, 16, first_step, 0)

    def second_step(i, _):
        ix, iy = i // 2, i % 2
        (a, b, c), (wx, wy, wz) = block_numbers(meta, 24 + 8 + 1, 1, ix, iy)
        x0, y0 = ix * 8 + 7 + a, iy * 8 + 7 + b
        inner = gather_xy(a1, x0, y0, wx, wy)
        outer = gather_xy(e1, x0, y0, wx, wy)
        masks = [((lane - (c + t - 1)) & -128) == 0 for t in range(4)]
        turns = [(1 - c - t) & 127 for t in range(4)]
        back = [(c + t - 1) & 127 for t in range(4)]
        in_w = [jnp.where(masks[t], wz[t], 0.0) for t in range(4)]
        out_w = [jnp.where(masks[t], 0.0, wz[t]) for t in range(4)]
        to_a, to_e = [], []
        for p in range(8):
            state = sum(wz[t] * pltpu.roll(jnp.where(masks[t], inner[p], outer[p]), turns[t], 1) for t in range(4))
            turned = [pltpu.roll(state, back[t], 1) for t in range(4)]
            to_a.append(sum(in_w[t] * turned[t] for t in range(4)))
            to_e.append(sum(out_w[t] * turned[t] for t in range(4)))
        scatter_xy(ra, to_a, x0, y0, wx, wy)
        scatter_xy(re, to_e, x0, y0, wx, wy)
        return 0

    lax.fori_loop(0, 4, second_step, 0)

    wide = lanes(32)
    quarter = ((wide + 16) & 127) // 32
    for h in range(2):
        for x in range(4):
            u, d = None, None
            for g in range(4):
                a, e = ra[16 * h + 4 * g + x, 0:32], re[16 * h + 4 * g + x, 0:32]
                rise = roll(jnp.where(wide >= 64, a, e), 32 * g)
                fall = roll(jnp.where(wide >= 64, e, a), 32 * g)
                u = rise if g == 0 else jnp.where(quarter == g, rise, u)
                d = fall if g == 0 else jnp.where(quarter == g, fall, d)
            up[h * 4 + x] = u
            down[h * 4 + x] = d


def sum_z_kernel(ra, own_up, own_down, low, high, up, down):
    wide = lanes(32)
    even = (wide // 16) % 2 == 0
    valid = (wide < 16) | (wide >= 112)
    for h in range(2):
        for x in range(4):
            a, b = low[h * 4 + x], high[h * 4 + x]
            inner = jnp.where(even, a, b)
            outer = jnp.where(even, own_up[h * 4 + x], own_down[h * 4 + x]) + jnp.where(even, b, a)
            down[pl.ds(R_E + (h * 4 + x) * T, T)] = outer[0:16]
            up[pl.ds(R_E + (h * 4 + x) * T, T)] = outer[16:32]
            for g in range(4):
                at = 16 * h + 4 * g + x
                value = ra[at, 0:32] + jnp.where(valid, roll(inner, -32 * g), 0.0)
                down[pl.ds(at * T, T)] = value[0:16]
                up[pl.ds(at * T, T)] = value[16:32]


def sum_y_kernel(own_up, own_down, low, high, up, down):
    for h, out in ((0, down), (1, up)):
        for start, planes in ((0, 16), (R_E, 4)):
            for x in range(planes):
                rows = pl.ds(start + (h * planes + x) * T, T)
                out[pl.ds(start + x * 32, T)] = own_down[rows] + low[rows]
                out[pl.ds(start + x * 32 + T, T)] = own_up[rows] + high[rows]


def last_step_kernel(own_up, own_down, low, high, meta_low, meta_own, meta_high, g, reg, out, a1, e1, acc, meta, sem):
    copies = []
    for n, ref in enumerate((meta_low, meta_own, meta_high)):
        copy = pltpu.make_async_copy(ref.at[pl.ds(X_META, 24)], meta.at[pl.ds(n * 24, 24)], sem.at[n])
        copy.start()
        copies.append(copy)
    wide = lanes(32)
    valid = (wide < 16) | (wide >= 112)
    for h, (mine, other) in enumerate(((own_down, low), (own_up, high))):
        for x in range(16):
            rows = pl.ds(x * 32, 32)
            a1[16 * h + x] = mine[rows] + other[rows]
        for x in range(4):
            rows = pl.ds(R_E + x * 32, 32)
            packed = mine[rows] + other[rows]
            for q in range(4):
                e1[16 * h + 4 * q + x] = jnp.where(valid, roll(packed, -32 * q), 0.0)
    acc[...] = jnp.zeros(acc.shape, F32)
    for copy in copies:
        copy.wait()
    lane = lanes()
    upper = lane >= 64

    def step(i, _):
        bx, by = i // 4, i % 4
        (slot_x, ix), (slot_y, iy) = block_of(bx), block_of(by)
        row = slot_x * 24 + slot_y * 8
        rows = pl.ds(pl.multiple_of(by * 8, 8), 8)
        inner = [a1[bx * 8 + p, rows, :] for p in range(8)]
        outer = [e1[bx * 8 + p, rows, :] for p in range(8)]
        for n in range(3):
            (a, b, c), (wx, wy, wz) = block_numbers(meta, row + n, 0, ix, iy)
            back = [(c + t - 1) & 127 for t in range(4)]
            if n == 1:
                w = [jnp.where(((lane - (c + t - 1)) & -128) == 0, wz[t], 0.0) for t in range(4)]
                values = inner
            else:
                keep = upper if n == 2 else jnp.logical_not(upper)
                w = [jnp.where(keep, wz[t], 0.0) for t in range(4)]
                values = [jnp.where(upper if n == 0 else jnp.logical_not(upper), value, 0.0) for value in outer]
            moved = [sum(w[t] * pltpu.roll(value, back[t], 1) for t in range(4)) for value in values]
            scatter_xy(acc, moved, bx * 8 + 7 + a, by * 8 + 7 + b, wx, wy)
        return 0

    lax.fori_loop(0, 16, step, 0)
    for x in range(T):
        first, second = acc[16 + x, 16:32], a1[8 + x, 8:24]
        for c in range(3):
            out[c, x] = reg[c, x] + STEP_SIZE * (g[1, c, x].astype(F32) * second + g[0, c, x].astype(F32) * first)


def laplace_kernel(v, zlow, zhigh, ylow, yhigh, xlow, xhigh, out, w):
    lane = lanes(T)
    half = (lane & 4) == 0
    sides = [-REG_WEIGHT * t for t in LAPLACE_TAPS]
    for c in range(3):
        rows = pl.ds(Z_V + c * T, T)
        faces = jnp.where(half, zhigh[rows], zlow[rows])
        for i in range(4):
            rows = pl.ds(X_V + (c * 4 + i) * T, T)
            w[i, 8:24] = xlow[rows]
            w[20 + i, 8:24] = xhigh[rows]
        for x in range(8):
            rows = pl.ds(Y_V + (c * 8 + x) * 8, 8)
            a, b = ylow[rows], yhigh[rows]
            w[4 + x, 0:8] = a
            w[12 + x, 0:8] = pltpu.roll(a, 4, 0)
            w[4 + x, 24:32] = b
            w[12 + x, 24:32] = pltpu.roll(b, 4, 0)
        for x in range(T):
            w[4 + x, 8:24] = v[c, x]
        for x in range(T):
            here = v[c, x]
            edge = roll(faces, -8 * x)
            total = 3.0 * sides[0] * here
            for k in range(1, 5):
                near = roll(jnp.where(lane < k, edge, here), -k) + roll(jnp.where(lane >= L - k, edge, here), k)
                near = near + w[4 + x - k, 8:24] + w[4 + x + k, 8:24]
                near = near + w[4 + x, 8 - k : 24 - k] + w[4 + x, 8 + k : 24 + k]
                total = total + sides[k] * near
            out[c, x] = total


VMEM = pl.BlockSpec(memory_space=pltpu.VMEM)
SMEM = pl.BlockSpec(memory_space=pltpu.SMEM)


def call(kernel, args, outs, scratch=(), smem=(), cost=20000):
    specs = [SMEM if i in smem else VMEM for i in range(len(args))]
    shapes = [jax.ShapeDtypeStruct(s, F32) for s in outs]
    return pl.pallas_call(
        kernel,
        out_shape=shapes,
        in_specs=specs,
        out_specs=[VMEM] * len(shapes),
        scratch_shapes=list(scratch),
        compiler_params=pltpu.CompilerParams(vmem_limit_bytes=24 * 1024 * 1024),
        cost_estimate=pl.CostEstimate(flops=cost, bytes_accessed=cost, transcendentals=0),
    )(*args)


def exchange(up, down, axis):
    n = lax.axis_size(axis)
    rise = [(i, i + 1) for i in range(n - 1)]
    fall = [(j, i) for i, j in rise]
    return lax.ppermute(up, axis, rise), lax.ppermute(down, axis, fall)


def body(velocity, gradients, shift_x, shift_y, shift_z, fractions):
    v, g = velocity, gradients
    tile = (T, T, L)
    s0, s1, zup, zdown = call(
        sources_kernel,
        (v, g, shift_x, shift_y, shift_z, fractions),
        [tile, tile, (Z_ROWS, L), (Z_ROWS, L)],
        smem=(2, 3, 4, 5),
    )
    zlow, zhigh = exchange(zup, zdown, "gz")
    yup, ydown = call(y_message_kernel, (s0, s1, v, zup, zlow, zhigh), [(Y_ROWS, L)] * 2)
    ylow, yhigh = exchange(yup, ydown, "gy")
    xup, xdown = call(x_message_kernel, (yup, ydown, ylow, yhigh, v), [(X_ROWS, L)] * 2)
    xlow, xhigh = exchange(xup, xdown, "gx")
    meta = [pltpu.SMEM((72, L), F32), pltpu.SemaphoreType.DMA((3,))]
    vm = lambda *s: pltpu.VMEM(s, F32)
    ra, zup, zdown = call(
        steps_kernel,
        (xup, xdown, xlow, xhigh),
        [(32, 40, L), (8, 32, L), (8, 32, L)],
        scratch=[vm(48, 48, L), vm(48, 48, L), vm(32, 32, L), vm(32, 32, L), vm(32, 40, L)] + meta,
    )
    (reg,) = call(
        laplace_kernel, (v, zlow, zhigh, ylow, yhigh, xlow, xhigh), [v.shape], scratch=[vm(24, 32, L)], cost=4000000
    )
    low, high = exchange(zup, zdown, "gz")
    up, down = call(sum_z_kernel, (ra, zup, zdown, low, high), [(R_ROWS, L)] * 2)
    low, high = exchange(up, down, "gy")
    up, down = call(sum_y_kernel, (up, down, low, high), [(R_ROWS, L)] * 2)
    low, high = exchange(up, down, "gx")
    (out,) = call(
        last_step_kernel,
        (up, down, low, high, xlow, xup, xhigh, g, reg),
        [v.shape],
        scratch=[vm(32, 32, L), vm(32, 32, L), vm(48, 56, L)] + meta,
    )
    return out


def solution(mesh):
    in_specs = (
        P(None, "gx", "gy", "gz"),
        P(None, None, "gx", "gy", "gz"),
        P(None, "gx", "gy", "gz"),
        P(None, "gx", "gy", "gz"),
        P(None, "gx", "gy", "gz"),
        P(None, None, "gx", "gy", "gz"),
    )
    out_specs = P(None, "gx", "gy", "gz")
    return jax.shard_map(body, mesh=mesh, in_specs=in_specs, out_specs=out_specs, check_vma=False)
```

```python
import jax
import jax.numpy as jnp
from jax import lax
from jax.experimental import pallas as pl
from jax.experimental.pallas import tpu as pltpu
from jax.sharding import PartitionSpec as P

F32 = jnp.float32
LAPLACE_TAPS = (-205.0 / 72.0, 8.0 / 5.0, -1.0 / 5.0, 8.0 / 315.0, -1.0 / 560.0)
STEP_SIZE = 0.5
REG_WEIGHT = 0.1
T = 16
L = 128
META = 48

Z_S0, Z_S1, Z_V, Z_META, Z_ROWS = 0, 64, 96, 144, 152
Y_S0, Y_M0, Y_S1, Y_M1, Y_V, Y_META, Y_ROWS = 0, 256, 384, 512, 544, 736, 744
X_S0, X_M0, X_S1, X_M1, X_V, X_META, X_ROWS = 0, 768, 1152, 1408, 1472, 1664, 1688
R_E, R_ROWS = 512, 640


def lanes(rows=8):
    return lax.broadcasted_iota(jnp.int32, (rows, L), 1)


def subs():
    return lax.broadcasted_iota(jnp.int32, (8, L), 0)


def roll(x, amount):
    amount = amount % L
    return x if amount == 0 else pltpu.roll(x, amount, 1)


def tap_weights(f):
    e = f * 0.125
    e2 = e * e
    e3 = e2 * e
    return [
        0.5 * (2.0 * e2 - e3 - e),
        0.5 * (3.0 * e3 - 5.0 * e2 + 2.0),
        0.5 * (4.0 * e2 - 3.0 * e3 + e),
        0.5 * (e3 - e2),
    ]


def block_numbers(meta, row, step, ix, iy, keep=None):
    at = ((step * 2 + ix) * 2 + iy) * 6
    numbers = [meta[row, at + d] for d in range(6)]
    if keep is not None:
        numbers = [number * keep for number in numbers]
    return [n.astype(jnp.int32) for n in numbers[:3]], [tap_weights(n) for n in numbers[3:]]


def inside(axis):
    i, n = lax.axis_index(axis), lax.axis_size(axis)
    return jnp.where(i > 0, 1.0, 0.0).astype(F32), jnp.where(i < n - 1, 1.0, 0.0).astype(F32)


def sources_kernel(v_hbm, g_hbm, sx_hbm, sy_hbm, sz_hbm, fr_hbm, s0, s1, up, down, v, g, sx, sy, sz, fr, sem, small_sem):
    copies = []
    for q in range(4):
        part = pl.ds(4 * q, 4)
        copies.append(pltpu.make_async_copy(v_hbm.at[:, part], v.at[:, part], sem.at[2 * q]))
        copies.append(pltpu.make_async_copy(g_hbm.at[:, :, part], g.at[:, :, part], sem.at[2 * q + 1]))
    small = [
        pltpu.make_async_copy(a, b, small_sem.at[n])
        for n, (a, b) in enumerate(((sx_hbm, sx), (sy_hbm, sy), (sz_hbm, sz), (fr_hbm, fr)))
    ]
    for copy in copies + small:
        copy.start()
    lane = lanes(T)
    for x in range(T):
        if x % 4 == 0:
            copies[x // 2].wait()
            copies[x // 2 + 1].wait()
        vel = [v[c, x] for c in range(3)]
        for k, s in ((0, s0), (1, s1)):
            total = g[k, 0, x].astype(F32) * vel[0]
            for c in (1, 2):
                total = total + g[k, c, x].astype(F32) * vel[c]
            s[x] = STEP_SIZE * total
    quarter = lane // 32
    for j in range(4):
        a, b, c, d = s0[j], roll(s0[j + 4], 32), roll(s0[j + 8], 64), roll(s0[j + 12], 96)
        rows = pl.ds(Z_S0 + j * T, T)
        up[rows] = jnp.where(quarter == 3, a, jnp.where(quarter == 1, c, jnp.where(quarter == 0, b, d)))
        down[rows] = jnp.where(quarter == 0, a, jnp.where(quarter == 2, c, jnp.where(quarter == 1, b, d)))
    eighth = lane // 16
    for h in range(2):
        u, d = s1[8 * h], s1[8 * h]
        for i in range(1, 8):
            r = roll(s1[8 * h + i], 16 * i)
            u = jnp.where(eighth == (7 + i) % 8, r, u)
            d = jnp.where(eighth == i, r, d)
        up[pl.ds(Z_S1 + h * T, T)] = u
        down[pl.ds(Z_S1 + h * T, T)] = d
    piece = lane // 8
    for c in range(3):
        u, d = v[c, 0], v[c, 0]
        for x in range(1, T):
            r = roll(v[c, x], 8 * x)
            u = jnp.where(piece == (15 + x) % 16, r, u)
            d = jnp.where(piece == x, r, d)
        up[pl.ds(Z_V + c * T, T)] = u
        down[pl.ds(Z_V + c * T, T)] = d
    lane = lanes()
    for copy in small:
        copy.wait()
    row = jnp.zeros((8, L), jnp.int32)
    for k in range(2):
        for ix in range(2):
            for iy in range(2):
                at = ((k * 2 + ix) * 2 + iy) * 6
                numbers = [sx[k, ix, 0, iy], sy[k, ix, 0, iy], sz[k, ix, 0, iy]]
                numbers += [fr[k, ix, iy, 0, d] for d in range(3)]
                for n, number in enumerate(numbers):
                    row = jnp.where(lane == at + n, number, row)
    up[pl.ds(Z_META, 8)] = row.astype(F32)
    down[pl.ds(Z_META, 8)] = row.astype(F32)


def y_message_kernel(s0, s1, v, own, low, high, up, down):
    low_in, high_in = inside("gz")
    lane = lanes(T)
    even = (lane // 32) % 2 == 0
    for x in range(T):
        for out in (up, down):
            out[pl.ds(Y_S0 + x * T, T)] = s0[x]
        up[pl.ds(Y_S1 + x * 8, 8)] = s1[x, 8:16]
        down[pl.ds(Y_S1 + x * 8, 8)] = s1[x, 0:8]
    for j in range(4):
        a, b = low_in * low[pl.ds(Z_S0 + j * T, T)], high_in * high[pl.ds(Z_S0 + j * T, T)]
        first = jnp.where(even, b, a)
        second = roll(jnp.where(even, a, b), -32)
        for out in (up, down):
            out[pl.ds(Y_M0 + j * T, T)] = first
            out[pl.ds(Y_M0 + (j + 4) * T, T)] = second
    even = (lane // 16) % 2 == 0
    for h in range(2):
        a, b = low_in * low[pl.ds(Z_S1 + h * T, T)], high_in * high[pl.ds(Z_S1 + h * T, T)]
        for j, value in enumerate((jnp.where(even, b, a), roll(jnp.where(even, a, b), -16))):
            up[pl.ds(Y_M1 + (h * 2 + j) * 8, 8)] = value[8:16]
            down[pl.ds(Y_M1 + (h * 2 + j) * 8, 8)] = value[0:8]
    first_half = subs() < 4
    for c in range(3):
        for x in range(8):
            rows = pl.ds(Y_V + (c * 8 + x) * 8, 8)
            up[rows] = jnp.where(first_half, pltpu.roll(v[c, x + 8, 8:16], 4, 0), v[c, x, 8:16])
            down[rows] = jnp.where(first_half, v[c, x, 0:8], pltpu.roll(v[c, x + 8, 0:8], 4, 0))
    sub = subs()
    meta = [ref[pl.ds(Z_META, 8)] for ref in (low, own, high)]
    row = jnp.where(sub == 0, low_in * meta[0], jnp.where(sub == 1, meta[1], high_in * meta[2]))
    up[pl.ds(Y_META, 8)] = row
    down[pl.ds(Y_META, 8)] = row


def x_message_kernel(own_up, own_down, low, high, v, up, down):
    low_in, high_in = inside("gy")

    def take(ref, rows):
        value = ref[rows]
        return low_in * value if ref is low else high_in * value if ref is high else value

    for n, (start, planes, to) in enumerate(((Y_S0, T, X_S0), (Y_M0, 8, X_M0))):
        for x in range(planes):
            for at, ref in enumerate((low, own_up, high)):
                value = take(ref, pl.ds(start + x * T, T))
                for out in (up, down):
                    out[pl.ds(to + x * 48 + at * T, T)] = value
    for h, out in ((1, up), (0, down)):
        for x in range(8):
            for at, ref in enumerate((low, own_down, own_up, high)):
                out[pl.ds(X_S1 + x * 32 + at * 8, 8)] = take(ref, pl.ds(Y_S1 + (8 * h + x) * 8, 8))
        for j in range(2):
            for at, ref in enumerate((low, own_down, own_up, high)):
                out[pl.ds(X_M1 + j * 32 + at * 8, 8)] = take(ref, pl.ds(Y_M1 + (h * 2 + j) * 8, 8))
        for c in range(3):
            for i in range(4):
                out[pl.ds(X_V + (c * 4 + i) * T, T)] = v[c, 12 * h + i]
        for at, ref in enumerate((low, own_up, high)):
            out[pl.ds(X_META + at * 8, 8)] = take(ref, pl.ds(Y_META, 8))


def gather_xy(ref, x0, y0, wx, wy):
    planes = []
    for i in range(11):
        plane = wy[0] * ref[x0 + i, pl.ds(y0, 8), :]
        for t in range(1, 4):
            plane = plane + wy[t] * ref[x0 + i, pl.ds(y0 + t, 8), :]
        planes.append(plane)
    out = []
    for i in range(8):
        value = wx[0] * planes[i]
        for t in range(1, 4):
            value = value + wx[t] * planes[i + t]
        out.append(value)
    return out


def scatter_xy(ref, vals, x0, y0, wx, wy):
    sub = subs()
    low_w = [jnp.where(sub >= t, wy[t], 0.0) for t in range(4)]
    high_w = [jnp.where(sub < t, wy[t], 0.0) for t in range(4)]
    pairs = []
    for value in vals:
        first, second = wy[0] * value, None
        for t in range(1, 4):
            turned = pltpu.roll(value, t, 0)
            first = first + low_w[t] * turned
            second = high_w[t] * turned if second is None else second + high_w[t] * turned
        pairs.append((first, second))
    for p in range(11):
        for half in range(2):
            total = None
            for t in range(4):
                if 0 <= p - t < 8:
                    term = wx[t] * pairs[p - t][half]
                    total = term if total is None else total + term
            rows = pl.ds(y0 + 8 * half, 8)
            ref[x0 + p, rows, :] = ref[x0 + p, rows, :] + total


def block_of(b):
    return (b + 1) // 2, (b + 1) % 2


def steps_kernel(own_up, own_down, low, high, ra, up, down, clo, chi, a1, e1, re, meta, sem):
    low_in, high_in = inside("gx")
    lane = lanes()
    upper = lane >= 64
    copies = []
    for n, ref in enumerate((low, own_up, high)):
        copy = pltpu.make_async_copy(ref.at[pl.ds(X_META, 24)], meta.at[pl.ds(n * 24, 24)], sem.at[n])
        copy.start()
        copies.append(copy)
    upper48 = lanes(48) >= 64
    for n, (ref, keep) in enumerate(((low, low_in), (own_up, None), (high, high_in))):

        def assemble(x, _, n=n, ref=ref, keep=keep):
            m = ref[pl.ds(pl.multiple_of(X_M0 + x * 48, 8), 48)]
            m = m if keep is None else keep * m
            for half, e in ((0, m), (1, roll(m, 64))):
                a = ref[pl.ds(pl.multiple_of(X_S0 + (x + 8 * half) * 48, 8), 48)]
                a = a if keep is None else keep * a
                clo[n * T + 8 * half + x] = jnp.where(upper48, e, a)
                chi[n * T + 8 * half + x] = jnp.where(upper48, a, e)
            return 0

        lax.fori_loop(0, 8, assemble, 0)
    for n, (ref, keep) in enumerate(((low, low_in), (own_down, None), (own_up, None), (high, high_in))):
        for x in range(8):
            a = ref[pl.ds(X_S1 + x * 32, 32)]
            e = roll(ref[pl.ds(X_M1 + (x % 2) * 32, 32)], -32 * (x // 2))
            a1[n * 8 + x] = a if keep is None else keep * a
            e1[n * 8 + x] = e if keep is None else keep * e
    ra[...] = jnp.zeros(ra.shape, F32)
    re[...] = jnp.zeros(re.shape, F32)
    for copy in copies:
        copy.wait()

    def first_step(i, _):
        bx, by = i // 4, i % 4
        (slot_x, ix), (slot_y, iy) = block_of(bx), block_of(by)
        row = slot_x * 24 + slot_y * 8
        keep = jnp.where(slot_x == 0, low_in, jnp.where(slot_x == 2, high_in, 1.0))
        edges = []
        for n, ref in ((0, clo), (2, chi)):
            (a, b, c), (wx, wy, wz) = block_numbers(meta, row + n, 0, ix, iy, keep)
            values = gather_xy(ref, bx * 8 + 7 + a, by * 8 + 7 + b, wx, wy)
            turns = [(1 - c - t) & 127 for t in range(4)]
            edges.append([sum(wz[t] * pltpu.roll(value, turns[t], 1) for t in range(4)) for value in values])
        (a, b, c), (wx, wy, wz) = block_numbers(meta, row + 1, 0, ix, iy, keep)
        x0, y0 = bx * 8 + 7 + a, by * 8 + 7 + b
        lows = gather_xy(clo, x0, y0, wx, wy)
        highs = gather_xy(chi, x0, y0, wx, wy)
        masks = [jnp.logical_xor(((lane - (c + t - 1)) & -128) == 0, upper) for t in range(4)]
        turns = [(1 - c - t) & 127 for t in range(4)]
        rows = pl.ds(pl.multiple_of(by * 8, 8), 8)
        for p in range(8):
            value = sum(wz[t] * pltpu.roll(jnp.where(masks[t], lows[p], highs[p]), turns[t], 1) for t in range(4))
            x = bx * 8 + p
            a1[x, rows, :] = a1[x, rows, :] + value
            e1[x, rows, :] = e1[x, rows, :] + jnp.where(upper, edges[0][p], edges[1][p])
        return 0

    lax.fori_loop(0, 16, first_step, 0)

    def second_step(i, _):
        ix, iy = i // 2, i % 2
        (a, b, c), (wx, wy, wz) = block_numbers(meta, 24 + 8 + 1, 1, ix, iy)
        x0, y0 = ix * 8 + 7 + a, iy * 8 + 7 + b
        inner = gather_xy(a1, x0, y0, wx, wy)
        outer = gather_xy(e1, x0, y0, wx, wy)
        masks = [((lane - (c + t - 1)) & -128) == 0 for t in range(4)]
        turns = [(1 - c - t) & 127 for t in range(4)]
        back = [(c + t - 1) & 127 for t in range(4)]
        in_w = [jnp.where(masks[t], wz[t], 0.0) for t in range(4)]
        out_w = [jnp.where(masks[t], 0.0, wz[t]) for t in range(4)]
        to_a, to_e = [], []
        for p in range(8):
            state = sum(wz[t] * pltpu.roll(jnp.where(masks[t], inner[p], outer[p]), turns[t], 1) for t in range(4))
            turned = [pltpu.roll(state, back[t], 1) for t in range(4)]
            to_a.append(sum(in_w[t] * turned[t] for t in range(4)))
            to_e.append(sum(out_w[t] * turned[t] for t in range(4)))
        scatter_xy(ra, to_a, x0, y0, wx, wy)
        scatter_xy(re, to_e, x0, y0, wx, wy)
        return 0

    lax.fori_loop(0, 4, second_step, 0)

    wide = lanes(32)
    quarter = ((wide + 16) & 127) // 32
    for h in range(2):
        for x in range(4):
            u, d = None, None
            for g in range(4):
                a, e = ra[16 * h + 4 * g + x, 0:32], re[16 * h + 4 * g + x, 0:32]
                rise = roll(jnp.where(wide >= 64, a, e), 32 * g)
                fall = roll(jnp.where(wide >= 64, e, a), 32 * g)
                u = rise if g == 0 else jnp.where(quarter == g, rise, u)
                d = fall if g == 0 else jnp.where(quarter == g, fall, d)
            up[h * 4 + x] = u
            down[h * 4 + x] = d


def sum_z_kernel(ra, own_up, own_down, low, high, up, down):
    low_in, high_in = inside("gz")
    wide = lanes(32)
    even = (wide // 16) % 2 == 0
    valid = (wide < 16) | (wide >= 112)
    for h in range(2):
        for x in range(4):
            a, b = low_in * low[h * 4 + x], high_in * high[h * 4 + x]
            inner = jnp.where(even, a, b)
            outer = jnp.where(even, own_up[h * 4 + x], own_down[h * 4 + x]) + jnp.where(even, b, a)
            down[pl.ds(R_E + (h * 4 + x) * T, T)] = outer[0:16]
            up[pl.ds(R_E + (h * 4 + x) * T, T)] = outer[16:32]
            for g in range(4):
                at = 16 * h + 4 * g + x
                value = ra[at, 0:32] + jnp.where(valid, roll(inner, -32 * g), 0.0)
                down[pl.ds(at * T, T)] = value[0:16]
                up[pl.ds(at * T, T)] = value[16:32]


def sum_y_kernel(own_up, own_down, low, high, up, down):
    low_in, high_in = inside("gy")
    for h, out in ((0, down), (1, up)):
        for start, planes in ((0, 16), (R_E, 4)):
            for x in range(planes):
                rows = pl.ds(start + (h * planes + x) * T, T)
                out[pl.ds(start + x * 32, T)] = own_down[rows] + low_in * low[rows]
                out[pl.ds(start + x * 32 + T, T)] = own_up[rows] + high_in * high[rows]


def last_step_kernel(own_up, own_down, low, high, meta_low, meta_own, meta_high, g, reg, out, a1, e1, acc, meta, sem):
    copies = []
    for n, ref in enumerate((meta_low, meta_own, meta_high)):
        copy = pltpu.make_async_copy(ref.at[pl.ds(X_META, 24)], meta.at[pl.ds(n * 24, 24)], sem.at[n])
        copy.start()
        copies.append(copy)
    low_in, high_in = inside("gx")
    wide = lanes(32)
    valid = (wide < 16) | (wide >= 112)
    for h, (mine, other, keep) in enumerate(((own_down, low, low_in), (own_up, high, high_in))):
        for x in range(16):
            rows = pl.ds(x * 32, 32)
            a1[16 * h + x] = mine[rows] + keep * other[rows]
        for x in range(4):
            rows = pl.ds(R_E + x * 32, 32)
            packed = mine[rows] + keep * other[rows]
            for q in range(4):
                e1[16 * h + 4 * q + x] = jnp.where(valid, roll(packed, -32 * q), 0.0)
    acc[...] = jnp.zeros(acc.shape, F32)
    for copy in copies:
        copy.wait()
    lane = lanes()
    upper = lane >= 64

    def step(i, _):
        bx, by = i // 4, i % 4
        (slot_x, ix), (slot_y, iy) = block_of(bx), block_of(by)
        row = slot_x * 24 + slot_y * 8
        keep = jnp.where(slot_x == 0, low_in, jnp.where(slot_x == 2, high_in, 1.0))
        rows = pl.ds(pl.multiple_of(by * 8, 8), 8)
        inner = [a1[bx * 8 + p, rows, :] for p in range(8)]
        outer = [e1[bx * 8 + p, rows, :] for p in range(8)]
        for n in range(3):
            (a, b, c), (wx, wy, wz) = block_numbers(meta, row + n, 0, ix, iy, keep)
            back = [(c + t - 1) & 127 for t in range(4)]
            if n == 1:
                w = [jnp.where(((lane - (c + t - 1)) & -128) == 0, wz[t], 0.0) for t in range(4)]
                values = inner
            else:
                lands = upper if n == 2 else jnp.logical_not(upper)
                w = [jnp.where(lands, wz[t], 0.0) for t in range(4)]
                values = [jnp.where(upper if n == 0 else jnp.logical_not(upper), value, 0.0) for value in outer]
            moved = [sum(w[t] * pltpu.roll(value, back[t], 1) for t in range(4)) for value in values]
            scatter_xy(acc, moved, bx * 8 + 7 + a, by * 8 + 7 + b, wx, wy)
        return 0

    lax.fori_loop(0, 16, step, 0)
    for x in range(T):
        first, second = acc[16 + x, 16:32], a1[8 + x, 8:24]
        for c in range(3):
            out[c, x] = reg[c, x] + STEP_SIZE * (g[1, c, x].astype(F32) * second + g[0, c, x].astype(F32) * first)


def laplace_kernel(v, zlow, zhigh, ylow, yhigh, xlow, xhigh, out, w):
    lane = lanes(T)
    half = (lane & 4) == 0
    (x_low, x_high), (y_low, y_high), (z_low, z_high) = inside("gx"), inside("gy"), inside("gz")
    sides = [-REG_WEIGHT * t for t in LAPLACE_TAPS]
    for c in range(3):
        rows = pl.ds(Z_V + c * T, T)
        faces = jnp.where(half, z_high * zhigh[rows], z_low * zlow[rows])
        for i in range(4):
            rows = pl.ds(X_V + (c * 4 + i) * T, T)
            w[i, 8:24] = x_low * xlow[rows]
            w[20 + i, 8:24] = x_high * xhigh[rows]
        for x in range(8):
            rows = pl.ds(Y_V + (c * 8 + x) * 8, 8)
            a, b = y_low * ylow[rows], y_high * yhigh[rows]
            w[4 + x, 0:8] = a
            w[12 + x, 0:8] = pltpu.roll(a, 4, 0)
            w[4 + x, 24:32] = b
            w[12 + x, 24:32] = pltpu.roll(b, 4, 0)
        for x in range(T):
            w[4 + x, 8:24] = v[c, x]
        for x in range(T):
            here = v[c, x]
            edge = roll(faces, -8 * x)
            total = 3.0 * sides[0] * here
            for k in range(1, 5):
                near = roll(jnp.where(lane < k, edge, here), -k) + roll(jnp.where(lane >= L - k, edge, here), k)
                near = near + w[4 + x - k, 8:24] + w[4 + x + k, 8:24]
                near = near + w[4 + x, 8 - k : 24 - k] + w[4 + x, 8 + k : 24 + k]
                total = total + sides[k] * near
            out[c, x] = total


VMEM = pl.BlockSpec(memory_space=pltpu.VMEM)
HBM = pl.BlockSpec(memory_space=pltpu.HBM)


def call(kernel, args, outs, scratch=(), hbm=(), cost=20000):
    specs = [HBM if i in hbm else VMEM for i in range(len(args))]
    shapes = [jax.ShapeDtypeStruct(s, F32) for s in outs]
    return pl.pallas_call(
        kernel,
        out_shape=shapes,
        in_specs=specs,
        out_specs=[VMEM] * len(shapes),
        scratch_shapes=list(scratch),
        compiler_params=pltpu.CompilerParams(vmem_limit_bytes=24 * 1024 * 1024),
        cost_estimate=pl.CostEstimate(flops=cost, bytes_accessed=cost, transcendentals=0),
    )(*args)


def exchange(up, down, axis):
    n = lax.axis_size(axis)
    rise = [(i, (i + 1) % n) for i in range(n)]
    fall = [(j, i) for i, j in rise]
    return lax.ppermute(up, axis, rise), lax.ppermute(down, axis, fall)


def body(velocity, gradients, shift_x, shift_y, shift_z, fractions):
    v, g = velocity, gradients
    tile = (T, T, L)
    vm = lambda *s: pltpu.VMEM(s, F32)
    shifts = [s.transpose(0, 1, 3, 2) for s in (shift_x, shift_y, shift_z)]
    s0, s1, zup, zdown = call(
        sources_kernel,
        [pltpu.with_memory_space_constraint(a, pltpu.HBM) for a in (v, g, *shifts, fractions.transpose(0, 2, 3, 4, 1))],
        [tile, tile, (Z_ROWS, L), (Z_ROWS, L)],
        scratch=[vm(*v.shape), pltpu.VMEM(g.shape, g.dtype)]
        + [pltpu.SMEM((2, 2, 1, 2), jnp.int32)] * 3
        + [pltpu.SMEM((2, 2, 2, 1, 3), jnp.int32), pltpu.SemaphoreType.DMA((8,)), pltpu.SemaphoreType.DMA((4,))],
        hbm=range(6),
    )
    zlow, zhigh = exchange(zup, zdown, "gz")
    yup, ydown = call(y_message_kernel, (s0, s1, v, zup, zlow, zhigh), [(Y_ROWS, L)] * 2)
    ylow, yhigh = exchange(yup, ydown, "gy")
    xup, xdown = call(x_message_kernel, (yup, ydown, ylow, yhigh, v), [(X_ROWS, L)] * 2)
    xlow, xhigh = exchange(xup, xdown, "gx")
    meta = [pltpu.SMEM((72, L), F32), pltpu.SemaphoreType.DMA((3,))]
    ra, zup, zdown = call(
        steps_kernel,
        (xup, xdown, xlow, xhigh),
        [(32, 40, L), (8, 32, L), (8, 32, L)],
        scratch=[vm(48, 48, L), vm(48, 48, L), vm(32, 32, L), vm(32, 32, L), vm(32, 40, L)] + meta,
    )
    (reg,) = call(
        laplace_kernel, (v, zlow, zhigh, ylow, yhigh, xlow, xhigh), [v.shape], scratch=[vm(24, 32, L)], cost=4000000
    )
    low, high = exchange(zup, zdown, "gz")
    up, down = call(sum_z_kernel, (ra, zup, zdown, low, high), [(R_ROWS, L)] * 2)
    low, high = exchange(up, down, "gy")
    up, down = call(sum_y_kernel, (up, down, low, high), [(R_ROWS, L)] * 2)
    low, high = exchange(up, down, "gx")
    (out,) = call(
        last_step_kernel,
        (up, down, low, high, xlow, xup, xhigh, g, reg),
        [v.shape],
        scratch=[vm(32, 32, L), vm(32, 32, L), vm(48, 56, L)] + meta,
    )
    return out


def solution(mesh):
    in_specs = (
        P(None, "gx", "gy", "gz"),
        P(None, None, "gx", "gy", "gz"),
        P(None, "gx", "gy", "gz"),
        P(None, "gx", "gy", "gz"),
        P(None, "gx", "gy", "gz"),
        P(None, None, "gx", "gy", "gz"),
    )
    out_specs = P(None, "gx", "gy", "gz")
    return jax.shard_map(body, mesh=mesh, in_specs=in_specs, out_specs=out_specs, check_vma=False)
```

```python
import jax
import jax.numpy as jnp
from jax import lax
from jax.experimental import pallas as pl
from jax.experimental.pallas import tpu as pltpu
from jax.sharding import PartitionSpec as P

F32 = jnp.float32
LAPLACE_TAPS = (-205.0 / 72.0, 8.0 / 5.0, -1.0 / 5.0, 8.0 / 315.0, -1.0 / 560.0)
STEP_SIZE = 0.5
REG_WEIGHT = 0.1
T = 16
L = 128
UN_ASM, UN_SEC, UN_FIRST, UN_SECOND, UN_PACK, UN_UNPACK, UN_STEP, UN_FIN = 8, 4, 16, 1, 8, 4, 16, 16
META = 15

Z_S0, Z_S1, Z_V, Z_META, Z_ROWS = 0, 64, 96, 144, 152
Y_S0, Y_M0, Y_S1, Y_M1, Y_V, Y_META, Y_ROWS = 0, 256, 384, 512, 544, 736, 744
X_S0, X_M0, X_S1, X_M1, X_V, X_META, X_ROWS = 0, 768, 1152, 1408, 1472, 1664, 1688
R_E, R_ROWS = 512, 640


def lanes(rows=8):
    return lax.broadcasted_iota(jnp.int32, (rows, L), 1)


def subs():
    return lax.broadcasted_iota(jnp.int32, (8, L), 0)


def roll(x, amount):
    amount = amount % L
    return x if amount == 0 else pltpu.roll(x, amount, 1)


def block_numbers(meta, row, step, ix, iy, keep=None):
    at = ((step * 2 + ix) * 2 + iy) * META
    shift = [meta[row, at + d].astype(jnp.int32) for d in range(3)]
    weights = [[meta[row, at + 3 + 4 * d + t] for t in range(4)] for d in range(3)]
    if keep is not None:
        weights[0] = [w * keep for w in weights[0]]
    return shift, weights


def loop(count, body, unroll=1):
    def step(i, _):
        body(i)
        return 0

    lax.fori_loop(0, count, step, 0, unroll=unroll)


def inside(axis):
    i, n = lax.axis_index(axis), lax.axis_size(axis)
    return jnp.where(i > 0, 1.0, 0.0).astype(F32), jnp.where(i < n - 1, 1.0, 0.0).astype(F32)


def sources_kernel(v_hbm, g_hbm, sx_hbm, sy_hbm, sz_hbm, fr_hbm, s0, s1, up, down, v, g, sx, sy, sz, fr, sem, small_sem):
    copies = []
    for q in range(4):
        part = pl.ds(4 * q, 4)
        copies.append(pltpu.make_async_copy(v_hbm.at[:, part], v.at[:, part], sem.at[2 * q]))
        copies.append(pltpu.make_async_copy(g_hbm.at[:, :, part], g.at[:, :, part], sem.at[2 * q + 1]))
    small = [
        pltpu.make_async_copy(a, b, small_sem.at[n])
        for n, (a, b) in enumerate(((sx_hbm, sx), (sy_hbm, sy), (sz_hbm, sz), (fr_hbm, fr)))
    ]
    for copy in copies + small:
        copy.start()
    lane = lanes(T)
    for x in range(T):
        if x % 4 == 0:
            copies[x // 2].wait()
            copies[x // 2 + 1].wait()
        vel = [v[c, x] for c in range(3)]
        for k, s in ((0, s0), (1, s1)):
            total = g[k, 0, x].astype(F32) * vel[0]
            for c in (1, 2):
                total = total + g[k, c, x].astype(F32) * vel[c]
            s[x] = STEP_SIZE * total
    quarter = lane // 32
    for j in range(4):
        a, b, c, d = s0[j], roll(s0[j + 4], 32), roll(s0[j + 8], 64), roll(s0[j + 12], 96)
        rows = pl.ds(Z_S0 + j * T, T)
        up[rows] = jnp.where(quarter == 3, a, jnp.where(quarter == 1, c, jnp.where(quarter == 0, b, d)))
        down[rows] = jnp.where(quarter == 0, a, jnp.where(quarter == 2, c, jnp.where(quarter == 1, b, d)))
    eighth = lane // 16
    for h in range(2):
        u, d = s1[8 * h], s1[8 * h]
        for i in range(1, 8):
            r = roll(s1[8 * h + i], 16 * i)
            u = jnp.where(eighth == (7 + i) % 8, r, u)
            d = jnp.where(eighth == i, r, d)
        up[pl.ds(Z_S1 + h * T, T)] = u
        down[pl.ds(Z_S1 + h * T, T)] = d
    piece = lane // 8
    for c in range(3):
        u, d = v[c, 0], v[c, 0]
        for x in range(1, T):
            r = roll(v[c, x], 8 * x)
            u = jnp.where(piece == (15 + x) % 16, r, u)
            d = jnp.where(piece == x, r, d)
        up[pl.ds(Z_V + c * T, T)] = u
        down[pl.ds(Z_V + c * T, T)] = d
    lane = lanes()
    for copy in small:
        copy.wait()
    shifts, eighths = jnp.zeros((8, L), jnp.int32), jnp.zeros((8, L), jnp.int32)
    for k in range(2):
        for ix in range(2):
            for iy in range(2):
                at = ((k * 2 + ix) * 2 + iy) * META
                for n, ref in enumerate((sx, sy, sz)):
                    shifts = jnp.where(lane == at + n, ref[k, ix, 0, iy], shifts)
                    first = at + 3 + 4 * n
                    eighths = jnp.where((lane >= first) & (lane < first + 4), fr[k, ix, iy, 0, n], eighths)
    e = eighths.astype(F32) / 8.0
    e2 = e * e
    e3 = e2 * e
    weights = [
        0.5 * (2.0 * e2 - e3 - e),
        0.5 * (3.0 * e3 - 5.0 * e2 + 2.0),
        0.5 * (4.0 * e2 - 3.0 * e3 + e),
        0.5 * (e3 - e2),
    ]
    place = lane % META
    tap = (place - 3) % 4
    row = jnp.where(tap == 0, weights[0], jnp.where(tap == 1, weights[1], jnp.where(tap == 2, weights[2], weights[3])))
    row = jnp.where(place < 3, shifts.astype(F32), row)
    up[pl.ds(Z_META, 8)] = row
    down[pl.ds(Z_META, 8)] = row


def y_message_kernel(s0, s1, v, own, low, high, up, down):
    low_in, high_in = inside("gz")
    lane = lanes(T)
    even = (lane // 32) % 2 == 0
    for x in range(T):
        for out in (up, down):
            out[pl.ds(Y_S0 + x * T, T)] = s0[x]
        up[pl.ds(Y_S1 + x * 8, 8)] = s1[x, 8:16]
        down[pl.ds(Y_S1 + x * 8, 8)] = s1[x, 0:8]
    for j in range(4):
        a, b = low_in * low[pl.ds(Z_S0 + j * T, T)], high_in * high[pl.ds(Z_S0 + j * T, T)]
        first = jnp.where(even, b, a)
        second = roll(jnp.where(even, a, b), -32)
        for out in (up, down):
            out[pl.ds(Y_M0 + j * T, T)] = first
            out[pl.ds(Y_M0 + (j + 4) * T, T)] = second
    even = (lane // 16) % 2 == 0
    for h in range(2):
        a, b = low_in * low[pl.ds(Z_S1 + h * T, T)], high_in * high[pl.ds(Z_S1 + h * T, T)]
        for j, value in enumerate((jnp.where(even, b, a), roll(jnp.where(even, a, b), -16))):
            up[pl.ds(Y_M1 + (h * 2 + j) * 8, 8)] = value[8:16]
            down[pl.ds(Y_M1 + (h * 2 + j) * 8, 8)] = value[0:8]
    first_half = subs() < 4
    for c in range(3):
        for x in range(8):
            rows = pl.ds(Y_V + (c * 8 + x) * 8, 8)
            up[rows] = jnp.where(first_half, pltpu.roll(v[c, x + 8, 8:16], 4, 0), v[c, x, 8:16])
            down[rows] = jnp.where(first_half, v[c, x, 0:8], pltpu.roll(v[c, x + 8, 0:8], 4, 0))
    sub = subs()
    meta = [ref[pl.ds(Z_META, 8)] for ref in (low, own, high)]
    row = jnp.where(sub == 0, low_in * meta[0], jnp.where(sub == 1, meta[1], high_in * meta[2]))
    up[pl.ds(Y_META, 8)] = row
    down[pl.ds(Y_META, 8)] = row


def x_message_kernel(own_up, own_down, low, high, v, up, down):
    low_in, high_in = inside("gy")

    def take(ref, rows):
        value = ref[rows]
        return low_in * value if ref is low else high_in * value if ref is high else value

    for n, (start, planes, to) in enumerate(((Y_S0, T, X_S0), (Y_M0, 8, X_M0))):
        for x in range(planes):
            for at, ref in enumerate((low, own_up, high)):
                value = take(ref, pl.ds(start + x * T, T))
                for out in (up, down):
                    out[pl.ds(to + x * 48 + at * T, T)] = value
    for h, out in ((1, up), (0, down)):
        for x in range(8):
            for at, ref in enumerate((low, own_down, own_up, high)):
                out[pl.ds(X_S1 + x * 32 + at * 8, 8)] = take(ref, pl.ds(Y_S1 + (8 * h + x) * 8, 8))
        for j in range(2):
            for at, ref in enumerate((low, own_down, own_up, high)):
                out[pl.ds(X_M1 + j * 32 + at * 8, 8)] = take(ref, pl.ds(Y_M1 + (h * 2 + j) * 8, 8))
        for c in range(3):
            for i in range(4):
                out[pl.ds(X_V + (c * 4 + i) * T, T)] = v[c, 12 * h + i]
        for at, ref in enumerate((low, own_up, high)):
            out[pl.ds(X_META + at * 8, 8)] = take(ref, pl.ds(Y_META, 8))


def gather_xy(ref, width, x0, y0, wx, wy):
    base = x0 * width + y0
    planes = []
    for i in range(11):
        plane = wy[0] * ref[pl.ds(base + i * width, 8), :]
        for t in range(1, 4):
            plane = plane + wy[t] * ref[pl.ds(base + (i * width + t), 8), :]
        planes.append(plane)
    out = []
    for i in range(8):
        value = wx[0] * planes[i]
        for t in range(1, 4):
            value = value + wx[t] * planes[i + t]
        out.append(value)
    return out


def scatter_xy(ref, width, vals, x0, y0, wx, wy):
    sub = subs()
    base = x0 * width + y0
    places = [pl.ds(base + (p * width + 8 * half), 8) for p in range(11) for half in range(2)]
    low_w = [jnp.where(sub >= t, wy[t], 0.0) for t in range(4)]
    high_w = [jnp.where(sub < t, wy[t], 0.0) for t in range(4)]
    pairs = []
    for value in vals:
        first, second = wy[0] * value, None
        for t in range(1, 4):
            turned = pltpu.roll(value, t, 0)
            first = first + low_w[t] * turned
            second = high_w[t] * turned if second is None else second + high_w[t] * turned
        pairs.append((first, second))
    sums = []
    for p in range(11):
        for half in range(2):
            total = ref[places[len(sums)], :]
            for t in range(4):
                if 0 <= p - t < 8:
                    total = total + wx[t] * pairs[p - t][half]
            sums.append(total)
    for place, total in zip(places, sums):
        ref[place, :] = total


def block_of(b):
    return (b + 1) // 2, (b + 1) % 2


def steps_kernel(own_up, own_down, low, high, ra, up, down, clo, chi, a1, e1, re, meta, sem):
    low_in, high_in = inside("gx")
    lane = lanes()
    upper = lane >= 64
    copies = []
    for n, ref in enumerate((low, own_up, high)):
        copy = pltpu.make_async_copy(ref.at[pl.ds(X_META, 24)], meta.at[pl.ds(n * 24, 24)], sem.at[n])
        copy.start()
        copies.append(copy)
    upper48 = lanes(48) >= 64
    for n, (ref, keep) in enumerate(((low, low_in), (own_up, None), (high, high_in))):

        def assemble(x, n=n, ref=ref, keep=keep):
            m = ref[pl.ds(pl.multiple_of(X_M0 + x * 48, 8), 48)]
            m = m if keep is None else keep * m
            for half, e in ((0, m), (1, roll(m, 64))):
                a = ref[pl.ds(pl.multiple_of(X_S0 + (x + 8 * half) * 48, 8), 48)]
                a = a if keep is None else keep * a
                rows = pl.ds(pl.multiple_of((n * T + 8 * half + x) * 48, 8), 48)
                clo[rows] = jnp.where(upper48, e, a)
                chi[rows] = jnp.where(upper48, a, e)

        loop(8, assemble, UN_ASM)
    for n, (ref, keep) in enumerate(((low, low_in), (own_down, None), (own_up, None), (high, high_in))):

        def assemble_second(q, n=n, ref=ref, keep=keep):
            for j in range(2):
                x = 2 * q + j
                a = ref[pl.ds(pl.multiple_of(X_S1 + x * 32, 8), 32)]
                e = pltpu.roll(ref[pl.ds(X_M1 + j * 32, 32)], (L - 32 * q) & 127, 1)
                rows = pl.ds(pl.multiple_of((n * 8 + x) * 32, 8), 32)
                a1[rows] = a if keep is None else keep * a
                e1[rows] = e if keep is None else keep * e

        loop(4, assemble_second, UN_SEC)

    def clear(i):
        rows = pl.ds(pl.multiple_of(i * 128, 8), 128)
        ra[rows] = jnp.zeros((128, L), F32)
        re[rows] = jnp.zeros((128, L), F32)

    loop(10, clear)
    for copy in copies:
        copy.wait()

    def first_step(i):
        bx, by = i // 4, i % 4
        (slot_x, ix), (slot_y, iy) = block_of(bx), block_of(by)
        row = slot_x * 24 + slot_y * 8
        keep = jnp.where(slot_x == 0, low_in, jnp.where(slot_x == 2, high_in, 1.0))
        rows = [pl.ds(pl.multiple_of(bx * 256 + by * 8, 8) + p * 32, 8) for p in range(8)]

        def numbers(n):
            (a, b, c), (wx, wy, wz) = block_numbers(meta, row + n, 0, ix, iy, keep)
            return bx * 8 + 7 + a, by * 8 + 7 + b, c, wx, wy, wz

        x0, y0, c, wx, wy, wz = numbers(1)
        lows = gather_xy(clo, 48, x0, y0, wx, wy)
        highs = gather_xy(chi, 48, x0, y0, wx, wy)
        masks = [jnp.logical_xor(((lane - (c + t - 1)) & -128) == 0, upper) for t in range(4)]
        turns = [(1 - c - t) & 127 for t in range(4)]
        for p in range(8):
            value = sum(wz[t] * pltpu.roll(jnp.where(masks[t], lows[p], highs[p]), turns[t], 1) for t in range(4))
            a1[rows[p], :] = a1[rows[p], :] + value
        edges = []
        for n, ref in ((0, clo), (2, chi)):
            x0, y0, c, wx, wy, wz = numbers(n)
            values = gather_xy(ref, 48, x0, y0, wx, wy)
            turns = [(1 - c - t) & 127 for t in range(4)]
            edges.append([sum(wz[t] * pltpu.roll(value, turns[t], 1) for t in range(4)) for value in values])
        for p in range(8):
            e1[rows[p], :] = e1[rows[p], :] + jnp.where(upper, edges[0][p], edges[1][p])

    loop(16, first_step, UN_FIRST)

    def second_step(i):
        ix, iy = i // 2, i % 2
        (a, b, c), (wx, wy, wz) = block_numbers(meta, 24 + 8 + 1, 1, ix, iy)
        x0, y0 = ix * 8 + 7 + a, iy * 8 + 7 + b
        inner = gather_xy(a1, 32, x0, y0, wx, wy)
        outer = gather_xy(e1, 32, x0, y0, wx, wy)
        masks = [((lane - (c + t - 1)) & -128) == 0 for t in range(4)]
        turns = [(1 - c - t) & 127 for t in range(4)]
        back = [(c + t - 1) & 127 for t in range(4)]
        in_w = [jnp.where(masks[t], wz[t], 0.0) for t in range(4)]
        out_w = [jnp.where(masks[t], 0.0, wz[t]) for t in range(4)]
        to_a, to_e = [], []
        for p in range(8):
            state = sum(wz[t] * pltpu.roll(jnp.where(masks[t], inner[p], outer[p]), turns[t], 1) for t in range(4))
            turned = [pltpu.roll(state, back[t], 1) for t in range(4)]
            to_a.append(sum(in_w[t] * turned[t] for t in range(4)))
            to_e.append(sum(out_w[t] * turned[t] for t in range(4)))
        scatter_xy(ra, 40, to_a, x0, y0, wx, wy)
        scatter_xy(re, 40, to_e, x0, y0, wx, wy)

    loop(4, second_step, UN_SECOND)

    wide = lanes(32)
    quarter = ((wide + 16) & 127) // 32

    def pack(i):
        u, d = None, None
        for g in range(4):
            rows = pl.ds(pl.multiple_of((16 * (i // 4) + 4 * g + i % 4) * 40, 8), 32)
            a, e = ra[rows], re[rows]
            rise = roll(jnp.where(wide >= 64, a, e), 32 * g)
            fall = roll(jnp.where(wide >= 64, e, a), 32 * g)
            u = rise if g == 0 else jnp.where(quarter == g, rise, u)
            d = fall if g == 0 else jnp.where(quarter == g, fall, d)
        up[i] = u
        down[i] = d

    loop(8, pack, UN_PACK)


def sum_z_kernel(ra, own_up, own_down, low, high, up, down):
    low_in, high_in = inside("gz")
    wide = lanes(32)
    even = (wide // 16) % 2 == 0
    valid = (wide < 16) | (wide >= 112)
    for h in range(2):
        for x in range(4):
            a, b = low_in * low[h * 4 + x], high_in * high[h * 4 + x]
            inner = jnp.where(even, a, b)
            outer = jnp.where(even, own_up[h * 4 + x], own_down[h * 4 + x]) + jnp.where(even, b, a)
            down[pl.ds(R_E + (h * 4 + x) * T, T)] = outer[0:16]
            up[pl.ds(R_E + (h * 4 + x) * T, T)] = outer[16:32]
            for g in range(4):
                at = 16 * h + 4 * g + x
                value = ra[pl.ds(at * 40, 32)] + jnp.where(valid, roll(inner, -32 * g), 0.0)
                down[pl.ds(at * T, T)] = value[0:16]
                up[pl.ds(at * T, T)] = value[16:32]


def sum_y_kernel(own_up, own_down, low, high, up, down):
    low_in, high_in = inside("gy")
    for h, out in ((0, down), (1, up)):
        for start, planes in ((0, 16), (R_E, 4)):
            for x in range(planes):
                rows = pl.ds(start + (h * planes + x) * T, T)
                out[pl.ds(start + x * 32, T)] = own_down[rows] + low_in * low[rows]
                out[pl.ds(start + x * 32 + T, T)] = own_up[rows] + high_in * high[rows]


def last_step_kernel(own_up, own_down, low, high, meta_low, meta_own, meta_high, g, reg, out, a1, e1, acc, meta, sem):
    copies = []
    for n, ref in enumerate((meta_low, meta_own, meta_high)):
        copy = pltpu.make_async_copy(ref.at[pl.ds(X_META, 24)], meta.at[pl.ds(n * 24, 24)], sem.at[n])
        copy.start()
        copies.append(copy)
    low_in, high_in = inside("gx")
    wide = lanes(32)
    valid = (wide < 16) | (wide >= 112)
    for h, (mine, other, keep) in enumerate(((own_down, low, low_in), (own_up, high, high_in))):

        def unpack(x, h=h, mine=mine, other=other, keep=keep):
            rows = pl.ds(pl.multiple_of(R_E + x * 32, 8), 32)
            packed = mine[rows] + keep * other[rows]
            for q in range(4):
                at = pl.multiple_of((4 * q + x) * 32, 8)
                e1[pl.ds(512 * h + at, 32)] = jnp.where(valid, roll(packed, -32 * q), 0.0)
                a1[pl.ds(512 * h + at, 32)] = mine[pl.ds(at, 32)] + keep * other[pl.ds(at, 32)]

        loop(4, unpack, UN_UNPACK)

    def clear(i):
        acc[pl.ds(pl.multiple_of(i * 168, 8), 168)] = jnp.zeros((168, L), F32)

    loop(16, clear)
    for copy in copies:
        copy.wait()
    lane = lanes()
    upper = lane >= 64

    def step(i):
        bx, by = i // 4, i % 4
        (slot_x, ix), (slot_y, iy) = block_of(bx), block_of(by)
        row = slot_x * 24 + slot_y * 8
        keep = jnp.where(slot_x == 0, low_in, jnp.where(slot_x == 2, high_in, 1.0))
        rows = [pl.ds(pl.multiple_of(bx * 256 + by * 8, 8) + p * 32, 8) for p in range(8)]
        inner = [a1[r, :] for r in rows]
        outer = [e1[r, :] for r in rows]
        for n in range(3):
            (a, b, c), (wx, wy, wz) = block_numbers(meta, row + n, 0, ix, iy, keep)
            back = [(c + t - 1) & 127 for t in range(4)]
            if n == 1:
                w = [jnp.where(((lane - (c + t - 1)) & -128) == 0, wz[t], 0.0) for t in range(4)]
                values = inner
            else:
                lands = upper if n == 2 else jnp.logical_not(upper)
                w = [jnp.where(lands, wz[t], 0.0) for t in range(4)]
                values = [jnp.where(upper if n == 0 else jnp.logical_not(upper), value, 0.0) for value in outer]
            moved = [sum(w[t] * pltpu.roll(value, back[t], 1) for t in range(4)) for value in values]
            scatter_xy(acc, 56, moved, bx * 8 + 7 + a, by * 8 + 7 + b, wx, wy)

    loop(16, step, UN_STEP)

    def finish(x):
        first, second = acc[pl.ds(pl.multiple_of((16 + x) * 56 + 16, 8), 16)], a1[pl.ds(pl.multiple_of((8 + x) * 32 + 8, 8), 16)]
        for c in range(3):
            out[c, x] = reg[c, x] + STEP_SIZE * (g[1, c, x].astype(F32) * second + g[0, c, x].astype(F32) * first)

    loop(T, finish, UN_FIN)


def laplace_kernel(v, zlow, zhigh, ylow, yhigh, xlow, xhigh, out, w):
    lane = lanes(T)
    half = (lane & 4) == 0
    (x_low, x_high), (y_low, y_high), (z_low, z_high) = inside("gx"), inside("gy"), inside("gz")
    sides = [-REG_WEIGHT * t for t in LAPLACE_TAPS]
    for c in range(3):
        rows = pl.ds(Z_V + c * T, T)
        faces = jnp.where(half, z_high * zhigh[rows], z_low * zlow[rows])
        for i in range(4):
            rows = pl.ds(X_V + (c * 4 + i) * T, T)
            w[i, 8:24] = x_low * xlow[rows]
            w[20 + i, 8:24] = x_high * xhigh[rows]
        for x in range(8):
            rows = pl.ds(Y_V + (c * 8 + x) * 8, 8)
            a, b = y_low * ylow[rows], y_high * yhigh[rows]
            w[4 + x, 0:8] = a
            w[12 + x, 0:8] = pltpu.roll(a, 4, 0)
            w[4 + x, 24:32] = b
            w[12 + x, 24:32] = pltpu.roll(b, 4, 0)
        for x in range(T):
            w[4 + x, 8:24] = v[c, x]
        for x in range(T):
            here = v[c, x]
            edge = roll(faces, -8 * x)
            total = 3.0 * sides[0] * here
            for k in range(1, 5):
                near = roll(jnp.where(lane < k, edge, here), -k) + roll(jnp.where(lane >= L - k, edge, here), k)
                near = near + w[4 + x - k, 8:24] + w[4 + x + k, 8:24]
                near = near + w[4 + x, 8 - k : 24 - k] + w[4 + x, 8 + k : 24 + k]
                total = total + sides[k] * near
            out[c, x] = total


VMEM = pl.BlockSpec(memory_space=pltpu.VMEM)
HBM = pl.BlockSpec(memory_space=pltpu.HBM)


def call(kernel, args, outs, scratch=(), hbm=(), cost=20000):
    specs = [HBM if i in hbm else VMEM for i in range(len(args))]
    shapes = [jax.ShapeDtypeStruct(s, F32) for s in outs]
    return pl.pallas_call(
        kernel,
        out_shape=shapes,
        in_specs=specs,
        out_specs=[VMEM] * len(shapes),
        scratch_shapes=list(scratch),
        compiler_params=pltpu.CompilerParams(vmem_limit_bytes=24 * 1024 * 1024),
        cost_estimate=pl.CostEstimate(flops=cost, bytes_accessed=cost, transcendentals=0),
    )(*args)


def exchange(up, down, axis):
    n = lax.axis_size(axis)
    rise = [(i, (i + 1) % n) for i in range(n)]
    fall = [(j, i) for i, j in rise]
    return lax.ppermute(up, axis, rise), lax.ppermute(down, axis, fall)


def body(velocity, gradients, shift_x, shift_y, shift_z, fractions):
    v, g = velocity, gradients
    tile = (T, T, L)
    vm = lambda *s: pltpu.VMEM(s, F32)
    shifts = [s.transpose(0, 1, 3, 2) for s in (shift_x, shift_y, shift_z)]
    s0, s1, zup, zdown = call(
        sources_kernel,
        [pltpu.with_memory_space_constraint(a, pltpu.HBM) for a in (v, g, *shifts, fractions.transpose(0, 2, 3, 4, 1))],
        [tile, tile, (Z_ROWS, L), (Z_ROWS, L)],
        scratch=[vm(*v.shape), pltpu.VMEM(g.shape, g.dtype)]
        + [pltpu.SMEM((2, 2, 1, 2), jnp.int32)] * 3
        + [pltpu.SMEM((2, 2, 2, 1, 3), jnp.int32), pltpu.SemaphoreType.DMA((8,)), pltpu.SemaphoreType.DMA((4,))],
        hbm=range(6),
    )
    zlow, zhigh = exchange(zup, zdown, "gz")
    yup, ydown = call(y_message_kernel, (s0, s1, v, zup, zlow, zhigh), [(Y_ROWS, L)] * 2)
    ylow, yhigh = exchange(yup, ydown, "gy")
    xup, xdown = call(x_message_kernel, (yup, ydown, ylow, yhigh, v), [(X_ROWS, L)] * 2)
    xlow, xhigh = exchange(xup, xdown, "gx")
    meta = [pltpu.SMEM((72, L), F32), pltpu.SemaphoreType.DMA((3,))]
    ra, zup, zdown = call(
        steps_kernel,
        (xup, xdown, xlow, xhigh),
        [(32 * 40, L), (8, 32, L), (8, 32, L)],
        scratch=[vm(48 * 48, L), vm(48 * 48, L), vm(32 * 32, L), vm(32 * 32, L), vm(32 * 40, L)] + meta,
    )
    (reg,) = call(
        laplace_kernel, (v, zlow, zhigh, ylow, yhigh, xlow, xhigh), [v.shape], scratch=[vm(24, 32, L)], cost=4000000
    )
    low, high = exchange(zup, zdown, "gz")
    up, down = call(sum_z_kernel, (ra, zup, zdown, low, high), [(R_ROWS, L)] * 2)
    low, high = exchange(up, down, "gy")
    up, down = call(sum_y_kernel, (up, down, low, high), [(R_ROWS, L)] * 2)
    low, high = exchange(up, down, "gx")
    (out,) = call(
        last_step_kernel,
        (up, down, low, high, xlow, xup, xhigh, g, reg),
        [v.shape],
        scratch=[vm(32 * 32, L), vm(32 * 32, L), vm(48 * 56, L)] + meta,
    )
    return out


def solution(mesh):
    in_specs = (
        P(None, "gx", "gy", "gz"),
        P(None, None, "gx", "gy", "gz"),
        P(None, "gx", "gy", "gz"),
        P(None, "gx", "gy", "gz"),
        P(None, "gx", "gy", "gz"),
        P(None, None, "gx", "gy", "gz"),
    )
    out_specs = P(None, "gx", "gy", "gz")
    return jax.shard_map(body, mesh=mesh, in_specs=in_specs, out_specs=out_specs, check_vma=False)
```

```python
import jax
import jax.numpy as jnp
from jax import lax
from jax.experimental import pallas as pl
from jax.experimental.pallas import tpu as pltpu
from jax.sharding import PartitionSpec as P

F32 = jnp.float32
LAPLACE_TAPS = (-205.0 / 72.0, 8.0 / 5.0, -1.0 / 5.0, 8.0 / 315.0, -1.0 / 560.0)
STEP_SIZE = 0.5
REG_WEIGHT = 0.1
T = 16
L = 128
UN_ASM, UN_CORNER, UN_FIRST, UN_SECOND, UN_PACK, UN_UNPACK, UN_STEP, UN_FIN = 4, 4, 16, 1, 8, 4, 16, 16
META = 15

Z_S0, Z_S1, Z_V, Z_META, Z_ROWS = 0, 128, 256, 304, 312
A0, E0, A1, E1, FACE, NUMBERS, ROWS = 0, 256, 512, 640, 768, 960, 968
C_LOW, C_HIGH, C_A1, C_E1, C_META, C_ROWS = 0, 512, 1024, 1152, 1280, 1296
R_E, R_ROWS = 512, 640


def lanes(rows=8):
    return lax.broadcasted_iota(jnp.int32, (rows, L), 1)


def subs():
    return lax.broadcasted_iota(jnp.int32, (8, L), 0)


def roll(x, amount):
    amount = amount % L
    return x if amount == 0 else pltpu.roll(x, amount, 1)


def block_numbers(meta, row, step, ix, iy):
    at = ((step * 2 + ix) * 2 + iy) * META
    shift = [meta[row, at + d].astype(jnp.int32) for d in range(3)]
    weights = [[meta[row, at + 3 + 4 * d + t] for t in range(4)] for d in range(3)]
    return shift, weights


def loop(count, body, unroll=1):
    def step(i, _):
        body(i)
        return 0

    lax.fori_loop(0, count, step, 0, unroll=unroll)


def inside(axis):
    i, n = lax.axis_index(axis), lax.axis_size(axis)
    return jnp.where(i > 0, 1.0, 0.0).astype(F32), jnp.where(i < n - 1, 1.0, 0.0).astype(F32)


def sources_kernel(v_hbm, g_hbm, sx_hbm, sy_hbm, sz_hbm, fr_hbm, s0, s1, up, down, v, g, sx, sy, sz, fr, sem, small_sem):
    copies = []
    for q in range(4):
        part = pl.ds(4 * q, 4)
        copies.append(pltpu.make_async_copy(v_hbm.at[:, part], v.at[:, part], sem.at[2 * q]))
        copies.append(pltpu.make_async_copy(g_hbm.at[:, :, part], g.at[:, :, part], sem.at[2 * q + 1]))
    small = [
        pltpu.make_async_copy(a, b, small_sem.at[n])
        for n, (a, b) in enumerate(((sx_hbm, sx), (sy_hbm, sy), (sz_hbm, sz), (fr_hbm, fr)))
    ]
    for copy in copies + small:
        copy.start()
    lane = lanes(T)
    for x in range(T):
        if x % 4 == 0:
            copies[x // 2].wait()
            copies[x // 2 + 1].wait()
        vel = [v[c, x] for c in range(3)]
        for k, s in ((0, s0), (1, s1)):
            total = g[k, 0, x].astype(F32) * vel[0]
            for c in (1, 2):
                total = total + g[k, c, x].astype(F32) * vel[c]
            s[x] = STEP_SIZE * total
    upper = lane >= 64
    for start, s in ((Z_S0, s0), (Z_S1, s1)):
        for x in range(8):
            rows = pl.ds(start + x * T, T)
            a, b = s[x], roll(s[x + 8], 64)
            up[rows] = jnp.where(upper, a, b)
            down[rows] = jnp.where(upper, b, a)
    piece = lane // 8
    for c in range(3):
        u, d = v[c, 0], v[c, 0]
        for x in range(1, T):
            r = roll(v[c, x], 8 * x)
            u = jnp.where(piece == (15 + x) % 16, r, u)
            d = jnp.where(piece == x, r, d)
        up[pl.ds(Z_V + c * T, T)] = u
        down[pl.ds(Z_V + c * T, T)] = d
    lane = lanes()
    for copy in small:
        copy.wait()
    shifts, eighths = jnp.zeros((8, L), jnp.int32), jnp.zeros((8, L), jnp.int32)
    for k in range(2):
        for ix in range(2):
            for iy in range(2):
                at = ((k * 2 + ix) * 2 + iy) * META
                for n, ref in enumerate((sx, sy, sz)):
                    shifts = jnp.where(lane == at + n, ref[k, ix, 0, iy], shifts)
                    first = at + 3 + 4 * n
                    eighths = jnp.where((lane >= first) & (lane < first + 4), fr[k, ix, iy, 0, n], eighths)
    e = eighths.astype(F32) / 8.0
    e2 = e * e
    e3 = e2 * e
    weights = [
        0.5 * (2.0 * e2 - e3 - e),
        0.5 * (3.0 * e3 - 5.0 * e2 + 2.0),
        0.5 * (4.0 * e2 - 3.0 * e3 + e),
        0.5 * (e3 - e2),
    ]
    place = lane % META
    tap = (place - 3) % 4
    row = jnp.where(tap == 0, weights[0], jnp.where(tap == 1, weights[1], jnp.where(tap == 2, weights[2], weights[3])))
    row = jnp.where(place < 3, shifts.astype(F32), row)
    up[pl.ds(Z_META, 8)] = row
    down[pl.ds(Z_META, 8)] = row


def tile_messages_kernel(s0, s1, v, own, low, high, yup, ydown, xup, xdown):
    low_in, high_in = inside("gz")
    upper = lanes(T) >= 64
    outs = (yup, ydown, xup, xdown)
    for start, to, s in ((Z_S0, 0, s0), (Z_S1, 1, s1)):
        for j in range(8):
            a, b = low_in * low[pl.ds(start + j * T, T)], high_in * high[pl.ds(start + j * T, T)]
            edges = (jnp.where(upper, a, b), roll(jnp.where(upper, b, a), 64))
            for h in range(2):
                x = j + 8 * h
                for at, value in ((0, s[x]), (1, edges[h])):
                    if to == 0:
                        for out in outs:
                            out[pl.ds((A0, E0)[at] + x * T, T)] = value
                    else:
                        yup[pl.ds((A1, E1)[at] + x * 8, 8)] = value[8:16]
                        ydown[pl.ds((A1, E1)[at] + x * 8, 8)] = value[0:8]
                        (xdown, xup)[h][pl.ds((A1, E1)[at] + j * T, T)] = value
    first_half = subs() < 4
    for c in range(3):
        for x in range(8):
            rows = pl.ds(FACE + (c * 8 + x) * 8, 8)
            yup[rows] = jnp.where(first_half, pltpu.roll(v[c, x + 8, 8:16], 4, 0), v[c, x, 8:16])
            ydown[rows] = jnp.where(first_half, v[c, x, 0:8], pltpu.roll(v[c, x + 8, 0:8], 4, 0))
        for i in range(4):
            xup[pl.ds(FACE + (c * 4 + i) * T, T)] = v[c, 12 + i]
            xdown[pl.ds(FACE + (c * 4 + i) * T, T)] = v[c, i]
    sub = subs()
    meta = [ref[pl.ds(Z_META, 8)] for ref in (low, own, high)]
    row = jnp.where(sub == 0, low_in * meta[0], jnp.where(sub == 1, meta[1], high_in * meta[2]))
    for out in outs:
        out[pl.ds(NUMBERS, 8)] = row


def corner_message_kernel(low, high, xlow, xhigh, up, down):
    del xlow, xhigh
    for y, (ref, keep, to) in enumerate(zip((low, high), inside("gy"), (C_LOW, C_HIGH))):
        for x in range(2 * T):
            value = keep * ref[pl.ds(A0 + x * T, T)]
            up[pl.ds(to + x * T, T)] = value
            down[pl.ds(to + x * T, T)] = value
        for start, place in ((A1, C_A1), (E1, C_E1)):
            for x in range(8):
                down[pl.ds(place + x * T + 8 * y, 8)] = keep * ref[pl.ds(start + x * 8, 8)]
                up[pl.ds(place + x * T + 8 * y, 8)] = keep * ref[pl.ds(start + (8 + x) * 8, 8)]
        value = keep * ref[pl.ds(NUMBERS, 8)]
        up[pl.ds(C_META + 8 * y, 8)] = value
        down[pl.ds(C_META + 8 * y, 8)] = value


def put(low, high, rows, upper, a, e):
    low[rows] = jnp.where(upper, e, a)
    high[rows] = jnp.where(upper, a, e)


def assemble_kernel(own_up, own_down, xlow, xhigh, ylow, yhigh, c_low, c_high, d_low, d_high):
    (xl, xh), (yl, yh) = inside("gx"), inside("gy")
    upper, upper8 = lanes(T) >= 64, lanes(8) >= 64

    def first(x):
        at = pl.multiple_of(x * T, 8)
        for ref, keep, dx, dy in ((own_up, None, 16, 16), (xlow, xl, 0, 16), (xhigh, xh, 32, 16), (ylow, yl, 16, 0), (yhigh, yh, 16, 32)):
            a, e = ref[pl.ds(A0 + at, T)], ref[pl.ds(E0 + at, T)]
            if keep is not None:
                a, e = keep * a, keep * e
            put(c_low, c_high, pl.ds(pl.multiple_of((dx + x) * 48 + dy, 8), T), upper, a, e)

    loop(T, first, UN_ASM)

    def second(x):
        at = pl.multiple_of(x * T, 8)
        for ref, keep, dx in ((own_down, None, 8), (own_up, None, 16), (xlow, xl, 0), (xhigh, xh, 24)):
            a, e = ref[pl.ds(A1 + at, T)], ref[pl.ds(E1 + at, T)]
            if keep is not None:
                a, e = keep * a, keep * e
            put(d_low, d_high, pl.ds(pl.multiple_of((dx + x) * 32 + 8, 8), T), upper, a, e)
        for h in range(2):
            at = pl.multiple_of((8 * h + x) * 8, 8)
            for ref, keep, dy in ((ylow, yl, 0), (yhigh, yh, 24)):
                a, e = keep * ref[pl.ds(A1 + at, 8)], keep * ref[pl.ds(E1 + at, 8)]
                put(d_low, d_high, pl.ds(pl.multiple_of((8 + 8 * h + x) * 32 + dy, 8), 8), upper8, a, e)

    loop(8, second, UN_ASM)


def gather_xy(ref, width, x0, y0, wx, wy):
    base = x0 * width + y0
    planes = []
    for i in range(11):
        plane = wy[0] * ref[pl.ds(base + i * width, 8), :]
        for t in range(1, 4):
            plane = plane + wy[t] * ref[pl.ds(base + (i * width + t), 8), :]
        planes.append(plane)
    out = []
    for i in range(8):
        value = wx[0] * planes[i]
        for t in range(1, 4):
            value = value + wx[t] * planes[i + t]
        out.append(value)
    return out


def scatter_xy(ref, width, vals, x0, y0, wx, wy):
    sub = subs()
    base = x0 * width + y0
    places = [pl.ds(base + (p * width + 8 * half), 8) for p in range(11) for half in range(2)]
    low_w = [jnp.where(sub >= t, wy[t], 0.0) for t in range(4)]
    high_w = [jnp.where(sub < t, wy[t], 0.0) for t in range(4)]
    pairs = []
    for value in vals:
        first, second = wy[0] * value, None
        for t in range(1, 4):
            turned = pltpu.roll(value, t, 0)
            first = first + low_w[t] * turned
            second = high_w[t] * turned if second is None else second + high_w[t] * turned
        pairs.append((first, second))
    sums = []
    for p in range(11):
        for half in range(2):
            total = ref[places[len(sums)], :]
            for t in range(4):
                if 0 <= p - t < 8:
                    total = total + wx[t] * pairs[p - t][half]
            sums.append(total)
    for place, total in zip(places, sums):
        ref[place, :] = total


def block_of(b):
    return (b + 1) // 2, (b + 1) % 2


def steps_kernel(
    own, xlow, xhigh, ylow, yhigh, corner_low, corner_high, c_low_in, c_high_in, d_low_in, d_high_in,
    up, down, numbers, c_low, c_high, d_low, d_high, r_low, r_high, meta, sem,
):
    (xl, xh), (yl, yh) = inside("gx"), inside("gy")
    lane = lanes()
    upper = lane >= 64
    tiles = (
        (0, xl * corner_low[pl.ds(C_META, 8)]),
        (8, xl * xlow[pl.ds(NUMBERS, 8)]),
        (16, xl * corner_low[pl.ds(C_META + 8, 8)]),
        (24, yl * ylow[pl.ds(NUMBERS, 8)]),
        (32, own[pl.ds(NUMBERS, 8)]),
        (40, yh * yhigh[pl.ds(NUMBERS, 8)]),
        (48, xh * corner_high[pl.ds(C_META, 8)]),
        (56, xh * xhigh[pl.ds(NUMBERS, 8)]),
        (64, xh * corner_high[pl.ds(C_META + 8, 8)]),
    )
    for at, value in tiles:
        numbers[pl.ds(at, 8)] = value
    copy = pltpu.make_async_copy(numbers, meta, sem)
    copy.start()
    upper16 = lanes(T) >= 64

    def corners(x):
        at = pl.multiple_of(x * T, 8)
        for ref, keep, dx in ((corner_low, xl, 0), (corner_high, xh, 32)):
            for start, dy in ((C_LOW, 0), (C_HIGH, 32)):
                a, e = keep * ref[pl.ds(start + at, T)], keep * ref[pl.ds(start + 256 + at, T)]
                put(c_low, c_high, pl.ds(pl.multiple_of((dx + x) * 48 + dy, 8), T), upper16, a, e)

    loop(T, corners, UN_CORNER)

    def corners_second(x):
        at = pl.multiple_of(x * T, 8)
        for ref, keep, dx in ((corner_low, xl, 0), (corner_high, xh, 24)):
            for half, dy in ((0, 0), (8, 24)):
                a, e = keep * ref[pl.ds(C_A1 + half + at, 8)], keep * ref[pl.ds(C_E1 + half + at, 8)]
                put(d_low, d_high, pl.ds(pl.multiple_of((dx + x) * 32 + dy, 8), 8), upper, a, e)

    loop(8, corners_second, UN_CORNER)

    def clear(i):
        rows = pl.ds(pl.multiple_of(i * 128, 8), 128)
        r_low[rows] = jnp.zeros((128, L), F32)
        r_high[rows] = jnp.zeros((128, L), F32)

    loop(10, clear)
    copy.wait()

    def apply(low, high, width, row, step, ix, iy, bx, by):
        places = []
        values = []
        for n in (1, 0, 2):
            (a, b, c), (wx, wy, wz) = block_numbers(meta, row + n, step, ix, iy)
            x0, y0 = bx * 8 + 7 + a, by * 8 + 7 + b
            turns = [(1 - c - t) & 127 for t in range(4)]
            places.append((x0, y0, c, wx, wy, wz))
            if n == 1:
                masks = [jnp.logical_xor(((lane - (c + t - 1)) & -128) == 0, upper) for t in range(4)]
                lows = gather_xy(low, width, x0, y0, wx, wy)
                highs = gather_xy(high, width, x0, y0, wx, wy)
                values.append(
                    [
                        sum(wz[t] * pltpu.roll(jnp.where(masks[t], lows[p], highs[p]), turns[t], 1) for t in range(4))
                        for p in range(8)
                    ]
                )
            else:
                ins = gather_xy(low if n == 0 else high, width, x0, y0, wx, wy)
                values.append([sum(wz[t] * pltpu.roll(value, turns[t], 1) for t in range(4)) for value in ins])
        return places, values

    def first_step(i):
        bx, by = i // 4, i % 4
        (slot_x, ix), (slot_y, iy) = block_of(bx), block_of(by)
        _, (own_z, below, above) = apply(c_low, c_high, 48, slot_x * 24 + slot_y * 8, 0, ix, iy, bx, by)
        for p in range(8):
            rows = pl.ds(pl.multiple_of(bx * 256 + by * 8, 8) + p * 32, 8)
            d_low[rows, :] = d_low[rows, :] + jnp.where(upper, below[p], own_z[p])
            d_high[rows, :] = d_high[rows, :] + jnp.where(upper, own_z[p], above[p])

    loop(16, first_step, UN_FIRST)

    def second_step(i):
        ix, iy = i // 2, i % 2
        places, (own_z, below, above) = apply(d_low, d_high, 32, 32, 1, ix, iy, ix, iy)
        below = [jnp.where(lane >= 96, value, 0.0) for value in below]
        above = [jnp.where(lane < 32, value, 0.0) for value in above]
        x0, y0, c, wx, wy, wz = places[0]
        back = [(c + t - 1) & 127 for t in range(4)]
        masks = [jnp.logical_xor(((lane - (c + t - 1)) & -128) == 0, upper) for t in range(4)]
        low_w = [jnp.where(masks[t], wz[t], 0.0) for t in range(4)]
        high_w = [jnp.where(masks[t], 0.0, wz[t]) for t in range(4)]
        to_low, to_high = [], []
        for value in own_z:
            turned = [pltpu.roll(value, back[t], 1) for t in range(4)]
            to_low.append(sum(low_w[t] * turned[t] for t in range(4)))
            to_high.append(sum(high_w[t] * turned[t] for t in range(4)))
        scatter_xy(r_low, 40, to_low, x0, y0, wx, wy)
        scatter_xy(r_high, 40, to_high, x0, y0, wx, wy)
        for (x0, y0, c, wx, wy, wz), values, ref in ((places[1], below, r_low), (places[2], above, r_high)):
            back = [(c + t - 1) & 127 for t in range(4)]
            moved = [sum(wz[t] * pltpu.roll(value, back[t], 1) for t in range(4)) for value in values]
            scatter_xy(ref, 40, moved, x0, y0, wx, wy)

    loop(4, second_step, UN_SECOND)

    wide = lanes(32)
    wide_upper = wide >= 64
    quarter = ((wide + 16) & 127) // 32

    def pack(i):
        packed = None
        for g in range(4):
            at = 16 * (i // 4) + 4 * g + i % 4
            rows = pl.ds(pl.multiple_of(at * 40, 8), 32)
            low, high = r_low[rows], r_high[rows]
            a = jnp.where(wide_upper, high, low)
            e = roll(jnp.where(wide_upper, low, high), 32 * g)
            packed = e if g == 0 else jnp.where(quarter == g, e, packed)
            down[pl.ds(pl.multiple_of(at * T, 8), T)] = a[0:16]
            up[pl.ds(pl.multiple_of(at * T, 8), T)] = a[16:32]
        down[pl.ds(pl.multiple_of(R_E + i * T, 8), T)] = packed[0:16]
        up[pl.ds(pl.multiple_of(R_E + i * T, 8), T)] = packed[16:32]

    loop(8, pack, UN_PACK)


def sum_y_kernel(own_up, own_down, low, high, up, down):
    low_in, high_in = inside("gy")
    for h, out in ((0, down), (1, up)):
        for start, planes in ((0, 16), (R_E, 4)):
            for x in range(planes):
                rows = pl.ds(start + (h * planes + x) * T, T)
                out[pl.ds(start + x * 32, T)] = own_down[rows] + low_in * low[rows]
                out[pl.ds(start + x * 32 + T, T)] = own_up[rows] + high_in * high[rows]


def last_step_kernel(own_up, own_down, low, high, numbers, g, reg, out, a1, e1, acc, meta, sem):
    copy = pltpu.make_async_copy(numbers, meta, sem)
    copy.start()
    low_in, high_in = inside("gx")
    wide = lanes(32)
    valid = (wide < 16) | (wide >= 112)
    for h, (mine, other, keep) in enumerate(((own_down, low, low_in), (own_up, high, high_in))):

        def unpack(x, h=h, mine=mine, other=other, keep=keep):
            rows = pl.ds(pl.multiple_of(R_E + x * 32, 8), 32)
            packed = mine[rows] + keep * other[rows]
            for q in range(4):
                at = pl.multiple_of((4 * q + x) * 32, 8)
                e1[pl.ds(512 * h + at, 32)] = jnp.where(valid, roll(packed, -32 * q), 0.0)
                a1[pl.ds(512 * h + at, 32)] = mine[pl.ds(at, 32)] + keep * other[pl.ds(at, 32)]

        loop(4, unpack, UN_UNPACK)

    def clear(i):
        acc[pl.ds(pl.multiple_of(i * 168, 8), 168)] = jnp.zeros((168, L), F32)

    loop(16, clear)
    copy.wait()
    lane = lanes()
    upper = lane >= 64

    def step(i):
        bx, by = i // 4, i % 4
        (slot_x, ix), (slot_y, iy) = block_of(bx), block_of(by)
        row = slot_x * 24 + slot_y * 8
        rows = [pl.ds(pl.multiple_of(bx * 256 + by * 8, 8) + p * 32, 8) for p in range(8)]
        inner = [a1[r, :] for r in rows]
        outer = [e1[r, :] for r in rows]
        for n in range(3):
            (a, b, c), (wx, wy, wz) = block_numbers(meta, row + n, 0, ix, iy)
            back = [(c + t - 1) & 127 for t in range(4)]
            if n == 1:
                w = [jnp.where(((lane - (c + t - 1)) & -128) == 0, wz[t], 0.0) for t in range(4)]
                values = inner
            else:
                lands = upper if n == 2 else jnp.logical_not(upper)
                w = [jnp.where(lands, wz[t], 0.0) for t in range(4)]
                values = [jnp.where(upper if n == 0 else jnp.logical_not(upper), value, 0.0) for value in outer]
            moved = [sum(w[t] * pltpu.roll(value, back[t], 1) for t in range(4)) for value in values]
            scatter_xy(acc, 56, moved, bx * 8 + 7 + a, by * 8 + 7 + b, wx, wy)

    loop(16, step, UN_STEP)

    def finish(x):
        first, second = acc[pl.ds(pl.multiple_of((16 + x) * 56 + 16, 8), 16)], a1[pl.ds(pl.multiple_of((8 + x) * 32 + 8, 8), 16)]
        for c in range(3):
            out[c, x] = reg[c, x] + STEP_SIZE * (g[1, c, x].astype(F32) * second + g[0, c, x].astype(F32) * first)

    loop(T, finish, UN_FIN)


def laplace_kernel(v, zlow, zhigh, ylow, yhigh, xlow, xhigh, out, w):
    lane = lanes(T)
    half = (lane & 4) == 0
    (x_low, x_high), (y_low, y_high), (z_low, z_high) = inside("gx"), inside("gy"), inside("gz")
    sides = [-REG_WEIGHT * t for t in LAPLACE_TAPS]
    for c in range(3):
        rows = pl.ds(Z_V + c * T, T)
        faces = jnp.where(half, z_high * zhigh[rows], z_low * zlow[rows])
        for i in range(4):
            rows = pl.ds(FACE + (c * 4 + i) * T, T)
            w[i, 8:24] = x_low * xlow[rows]
            w[20 + i, 8:24] = x_high * xhigh[rows]
        for x in range(8):
            rows = pl.ds(FACE + (c * 8 + x) * 8, 8)
            a, b = y_low * ylow[rows], y_high * yhigh[rows]
            w[4 + x, 0:8] = a
            w[12 + x, 0:8] = pltpu.roll(a, 4, 0)
            w[4 + x, 24:32] = b
            w[12 + x, 24:32] = pltpu.roll(b, 4, 0)
        for x in range(T):
            w[4 + x, 8:24] = v[c, x]
        for x in range(T):
            here = v[c, x]
            edge = roll(faces, -8 * x)
            total = 3.0 * sides[0] * here
            for k in range(1, 5):
                near = roll(jnp.where(lane < k, edge, here), -k) + roll(jnp.where(lane >= L - k, edge, here), k)
                near = near + w[4 + x - k, 8:24] + w[4 + x + k, 8:24]
                near = near + w[4 + x, 8 - k : 24 - k] + w[4 + x, 8 + k : 24 + k]
                total = total + sides[k] * near
            out[c, x] = total


VMEM = pl.BlockSpec(memory_space=pltpu.VMEM)
HBM = pl.BlockSpec(memory_space=pltpu.HBM)


def call(kernel, args, outs, scratch=(), hbm=(), cost=20000, alias=None):
    specs = [HBM if i in hbm else VMEM for i in range(len(args))]
    shapes = [jax.ShapeDtypeStruct(s, F32) for s in outs]
    return pl.pallas_call(
        kernel,
        out_shape=shapes,
        in_specs=specs,
        out_specs=[VMEM] * len(shapes),
        input_output_aliases=alias or {},
        scratch_shapes=list(scratch),
        compiler_params=pltpu.CompilerParams(vmem_limit_bytes=24 * 1024 * 1024),
        cost_estimate=pl.CostEstimate(flops=cost, bytes_accessed=cost, transcendentals=0),
    )(*args)


def exchange(up, down, axis):
    n = lax.axis_size(axis)
    rise = [(i, (i + 1) % n) for i in range(n)]
    fall = [(j, i) for i, j in rise]
    return lax.ppermute(up, axis, rise), lax.ppermute(down, axis, fall)


def body(velocity, gradients, shift_x, shift_y, shift_z, fractions):
    v, g = velocity, gradients
    tile = (T, T, L)
    vm = lambda *s: pltpu.VMEM(s, F32)
    shifts = [s.transpose(0, 1, 3, 2) for s in (shift_x, shift_y, shift_z)]
    s0, s1, zup, zdown = call(
        sources_kernel,
        [pltpu.with_memory_space_constraint(a, pltpu.HBM) for a in (v, g, *shifts, fractions.transpose(0, 2, 3, 4, 1))],
        [tile, tile, (Z_ROWS, L), (Z_ROWS, L)],
        scratch=[vm(*v.shape), pltpu.VMEM(g.shape, g.dtype)]
        + [pltpu.SMEM((2, 2, 1, 2), jnp.int32)] * 3
        + [pltpu.SMEM((2, 2, 2, 1, 3), jnp.int32), pltpu.SemaphoreType.DMA((8,)), pltpu.SemaphoreType.DMA((4,))],
        hbm=range(6),
    )
    zlow, zhigh = exchange(zup, zdown, "gz")
    yup, ydown, xup, xdown = call(tile_messages_kernel, (s0, s1, v, zup, zlow, zhigh), [(ROWS, L)] * 4)
    ylow, yhigh = exchange(yup, ydown, "gy")
    xlow, xhigh = exchange(xup, xdown, "gx")
    up, down = call(corner_message_kernel, (ylow, yhigh, xlow, xhigh), [(C_ROWS, L)] * 2)
    corner_low, corner_high = exchange(up, down, "gx")
    fields = [(48 * 48, L)] * 2 + [(32 * 32, L)] * 2
    filled = call(assemble_kernel, (xup, xdown, xlow, xhigh, ylow, yhigh), fields)
    meta = [pltpu.SMEM((72, L), F32), pltpu.SemaphoreType.DMA]
    up, down, numbers, *_ = call(
        steps_kernel,
        (xup, xlow, xhigh, ylow, yhigh, corner_low, corner_high, *filled),
        [(R_ROWS, L), (R_ROWS, L), (72, L)] + fields,
        scratch=[vm(32 * 40, L), vm(32 * 40, L)] + meta,
        alias={7: 3, 8: 4, 9: 5, 10: 6},
    )
    (reg,) = call(
        laplace_kernel, (v, zlow, zhigh, ylow, yhigh, xlow, xhigh), [v.shape], scratch=[vm(24, 32, L)], cost=4000000
    )
    low, high = exchange(up, down, "gy")
    up, down = call(sum_y_kernel, (up, down, low, high), [(R_ROWS, L)] * 2)
    low, high = exchange(up, down, "gx")
    (out,) = call(
        last_step_kernel,
        (up, down, low, high, numbers, g, reg),
        [v.shape],
        scratch=[vm(32 * 32, L), vm(32 * 32, L), vm(48 * 56, L)] + meta,
    )
    return out


def solution(mesh):
    in_specs = (
        P(None, "gx", "gy", "gz"),
        P(None, None, "gx", "gy", "gz"),
        P(None, "gx", "gy", "gz"),
        P(None, "gx", "gy", "gz"),
        P(None, "gx", "gy", "gz"),
        P(None, None, "gx", "gy", "gz"),
    )
    out_specs = P(None, "gx", "gy", "gz")
    return jax.shard_map(body, mesh=mesh, in_specs=in_specs, out_specs=out_specs, check_vma=False)
```

```python
import jax
import jax.numpy as jnp
from jax import lax
from jax.experimental import pallas as pl
from jax.experimental.pallas import tpu as pltpu
from jax.sharding import PartitionSpec as P

F32 = jnp.float32
LAPLACE_TAPS = (-205.0 / 72.0, 8.0 / 5.0, -1.0 / 5.0, 8.0 / 315.0, -1.0 / 560.0)
STEP_SIZE = 0.5
REG_WEIGHT = 0.1
T = 16
L = 128
UN_ASM, UN_CORNER, UN_FIRST, UN_SECOND, UN_PACK, UN_UNPACK, UN_STEP, UN_FIN = 4, 4, 16, 1, 8, 4, 16, 16
META = 15

Z_S0, Z_S1, Z_V, Z_META, Z_ROWS = 0, 128, 256, 304, 312
Y_S0, Y_S1, Y_FACE, Y_ROWS = 0, 256, 384, 576
Y_E0, Y_E1, Y_META, Y_EROWS = 0, 256, 384, 392
A0, E0, A1, E1, FACE, NUMBERS, ROWS = 0, 256, 512, 640, 768, 960, 968
C_LOW, C_HIGH, C_A1, C_E1, C_META, C_ROWS = 0, 512, 1024, 1152, 1280, 1296
R_E, R_ROWS = 512, 640


def lanes(rows=8):
    return lax.broadcasted_iota(jnp.int32, (rows, L), 1)


def subs():
    return lax.broadcasted_iota(jnp.int32, (8, L), 0)


def roll(x, amount):
    amount = amount % L
    return x if amount == 0 else pltpu.roll(x, amount, 1)


def block_numbers(meta, row, step, ix, iy):
    at = ((step * 2 + ix) * 2 + iy) * META
    shift = [meta[row, at + d].astype(jnp.int32) for d in range(3)]
    weights = [[meta[row, at + 3 + 4 * d + t] for t in range(4)] for d in range(3)]
    return shift, weights


def loop(count, body, unroll=1):
    def step(i, _):
        body(i)
        return 0

    lax.fori_loop(0, count, step, 0, unroll=unroll)


def inside(axis):
    i, n = lax.axis_index(axis), lax.axis_size(axis)
    return jnp.where(i > 0, 1.0, 0.0).astype(F32), jnp.where(i < n - 1, 1.0, 0.0).astype(F32)


def sources_kernel(
    v_hbm, g_hbm, sx_hbm, sy_hbm, sz_hbm, fr_hbm, v, s0, s1, up, down, yup, ydown, g, sx, sy, sz, fr, sem, small_sem
):
    copies = []
    for q in range(4):
        part = pl.ds(4 * q, 4)
        copies.append(pltpu.make_async_copy(v_hbm.at[:, part], v.at[:, part], sem.at[2 * q]))
        copies.append(pltpu.make_async_copy(g_hbm.at[:, :, part], g.at[:, :, part], sem.at[2 * q + 1]))
    small = [
        pltpu.make_async_copy(a, b, small_sem.at[n])
        for n, (a, b) in enumerate(((sx_hbm, sx), (sy_hbm, sy), (sz_hbm, sz), (fr_hbm, fr)))
    ]
    for copy in copies + small:
        copy.start()
    lane = lanes(T)
    for x in range(T):
        if x % 4 == 0:
            copies[x // 2].wait()
            copies[x // 2 + 1].wait()
        vel = [v[c, x] for c in range(3)]
        for k, s in ((0, s0), (1, s1)):
            total = g[k, 0, x].astype(F32) * vel[0]
            for c in (1, 2):
                total = total + g[k, c, x].astype(F32) * vel[c]
            value = STEP_SIZE * total
            s[x] = value
            if k == 0:
                yup[pl.ds(Y_S0 + x * T, T)] = value
                ydown[pl.ds(Y_S0 + x * T, T)] = value
            else:
                yup[pl.ds(Y_S1 + x * 8, 8)] = value[8:16]
                ydown[pl.ds(Y_S1 + x * 8, 8)] = value[0:8]
    first_half = subs() < 4
    for c in range(3):
        for x in range(8):
            rows = pl.ds(Y_FACE + (c * 8 + x) * 8, 8)
            yup[rows] = jnp.where(first_half, pltpu.roll(v[c, x + 8, 8:16], 4, 0), v[c, x, 8:16])
            ydown[rows] = jnp.where(first_half, v[c, x, 0:8], pltpu.roll(v[c, x + 8, 0:8], 4, 0))
    upper = lane >= 64
    for start, s in ((Z_S0, s0), (Z_S1, s1)):
        for x in range(8):
            rows = pl.ds(start + x * T, T)
            a, b = s[x], roll(s[x + 8], 64)
            up[rows] = jnp.where(upper, a, b)
            down[rows] = jnp.where(upper, b, a)
    piece = lane // 8
    for c in range(3):
        u, d = v[c, 0], v[c, 0]
        for x in range(1, T):
            r = roll(v[c, x], 8 * x)
            u = jnp.where(piece == (15 + x) % 16, r, u)
            d = jnp.where(piece == x, r, d)
        up[pl.ds(Z_V + c * T, T)] = u
        down[pl.ds(Z_V + c * T, T)] = d
    lane = lanes()
    for copy in small:
        copy.wait()
    shifts, eighths = jnp.zeros((8, L), jnp.int32), jnp.zeros((8, L), jnp.int32)
    for k in range(2):
        for ix in range(2):
            for iy in range(2):
                at = ((k * 2 + ix) * 2 + iy) * META
                for n, ref in enumerate((sx, sy, sz)):
                    shifts = jnp.where(lane == at + n, ref[k, ix, 0, iy], shifts)
                    first = at + 3 + 4 * n
                    eighths = jnp.where((lane >= first) & (lane < first + 4), fr[k, ix, iy, 0, n], eighths)
    e = eighths.astype(F32) / 8.0
    e2 = e * e
    e3 = e2 * e
    weights = [
        0.5 * (2.0 * e2 - e3 - e),
        0.5 * (3.0 * e3 - 5.0 * e2 + 2.0),
        0.5 * (4.0 * e2 - 3.0 * e3 + e),
        0.5 * (e3 - e2),
    ]
    place = lane % META
    tap = (place - 3) % 4
    row = jnp.where(tap == 0, weights[0], jnp.where(tap == 1, weights[1], jnp.where(tap == 2, weights[2], weights[3])))
    row = jnp.where(place < 3, shifts.astype(F32), row)
    up[pl.ds(Z_META, 8)] = row
    down[pl.ds(Z_META, 8)] = row


def tile_messages_kernel(s0, s1, v, own, low, high, ylow, yhigh, yup, ydown, xup, xdown):
    del ylow, yhigh
    low_in, high_in = inside("gz")
    upper = lanes(T) >= 64
    for start, s in ((Z_S0, s0), (Z_S1, s1)):
        for j in range(8):
            a, b = low_in * low[pl.ds(start + j * T, T)], high_in * high[pl.ds(start + j * T, T)]
            edges = (jnp.where(upper, a, b), roll(jnp.where(upper, b, a), 64))
            for h, edge in enumerate(edges):
                x = j + 8 * h
                if start == Z_S0:
                    for out in (xup, xdown):
                        out[pl.ds(A0 + x * T, T)] = s[x]
                        out[pl.ds(E0 + x * T, T)] = edge
                    for out in (yup, ydown):
                        out[pl.ds(Y_E0 + x * T, T)] = edge
                else:
                    yup[pl.ds(Y_E1 + x * 8, 8)] = edge[8:16]
                    ydown[pl.ds(Y_E1 + x * 8, 8)] = edge[0:8]
                    out = (xdown, xup)[h]
                    out[pl.ds(A1 + j * T, T)] = s[x]
                    out[pl.ds(E1 + j * T, T)] = edge
    for c in range(3):
        for i in range(4):
            xup[pl.ds(FACE + (c * 4 + i) * T, T)] = v[c, 12 + i]
            xdown[pl.ds(FACE + (c * 4 + i) * T, T)] = v[c, i]
    sub = subs()
    meta = [ref[pl.ds(Z_META, 8)] for ref in (low, own, high)]
    row = jnp.where(sub == 0, low_in * meta[0], jnp.where(sub == 1, meta[1], high_in * meta[2]))
    for out, at in ((yup, Y_META), (ydown, Y_META), (xup, NUMBERS), (xdown, NUMBERS)):
        out[pl.ds(at, 8)] = row


def corner_message_kernel(low, high, elow, ehigh, xlow, xhigh, up, down):
    del xlow, xhigh
    sides = ((low, elow, C_LOW), (high, ehigh, C_HIGH))
    for y, ((a, e, to), keep) in enumerate(zip(sides, inside("gy"))):
        for x in range(T):
            for at, value in ((0, a[pl.ds(Y_S0 + x * T, T)]), (256, e[pl.ds(Y_E0 + x * T, T)])):
                value = keep * value
                up[pl.ds(to + at + x * T, T)] = value
                down[pl.ds(to + at + x * T, T)] = value
        for ref, start, place in ((a, Y_S1, C_A1), (e, Y_E1, C_E1)):
            for x in range(8):
                down[pl.ds(place + x * T + 8 * y, 8)] = keep * ref[pl.ds(start + x * 8, 8)]
                up[pl.ds(place + x * T + 8 * y, 8)] = keep * ref[pl.ds(start + (8 + x) * 8, 8)]
        value = keep * e[pl.ds(Y_META, 8)]
        up[pl.ds(C_META + 8 * y, 8)] = value
        down[pl.ds(C_META + 8 * y, 8)] = value


def put(low, high, rows, upper, a, e):
    low[rows] = jnp.where(upper, e, a)
    high[rows] = jnp.where(upper, a, e)


def assemble_kernel(own_up, own_down, xlow, xhigh, ylow, yhigh, elow, ehigh, c_low, c_high, d_low, d_high):
    (xl, xh), (yl, yh) = inside("gx"), inside("gy")
    upper, upper8 = lanes(T) >= 64, lanes(8) >= 64

    def first(x):
        at = pl.multiple_of(x * T, 8)
        for ref, keep, dx in ((own_up, None, 16), (xlow, xl, 0), (xhigh, xh, 32)):
            a, e = ref[pl.ds(A0 + at, T)], ref[pl.ds(E0 + at, T)]
            if keep is not None:
                a, e = keep * a, keep * e
            put(c_low, c_high, pl.ds(pl.multiple_of((dx + x) * 48 + 16, 8), T), upper, a, e)
        for ref, eref, keep, dy in ((ylow, elow, yl, 0), (yhigh, ehigh, yh, 32)):
            a, e = keep * ref[pl.ds(Y_S0 + at, T)], keep * eref[pl.ds(Y_E0 + at, T)]
            put(c_low, c_high, pl.ds(pl.multiple_of((16 + x) * 48 + dy, 8), T), upper, a, e)

    loop(T, first, UN_ASM)

    def second(x):
        at = pl.multiple_of(x * T, 8)
        for ref, keep, dx in ((own_down, None, 8), (own_up, None, 16), (xlow, xl, 0), (xhigh, xh, 24)):
            a, e = ref[pl.ds(A1 + at, T)], ref[pl.ds(E1 + at, T)]
            if keep is not None:
                a, e = keep * a, keep * e
            put(d_low, d_high, pl.ds(pl.multiple_of((dx + x) * 32 + 8, 8), T), upper, a, e)
        for h in range(2):
            at = pl.multiple_of((8 * h + x) * 8, 8)
            for ref, eref, keep, dy in ((ylow, elow, yl, 0), (yhigh, ehigh, yh, 24)):
                a, e = keep * ref[pl.ds(Y_S1 + at, 8)], keep * eref[pl.ds(Y_E1 + at, 8)]
                put(d_low, d_high, pl.ds(pl.multiple_of((8 + 8 * h + x) * 32 + dy, 8), 8), upper8, a, e)

    loop(8, second, UN_ASM)


def gather_xy(ref, width, x0, y0, wx, wy):
    base = x0 * width + y0
    planes = []
    for i in range(11):
        plane = wy[0] * ref[pl.ds(base + i * width, 8), :]
        for t in range(1, 4):
            plane = plane + wy[t] * ref[pl.ds(base + (i * width + t), 8), :]
        planes.append(plane)
    out = []
    for i in range(8):
        value = wx[0] * planes[i]
        for t in range(1, 4):
            value = value + wx[t] * planes[i + t]
        out.append(value)
    return out


def scatter_xy(ref, width, vals, x0, y0, wx, wy):
    sub = subs()
    base = x0 * width + y0
    places = [pl.ds(base + (p * width + 8 * half), 8) for p in range(11) for half in range(2)]
    low_w = [jnp.where(sub >= t, wy[t], 0.0) for t in range(4)]
    high_w = [jnp.where(sub < t, wy[t], 0.0) for t in range(4)]
    pairs = []
    for value in vals:
        first, second = wy[0] * value, None
        for t in range(1, 4):
            turned = pltpu.roll(value, t, 0)
            first = first + low_w[t] * turned
            second = high_w[t] * turned if second is None else second + high_w[t] * turned
        pairs.append((first, second))
    sums = []
    for p in range(11):
        for half in range(2):
            total = ref[places[len(sums)], :]
            for t in range(4):
                if 0 <= p - t < 8:
                    total = total + wx[t] * pairs[p - t][half]
            sums.append(total)
    for place, total in zip(places, sums):
        ref[place, :] = total


def block_of(b):
    return (b + 1) // 2, (b + 1) % 2


def steps_kernel(
    own, xlow, xhigh, ylow, yhigh, corner_low, corner_high, c_low_in, c_high_in, d_low_in, d_high_in,
    up, down, numbers, c_low, c_high, d_low, d_high, r_low, r_high, meta, sem,
):
    (xl, xh), (yl, yh) = inside("gx"), inside("gy")
    lane = lanes()
    upper = lane >= 64
    tiles = (
        (0, xl * corner_low[pl.ds(C_META, 8)]),
        (8, xl * xlow[pl.ds(NUMBERS, 8)]),
        (16, xl * corner_low[pl.ds(C_META + 8, 8)]),
        (24, yl * ylow[pl.ds(Y_META, 8)]),
        (32, own[pl.ds(NUMBERS, 8)]),
        (40, yh * yhigh[pl.ds(Y_META, 8)]),
        (48, xh * corner_high[pl.ds(C_META, 8)]),
        (56, xh * xhigh[pl.ds(NUMBERS, 8)]),
        (64, xh * corner_high[pl.ds(C_META + 8, 8)]),
    )
    for at, value in tiles:
        numbers[pl.ds(at, 8)] = value
    copy = pltpu.make_async_copy(numbers, meta, sem)
    copy.start()
    upper16 = lanes(T) >= 64

    def corners(x):
        at = pl.multiple_of(x * T, 8)
        for ref, keep, dx in ((corner_low, xl, 0), (corner_high, xh, 32)):
            for start, dy in ((C_LOW, 0), (C_HIGH, 32)):
                a, e = keep * ref[pl.ds(start + at, T)], keep * ref[pl.ds(start + 256 + at, T)]
                put(c_low, c_high, pl.ds(pl.multiple_of((dx + x) * 48 + dy, 8), T), upper16, a, e)

    loop(T, corners, UN_CORNER)

    def corners_second(x):
        at = pl.multiple_of(x * T, 8)
        for ref, keep, dx in ((corner_low, xl, 0), (corner_high, xh, 24)):
            for half, dy in ((0, 0), (8, 24)):
                a, e = keep * ref[pl.ds(C_A1 + half + at, 8)], keep * ref[pl.ds(C_E1 + half + at, 8)]
                put(d_low, d_high, pl.ds(pl.multiple_of((dx + x) * 32 + dy, 8), 8), upper, a, e)

    loop(8, corners_second, UN_CORNER)

    def clear(i):
        rows = pl.ds(pl.multiple_of(i * 128, 8), 128)
        r_low[rows] = jnp.zeros((128, L), F32)
        r_high[rows] = jnp.zeros((128, L), F32)

    loop(10, clear)
    copy.wait()

    def apply(low, high, width, row, step, ix, iy, bx, by):
        places = []
        values = []
        for n in (1, 0, 2):
            (a, b, c), (wx, wy, wz) = block_numbers(meta, row + n, step, ix, iy)
            x0, y0 = bx * 8 + 7 + a, by * 8 + 7 + b
            turns = [(1 - c - t) & 127 for t in range(4)]
            places.append((x0, y0, c, wx, wy, wz))
            if n == 1:
                masks = [jnp.logical_xor(((lane - (c + t - 1)) & -128) == 0, upper) for t in range(4)]
                lows = gather_xy(low, width, x0, y0, wx, wy)
                highs = gather_xy(high, width, x0, y0, wx, wy)
                values.append(
                    [
                        sum(wz[t] * pltpu.roll(jnp.where(masks[t], lows[p], highs[p]), turns[t], 1) for t in range(4))
                        for p in range(8)
                    ]
                )
            else:
                ins = gather_xy(low if n == 0 else high, width, x0, y0, wx, wy)
                values.append([sum(wz[t] * pltpu.roll(value, turns[t], 1) for t in range(4)) for value in ins])
        return places, values

    def first_step(i):
        bx, by = i // 4, i % 4
        (slot_x, ix), (slot_y, iy) = block_of(bx), block_of(by)
        _, (own_z, below, above) = apply(c_low, c_high, 48, slot_x * 24 + slot_y * 8, 0, ix, iy, bx, by)
        for p in range(8):
            rows = pl.ds(pl.multiple_of(bx * 256 + by * 8, 8) + p * 32, 8)
            d_low[rows, :] = d_low[rows, :] + jnp.where(upper, below[p], own_z[p])
            d_high[rows, :] = d_high[rows, :] + jnp.where(upper, own_z[p], above[p])

    loop(16, first_step, UN_FIRST)

    def second_step(i):
        ix, iy = i // 2, i % 2
        places, (own_z, below, above) = apply(d_low, d_high, 32, 32, 1, ix, iy, ix, iy)
        below = [jnp.where(lane >= 96, value, 0.0) for value in below]
        above = [jnp.where(lane < 32, value, 0.0) for value in above]
        x0, y0, c, wx, wy, wz = places[0]
        back = [(c + t - 1) & 127 for t in range(4)]
        masks = [jnp.logical_xor(((lane - (c + t - 1)) & -128) == 0, upper) for t in range(4)]
        low_w = [jnp.where(masks[t], wz[t], 0.0) for t in range(4)]
        high_w = [jnp.where(masks[t], 0.0, wz[t]) for t in range(4)]
        to_low, to_high = [], []
        for value in own_z:
            turned = [pltpu.roll(value, back[t], 1) for t in range(4)]
            to_low.append(sum(low_w[t] * turned[t] for t in range(4)))
            to_high.append(sum(high_w[t] * turned[t] for t in range(4)))
        scatter_xy(r_low, 40, to_low, x0, y0, wx, wy)
        scatter_xy(r_high, 40, to_high, x0, y0, wx, wy)
        for (x0, y0, c, wx, wy, wz), values, ref in ((places[1], below, r_low), (places[2], above, r_high)):
            back = [(c + t - 1) & 127 for t in range(4)]
            moved = [sum(wz[t] * pltpu.roll(value, back[t], 1) for t in range(4)) for value in values]
            scatter_xy(ref, 40, moved, x0, y0, wx, wy)

    loop(4, second_step, UN_SECOND)

    wide = lanes(32)
    wide_upper = wide >= 64
    quarter = ((wide + 16) & 127) // 32

    def pack(i):
        packed = None
        for g in range(4):
            at = 16 * (i // 4) + 4 * g + i % 4
            rows = pl.ds(pl.multiple_of(at * 40, 8), 32)
            low, high = r_low[rows], r_high[rows]
            a = jnp.where(wide_upper, high, low)
            e = roll(jnp.where(wide_upper, low, high), 32 * g)
            packed = e if g == 0 else jnp.where(quarter == g, e, packed)
            down[pl.ds(pl.multiple_of(at * T, 8), T)] = a[0:16]
            up[pl.ds(pl.multiple_of(at * T, 8), T)] = a[16:32]
        down[pl.ds(pl.multiple_of(R_E + i * T, 8), T)] = packed[0:16]
        up[pl.ds(pl.multiple_of(R_E + i * T, 8), T)] = packed[16:32]

    loop(8, pack, UN_PACK)


def sum_y_kernel(own_up, own_down, low, high, up, down):
    low_in, high_in = inside("gy")
    for h, out in ((0, down), (1, up)):
        for start, planes in ((0, 16), (R_E, 4)):
            for x in range(planes):
                rows = pl.ds(start + (h * planes + x) * T, T)
                out[pl.ds(start + x * 32, T)] = own_down[rows] + low_in * low[rows]
                out[pl.ds(start + x * 32 + T, T)] = own_up[rows] + high_in * high[rows]


def last_step_kernel(own_up, own_down, low, high, numbers, g, reg, out, a1, e1, acc, meta, sem):
    copy = pltpu.make_async_copy(numbers, meta, sem)
    copy.start()
    low_in, high_in = inside("gx")
    wide = lanes(32)
    valid = (wide < 16) | (wide >= 112)
    for h, (mine, other, keep) in enumerate(((own_down, low, low_in), (own_up, high, high_in))):

        def unpack(x, h=h, mine=mine, other=other, keep=keep):
            rows = pl.ds(pl.multiple_of(R_E + x * 32, 8), 32)
            packed = mine[rows] + keep * other[rows]
            for q in range(4):
                at = pl.multiple_of((4 * q + x) * 32, 8)
                e1[pl.ds(512 * h + at, 32)] = jnp.where(valid, roll(packed, -32 * q), 0.0)
                a1[pl.ds(512 * h + at, 32)] = mine[pl.ds(at, 32)] + keep * other[pl.ds(at, 32)]

        loop(4, unpack, UN_UNPACK)

    def clear(i):
        acc[pl.ds(pl.multiple_of(i * 168, 8), 168)] = jnp.zeros((168, L), F32)

    loop(16, clear)
    copy.wait()
    lane = lanes()
    upper = lane >= 64

    def step(i):
        bx, by = i // 4, i % 4
        (slot_x, ix), (slot_y, iy) = block_of(bx), block_of(by)
        row = slot_x * 24 + slot_y * 8
        rows = [pl.ds(pl.multiple_of(bx * 256 + by * 8, 8) + p * 32, 8) for p in range(8)]
        inner = [a1[r, :] for r in rows]
        outer = [e1[r, :] for r in rows]
        for n in range(3):
            (a, b, c), (wx, wy, wz) = block_numbers(meta, row + n, 0, ix, iy)
            back = [(c + t - 1) & 127 for t in range(4)]
            if n == 1:
                w = [jnp.where(((lane - (c + t - 1)) & -128) == 0, wz[t], 0.0) for t in range(4)]
                values = inner
            else:
                lands = upper if n == 2 else jnp.logical_not(upper)
                w = [jnp.where(lands, wz[t], 0.0) for t in range(4)]
                values = [jnp.where(upper if n == 0 else jnp.logical_not(upper), value, 0.0) for value in outer]
            moved = [sum(w[t] * pltpu.roll(value, back[t], 1) for t in range(4)) for value in values]
            scatter_xy(acc, 56, moved, bx * 8 + 7 + a, by * 8 + 7 + b, wx, wy)

    loop(16, step, UN_STEP)

    def finish(x):
        first, second = acc[pl.ds(pl.multiple_of((16 + x) * 56 + 16, 8), 16)], a1[pl.ds(pl.multiple_of((8 + x) * 32 + 8, 8), 16)]
        for c in range(3):
            out[c, x] = reg[c, x] + STEP_SIZE * (g[1, c, x].astype(F32) * second + g[0, c, x].astype(F32) * first)

    loop(T, finish, UN_FIN)


def laplace_kernel(v, zlow, zhigh, ylow, yhigh, xlow, xhigh, out, w):
    lane = lanes(T)
    half = (lane & 4) == 0
    (x_low, x_high), (y_low, y_high), (z_low, z_high) = inside("gx"), inside("gy"), inside("gz")
    sides = [-REG_WEIGHT * t for t in LAPLACE_TAPS]
    for c in range(3):
        rows = pl.ds(Z_V + c * T, T)
        faces = jnp.where(half, z_high * zhigh[rows], z_low * zlow[rows])
        for i in range(4):
            rows = pl.ds(FACE + (c * 4 + i) * T, T)
            w[i, 8:24] = x_low * xlow[rows]
            w[20 + i, 8:24] = x_high * xhigh[rows]
        for x in range(8):
            rows = pl.ds(Y_FACE + (c * 8 + x) * 8, 8)
            a, b = y_low * ylow[rows], y_high * yhigh[rows]
            w[4 + x, 0:8] = a
            w[12 + x, 0:8] = pltpu.roll(a, 4, 0)
            w[4 + x, 24:32] = b
            w[12 + x, 24:32] = pltpu.roll(b, 4, 0)
        for x in range(T):
            w[4 + x, 8:24] = v[c, x]
        for x in range(T):
            here = v[c, x]
            edge = roll(faces, -8 * x)
            total = 3.0 * sides[0] * here
            for k in range(1, 5):
                near = roll(jnp.where(lane < k, edge, here), -k) + roll(jnp.where(lane >= L - k, edge, here), k)
                near = near + w[4 + x - k, 8:24] + w[4 + x + k, 8:24]
                near = near + w[4 + x, 8 - k : 24 - k] + w[4 + x, 8 + k : 24 + k]
                total = total + sides[k] * near
            out[c, x] = total


VMEM = pl.BlockSpec(memory_space=pltpu.VMEM)
HBM = pl.BlockSpec(memory_space=pltpu.HBM)


def call(kernel, args, outs, scratch=(), hbm=(), cost=20000, alias=None):
    specs = [HBM if i in hbm else VMEM for i in range(len(args))]
    shapes = [jax.ShapeDtypeStruct(s, F32) for s in outs]
    return pl.pallas_call(
        kernel,
        out_shape=shapes,
        in_specs=specs,
        out_specs=[VMEM] * len(shapes),
        input_output_aliases=alias or {},
        scratch_shapes=list(scratch),
        compiler_params=pltpu.CompilerParams(vmem_limit_bytes=24 * 1024 * 1024),
        cost_estimate=pl.CostEstimate(flops=cost, bytes_accessed=cost, transcendentals=0),
    )(*args)


def exchange(up, down, axis):
    n = lax.axis_size(axis)
    rise = [(i, (i + 1) % n) for i in range(n)]
    fall = [(j, i) for i, j in rise]
    return lax.ppermute(up, axis, rise), lax.ppermute(down, axis, fall)


def body(velocity, gradients, shift_x, shift_y, shift_z, fractions):
    v, g = velocity, gradients
    tile = (T, T, L)
    vm = lambda *s: pltpu.VMEM(s, F32)
    shifts = [s.transpose(0, 1, 3, 2) for s in (shift_x, shift_y, shift_z)]
    inputs = [v, g, *shifts, fractions.transpose(0, 2, 3, 4, 1)]
    v, s0, s1, zup, zdown, yup, ydown = call(
        sources_kernel,
        [pltpu.with_memory_space_constraint(a, pltpu.HBM) for a in inputs],
        [v.shape, tile, tile, (Z_ROWS, L), (Z_ROWS, L), (Y_ROWS, L), (Y_ROWS, L)],
        scratch=[pltpu.VMEM(g.shape, g.dtype)]
        + [pltpu.SMEM((2, 2, 1, 2), jnp.int32)] * 3
        + [pltpu.SMEM((2, 2, 2, 1, 3), jnp.int32), pltpu.SemaphoreType.DMA((8,)), pltpu.SemaphoreType.DMA((4,))],
        hbm=range(6),
    )
    zlow, zhigh = exchange(zup, zdown, "gz")
    ylow, yhigh = exchange(yup, ydown, "gy")
    yup, ydown, xup, xdown = call(
        tile_messages_kernel, (s0, s1, v, zup, zlow, zhigh, ylow, yhigh), [(Y_EROWS, L)] * 2 + [(ROWS, L)] * 2
    )
    elow, ehigh = exchange(yup, ydown, "gy")
    xlow, xhigh = exchange(xup, xdown, "gx")
    up, down = call(corner_message_kernel, (ylow, yhigh, elow, ehigh, xlow, xhigh), [(C_ROWS, L)] * 2)
    corner_low, corner_high = exchange(up, down, "gx")
    fields = [(48 * 48, L)] * 2 + [(32 * 32, L)] * 2
    filled = call(assemble_kernel, (xup, xdown, xlow, xhigh, ylow, yhigh, elow, ehigh), fields)
    meta = [pltpu.SMEM((72, L), F32), pltpu.SemaphoreType.DMA]
    up, down, numbers, *_ = call(
        steps_kernel,
        (xup, xlow, xhigh, elow, ehigh, corner_low, corner_high, *filled),
        [(R_ROWS, L), (R_ROWS, L), (72, L)] + fields,
        scratch=[vm(32 * 40, L), vm(32 * 40, L)] + meta,
        alias={7: 3, 8: 4, 9: 5, 10: 6},
    )
    (reg,) = call(
        laplace_kernel, (v, zlow, zhigh, ylow, yhigh, xlow, xhigh), [v.shape], scratch=[vm(24, 32, L)], cost=4000000
    )
    low, high = exchange(up, down, "gy")
    up, down = call(sum_y_kernel, (up, down, low, high), [(R_ROWS, L)] * 2)
    low, high = exchange(up, down, "gx")
    (out,) = call(
        last_step_kernel,
        (up, down, low, high, numbers, g, reg),
        [v.shape],
        scratch=[vm(32 * 32, L), vm(32 * 32, L), vm(48 * 56, L)] + meta,
    )
    return out


def solution(mesh):
    in_specs = (
        P(None, "gx", "gy", "gz"),
        P(None, None, "gx", "gy", "gz"),
        P(None, "gx", "gy", "gz"),
        P(None, "gx", "gy", "gz"),
        P(None, "gx", "gy", "gz"),
        P(None, None, "gx", "gy", "gz"),
    )
    out_specs = P(None, "gx", "gy", "gz")
    return jax.shard_map(body, mesh=mesh, in_specs=in_specs, out_specs=out_specs, check_vma=False)
```

```python
import jax
import jax.numpy as jnp
from jax import lax
from jax.experimental import pallas as pl
from jax.experimental.pallas import tpu as pltpu
from jax.sharding import PartitionSpec as P

F32 = jnp.float32
LAPLACE_TAPS = (-205.0 / 72.0, 8.0 / 5.0, -1.0 / 5.0, 8.0 / 315.0, -1.0 / 560.0)
STEP_SIZE = 0.5
REG_WEIGHT = 0.1
T = 16
L = 128
UN_ASM, UN_CORNER, UN_FIRST, UN_SECOND, UN_PACK, UN_UNPACK = 8, 16, 16, 4, 8, 4
META = 15

Z_S0, Z_S1, Z_V, Z_META, Z_ROWS = 0, 128, 256, 304, 312
Y_S0, Y_S1, Y_FACE, Y_ROWS = 0, 256, 384, 576
Y_E0, Y_E1, Y_META, Y_EROWS = 0, 256, 384, 392
A0, E0, A1, E1, FACE, NUMBERS, ROWS = 0, 256, 512, 640, 768, 960, 968
C_LOW, C_HIGH, C_A1, C_E1, C_META, C_ROWS = 0, 512, 1024, 1152, 1280, 1296
R_E, R_ROWS = 512, 640


def lanes(rows=8):
    return lax.broadcasted_iota(jnp.int32, (rows, L), 1)


def subs():
    return lax.broadcasted_iota(jnp.int32, (8, L), 0)


def roll(x, amount):
    amount = amount % L
    return x if amount == 0 else pltpu.roll(x, amount, 1)


def block_numbers(meta, row, step, ix, iy):
    at = ((step * 2 + ix) * 2 + iy) * META
    shift = [meta[row, at + d].astype(jnp.int32) for d in range(3)]
    weights = [[meta[row, at + 3 + 4 * d + t] for t in range(4)] for d in range(3)]
    return shift, weights


def loop(count, body, unroll=1):
    def step(i, _):
        body(i)
        return 0

    lax.fori_loop(0, count, step, 0, unroll=unroll)


def inside(axis):
    i, n = lax.axis_index(axis), lax.axis_size(axis)
    return jnp.where(i > 0, 1.0, 0.0).astype(F32), jnp.where(i < n - 1, 1.0, 0.0).astype(F32)


def sources_kernel(
    v_hbm, g_hbm, sx_hbm, sy_hbm, sz_hbm, fr_hbm, v, s0, s1, up, down, yup, ydown, g, sx, sy, sz, fr, sem, small_sem
):
    copies = []
    for q in range(4):
        part = pl.ds(4 * q, 4)
        copies.append(pltpu.make_async_copy(v_hbm.at[:, part], v.at[:, part], sem.at[2 * q]))
        copies.append(pltpu.make_async_copy(g_hbm.at[:, :, part], g.at[:, :, part], sem.at[2 * q + 1]))
    small = [
        pltpu.make_async_copy(a, b, small_sem.at[n])
        for n, (a, b) in enumerate(((sx_hbm, sx), (sy_hbm, sy), (sz_hbm, sz), (fr_hbm, fr)))
    ]
    for copy in copies + small:
        copy.start()
    lane = lanes(T)
    for x in range(T):
        if x % 4 == 0:
            copies[x // 2].wait()
            copies[x // 2 + 1].wait()
        vel = [v[c, x] for c in range(3)]
        for k, s in ((0, s0), (1, s1)):
            total = g[k, 0, x].astype(F32) * vel[0]
            for c in (1, 2):
                total = total + g[k, c, x].astype(F32) * vel[c]
            value = STEP_SIZE * total
            s[x] = value
            if k == 0:
                yup[pl.ds(Y_S0 + x * T, T)] = value
                ydown[pl.ds(Y_S0 + x * T, T)] = value
            else:
                yup[pl.ds(Y_S1 + x * 8, 8)] = value[8:16]
                ydown[pl.ds(Y_S1 + x * 8, 8)] = value[0:8]
    first_half = subs() < 4
    for c in range(3):
        for x in range(8):
            rows = pl.ds(Y_FACE + (c * 8 + x) * 8, 8)
            yup[rows] = jnp.where(first_half, pltpu.roll(v[c, x + 8, 8:16], 4, 0), v[c, x, 8:16])
            ydown[rows] = jnp.where(first_half, v[c, x, 0:8], pltpu.roll(v[c, x + 8, 0:8], 4, 0))
    upper = lane >= 64
    for start, s in ((Z_S0, s0), (Z_S1, s1)):
        for x in range(8):
            rows = pl.ds(start + x * T, T)
            a, b = s[x], roll(s[x + 8], 64)
            up[rows] = jnp.where(upper, a, b)
            down[rows] = jnp.where(upper, b, a)
    piece = lane // 8
    for c in range(3):
        u, d = v[c, 0], v[c, 0]
        for x in range(1, T):
            r = roll(v[c, x], 8 * x)
            u = jnp.where(piece == (15 + x) % 16, r, u)
            d = jnp.where(piece == x, r, d)
        up[pl.ds(Z_V + c * T, T)] = u
        down[pl.ds(Z_V + c * T, T)] = d
    lane = lanes()
    for copy in small:
        copy.wait()
    shifts, eighths = jnp.zeros((8, L), jnp.int32), jnp.zeros((8, L), jnp.int32)
    for k in range(2):
        for ix in range(2):
            for iy in range(2):
                at = ((k * 2 + ix) * 2 + iy) * META
                for n, ref in enumerate((sx, sy, sz)):
                    shifts = jnp.where(lane == at + n, ref[k, ix, 0, iy], shifts)
                    first = at + 3 + 4 * n
                    eighths = jnp.where((lane >= first) & (lane < first + 4), fr[k, ix, iy, 0, n], eighths)
    e = eighths.astype(F32) / 8.0
    e2 = e * e
    e3 = e2 * e
    weights = [
        0.5 * (2.0 * e2 - e3 - e),
        0.5 * (3.0 * e3 - 5.0 * e2 + 2.0),
        0.5 * (4.0 * e2 - 3.0 * e3 + e),
        0.5 * (e3 - e2),
    ]
    place = lane % META
    tap = (place - 3) % 4
    row = jnp.where(tap == 0, weights[0], jnp.where(tap == 1, weights[1], jnp.where(tap == 2, weights[2], weights[3])))
    row = jnp.where(place < 3, shifts.astype(F32), row)
    up[pl.ds(Z_META, 8)] = row
    down[pl.ds(Z_META, 8)] = row


def tile_messages_kernel(s0, s1, v, own, low, high, ylow, yhigh, yup, ydown, xup, xdown):
    del ylow, yhigh
    low_in, high_in = inside("gz")
    upper = lanes(T) >= 64
    for start, s in ((Z_S0, s0), (Z_S1, s1)):
        for j in range(8):
            a, b = low_in * low[pl.ds(start + j * T, T)], high_in * high[pl.ds(start + j * T, T)]
            edges = (jnp.where(upper, a, b), roll(jnp.where(upper, b, a), 64))
            for h, edge in enumerate(edges):
                x = j + 8 * h
                if start == Z_S0:
                    for out in (xup, xdown):
                        out[pl.ds(A0 + x * T, T)] = s[x]
                        out[pl.ds(E0 + x * T, T)] = edge
                    for out in (yup, ydown):
                        out[pl.ds(Y_E0 + x * T, T)] = edge
                else:
                    yup[pl.ds(Y_E1 + x * 8, 8)] = edge[8:16]
                    ydown[pl.ds(Y_E1 + x * 8, 8)] = edge[0:8]
                    out = (xdown, xup)[h]
                    out[pl.ds(A1 + j * T, T)] = s[x]
                    out[pl.ds(E1 + j * T, T)] = edge
    for c in range(3):
        for i in range(4):
            xup[pl.ds(FACE + (c * 4 + i) * T, T)] = v[c, 12 + i]
            xdown[pl.ds(FACE + (c * 4 + i) * T, T)] = v[c, i]
    sub = subs()
    meta = [ref[pl.ds(Z_META, 8)] for ref in (low, own, high)]
    row = jnp.where(sub == 0, low_in * meta[0], jnp.where(sub == 1, meta[1], high_in * meta[2]))
    for out, at in ((yup, Y_META), (ydown, Y_META), (xup, NUMBERS), (xdown, NUMBERS)):
        out[pl.ds(at, 8)] = row


def corner_message_kernel(low, high, elow, ehigh, xlow, xhigh, up, down):
    del xlow, xhigh
    sides = ((low, elow, C_LOW), (high, ehigh, C_HIGH))
    for y, ((a, e, to), keep) in enumerate(zip(sides, inside("gy"))):
        for x in range(T):
            for at, value in ((0, a[pl.ds(Y_S0 + x * T, T)]), (256, e[pl.ds(Y_E0 + x * T, T)])):
                value = keep * value
                up[pl.ds(to + at + x * T, T)] = value
                down[pl.ds(to + at + x * T, T)] = value
        for ref, start, place in ((a, Y_S1, C_A1), (e, Y_E1, C_E1)):
            for x in range(8):
                down[pl.ds(place + x * T + 8 * y, 8)] = keep * ref[pl.ds(start + x * 8, 8)]
                up[pl.ds(place + x * T + 8 * y, 8)] = keep * ref[pl.ds(start + (8 + x) * 8, 8)]
        value = keep * e[pl.ds(Y_META, 8)]
        up[pl.ds(C_META + 8 * y, 8)] = value
        down[pl.ds(C_META + 8 * y, 8)] = value


def put(low, high, rows, upper, a, e):
    low[rows] = jnp.where(upper, e, a)
    high[rows] = jnp.where(upper, a, e)


def assemble_kernel(own_up, own_down, xlow, xhigh, ylow, yhigh, elow, ehigh, c_low, c_high, d_low, d_high):
    (xl, xh), (yl, yh) = inside("gx"), inside("gy")
    upper, upper8 = lanes(T) >= 64, lanes(8) >= 64

    def first(x):
        at = pl.multiple_of(x * T, 8)
        for ref, keep, dx in ((own_up, None, 16), (xlow, xl, 0), (xhigh, xh, 32)):
            a, e = ref[pl.ds(A0 + at, T)], ref[pl.ds(E0 + at, T)]
            if keep is not None:
                a, e = keep * a, keep * e
            put(c_low, c_high, pl.ds(pl.multiple_of((dx + x) * 48 + 16, 8), T), upper, a, e)
        for ref, eref, keep, dy in ((ylow, elow, yl, 0), (yhigh, ehigh, yh, 32)):
            a, e = keep * ref[pl.ds(Y_S0 + at, T)], keep * eref[pl.ds(Y_E0 + at, T)]
            put(c_low, c_high, pl.ds(pl.multiple_of((16 + x) * 48 + dy, 8), T), upper, a, e)

    loop(T, first, UN_ASM)

    def second(x):
        at = pl.multiple_of(x * T, 8)
        for ref, keep, dx in ((own_down, None, 8), (own_up, None, 16), (xlow, xl, 0), (xhigh, xh, 24)):
            a, e = ref[pl.ds(A1 + at, T)], ref[pl.ds(E1 + at, T)]
            if keep is not None:
                a, e = keep * a, keep * e
            put(d_low, d_high, pl.ds(pl.multiple_of((dx + x) * 32 + 8, 8), T), upper, a, e)
        for h in range(2):
            at = pl.multiple_of((8 * h + x) * 8, 8)
            for ref, eref, keep, dy in ((ylow, elow, yl, 0), (yhigh, ehigh, yh, 24)):
                a, e = keep * ref[pl.ds(Y_S1 + at, 8)], keep * eref[pl.ds(Y_E1 + at, 8)]
                put(d_low, d_high, pl.ds(pl.multiple_of((8 + 8 * h + x) * 32 + dy, 8), 8), upper8, a, e)

    loop(8, second, UN_ASM)


def gather_xy(ref, width, x0, y0, wx, wy):
    base = x0 * width + y0
    planes = []
    for i in range(11):
        plane = wy[0] * ref[pl.ds(base + i * width, 8), :]
        for t in range(1, 4):
            plane = plane + wy[t] * ref[pl.ds(base + (i * width + t), 8), :]
        planes.append(plane)
    out = []
    for i in range(8):
        value = wx[0] * planes[i]
        for t in range(1, 4):
            value = value + wx[t] * planes[i + t]
        out.append(value)
    return out


def scatter_xy(ref, width, vals, x0, y0, wx, wy):
    sub = subs()
    base = x0 * width + y0
    places = [pl.ds(base + (p * width + 8 * half), 8) for p in range(11) for half in range(2)]
    low_w = [jnp.where(sub >= t, wy[t], 0.0) for t in range(4)]
    high_w = [jnp.where(sub < t, wy[t], 0.0) for t in range(4)]
    pairs = []
    for value in vals:
        first, second = wy[0] * value, None
        for t in range(1, 4):
            turned = pltpu.roll(value, t, 0)
            first = first + low_w[t] * turned
            second = high_w[t] * turned if second is None else second + high_w[t] * turned
        pairs.append((first, second))
    sums = []
    for p in range(11):
        for half in range(2):
            total = ref[places[len(sums)], :]
            for t in range(4):
                if 0 <= p - t < 8:
                    total = total + wx[t] * pairs[p - t][half]
            sums.append(total)
    for place, total in zip(places, sums):
        ref[place, :] = total


def block_of(b):
    return (b + 1) // 2, (b + 1) % 2


def steps_kernel(
    own, xlow, xhigh, ylow, yhigh, corner_low, corner_high, c_low_in, c_high_in, d_low_in, d_high_in,
    up, down, numbers, c_low, c_high, d_low, d_high, r_low, r_high, meta, sem,
):
    (xl, xh), (yl, yh) = inside("gx"), inside("gy")
    lane = lanes()
    upper = lane >= 64
    tiles = (
        (0, xl * corner_low[pl.ds(C_META, 8)]),
        (8, xl * xlow[pl.ds(NUMBERS, 8)]),
        (16, xl * corner_low[pl.ds(C_META + 8, 8)]),
        (24, yl * ylow[pl.ds(Y_META, 8)]),
        (32, own[pl.ds(NUMBERS, 8)]),
        (40, yh * yhigh[pl.ds(Y_META, 8)]),
        (48, xh * corner_high[pl.ds(C_META, 8)]),
        (56, xh * xhigh[pl.ds(NUMBERS, 8)]),
        (64, xh * corner_high[pl.ds(C_META + 8, 8)]),
    )
    for at, value in tiles:
        numbers[pl.ds(at, 8)] = value
    copy = pltpu.make_async_copy(numbers, meta, sem)
    copy.start()
    upper16 = lanes(T) >= 64

    def corners(x):
        at = pl.multiple_of(x * T, 8)
        for ref, keep, dx in ((corner_low, xl, 0), (corner_high, xh, 32)):
            for start, dy in ((C_LOW, 0), (C_HIGH, 32)):
                a, e = keep * ref[pl.ds(start + at, T)], keep * ref[pl.ds(start + 256 + at, T)]
                put(c_low, c_high, pl.ds(pl.multiple_of((dx + x) * 48 + dy, 8), T), upper16, a, e)

    loop(T, corners, UN_CORNER)

    def corners_second(x):
        at = pl.multiple_of(x * T, 8)
        for ref, keep, dx in ((corner_low, xl, 0), (corner_high, xh, 24)):
            for half, dy in ((0, 0), (8, 24)):
                a, e = keep * ref[pl.ds(C_A1 + half + at, 8)], keep * ref[pl.ds(C_E1 + half + at, 8)]
                put(d_low, d_high, pl.ds(pl.multiple_of((dx + x) * 32 + dy, 8), 8), upper, a, e)

    loop(8, corners_second, UN_CORNER)

    def clear(i):
        rows = pl.ds(pl.multiple_of(i * 128, 8), 128)
        r_low[rows] = jnp.zeros((128, L), F32)
        r_high[rows] = jnp.zeros((128, L), F32)

    loop(10, clear)
    copy.wait()

    def apply(low, high, width, row, step, ix, iy, bx, by):
        places = []
        values = []
        for n in (1, 0, 2):
            (a, b, c), (wx, wy, wz) = block_numbers(meta, row + n, step, ix, iy)
            x0, y0 = bx * 8 + 7 + a, by * 8 + 7 + b
            turns = [(1 - c - t) & 127 for t in range(4)]
            places.append((x0, y0, c, wx, wy, wz))
            if n == 1:
                masks = [jnp.logical_xor(((lane - (c + t - 1)) & -128) == 0, upper) for t in range(4)]
                lows = gather_xy(low, width, x0, y0, wx, wy)
                highs = gather_xy(high, width, x0, y0, wx, wy)
                values.append(
                    [
                        sum(wz[t] * pltpu.roll(jnp.where(masks[t], lows[p], highs[p]), turns[t], 1) for t in range(4))
                        for p in range(8)
                    ]
                )
            else:
                ins = gather_xy(low if n == 0 else high, width, x0, y0, wx, wy)
                values.append([sum(wz[t] * pltpu.roll(value, turns[t], 1) for t in range(4)) for value in ins])
        return places, values

    def first_step(i):
        bx, by = i // 4, i % 4
        (slot_x, ix), (slot_y, iy) = block_of(bx), block_of(by)
        _, (own_z, below, above) = apply(c_low, c_high, 48, slot_x * 24 + slot_y * 8, 0, ix, iy, bx, by)
        for p in range(8):
            rows = pl.ds(pl.multiple_of(bx * 256 + by * 8, 8) + p * 32, 8)
            d_low[rows, :] = d_low[rows, :] + jnp.where(upper, below[p], own_z[p])
            d_high[rows, :] = d_high[rows, :] + jnp.where(upper, own_z[p], above[p])

    loop(16, first_step, UN_FIRST)

    def second_step(i):
        ix, iy = i // 2, i % 2
        places, (own_z, below, above) = apply(d_low, d_high, 32, 32, 1, ix, iy, ix, iy)
        below = [jnp.where(lane >= 96, value, 0.0) for value in below]
        above = [jnp.where(lane < 32, value, 0.0) for value in above]
        x0, y0, c, wx, wy, wz = places[0]
        back = [(c + t - 1) & 127 for t in range(4)]
        masks = [jnp.logical_xor(((lane - (c + t - 1)) & -128) == 0, upper) for t in range(4)]
        low_w = [jnp.where(masks[t], wz[t], 0.0) for t in range(4)]
        high_w = [jnp.where(masks[t], 0.0, wz[t]) for t in range(4)]
        to_low, to_high = [], []
        for value in own_z:
            turned = [pltpu.roll(value, back[t], 1) for t in range(4)]
            to_low.append(sum(low_w[t] * turned[t] for t in range(4)))
            to_high.append(sum(high_w[t] * turned[t] for t in range(4)))
        scatter_xy(r_low, 40, to_low, x0, y0, wx, wy)
        scatter_xy(r_high, 40, to_high, x0, y0, wx, wy)
        for (x0, y0, c, wx, wy, wz), values, ref in ((places[1], below, r_low), (places[2], above, r_high)):
            back = [(c + t - 1) & 127 for t in range(4)]
            moved = [sum(wz[t] * pltpu.roll(value, back[t], 1) for t in range(4)) for value in values]
            scatter_xy(ref, 40, moved, x0, y0, wx, wy)

    loop(4, second_step, UN_SECOND)

    wide = lanes(32)
    wide_upper = wide >= 64
    quarter = ((wide + 16) & 127) // 32

    def pack(i):
        packed = None
        for g in range(4):
            at = 16 * (i // 4) + 4 * g + i % 4
            rows = pl.ds(pl.multiple_of(at * 40, 8), 32)
            low, high = r_low[rows], r_high[rows]
            a = jnp.where(wide_upper, high, low)
            e = roll(jnp.where(wide_upper, low, high), 32 * g)
            packed = e if g == 0 else jnp.where(quarter == g, e, packed)
            down[pl.ds(pl.multiple_of(at * T, 8), T)] = a[0:16]
            up[pl.ds(pl.multiple_of(at * T, 8), T)] = a[16:32]
        down[pl.ds(pl.multiple_of(R_E + i * T, 8), T)] = packed[0:16]
        up[pl.ds(pl.multiple_of(R_E + i * T, 8), T)] = packed[16:32]

    loop(8, pack, UN_PACK)


def sum_y_kernel(own_up, own_down, low, high, up, down):
    low_in, high_in = inside("gy")
    for h, out in ((0, down), (1, up)):
        for start, planes in ((0, 16), (R_E, 4)):
            for x in range(planes):
                rows = pl.ds(start + (h * planes + x) * T, T)
                out[pl.ds(start + x * 32, T)] = own_down[rows] + low_in * low[rows]
                out[pl.ds(start + x * 32 + T, T)] = own_up[rows] + high_in * high[rows]


def last_step_kernel(own_up, own_down, low, high, numbers, g, reg, result, a1, e1, acc, out, meta, sem, out_sem):
    copy = pltpu.make_async_copy(numbers, meta, sem)
    copy.start()
    low_in, high_in = inside("gx")
    wide = lanes(32)
    valid = (wide < 16) | (wide >= 112)
    for h, (mine, other, keep) in enumerate(((own_down, low, low_in), (own_up, high, high_in))):

        def unpack(x, h=h, mine=mine, other=other, keep=keep):
            rows = pl.ds(pl.multiple_of(R_E + x * 32, 8), 32)
            packed = mine[rows] + keep * other[rows]
            for q in range(4):
                at = pl.multiple_of((4 * q + x) * 32, 8)
                e1[pl.ds(512 * h + at, 32)] = jnp.where(valid, roll(packed, -32 * q), 0.0)
                a1[pl.ds(512 * h + at, 32)] = mine[pl.ds(at, 32)] + keep * other[pl.ds(at, 32)]

        loop(4, unpack, UN_UNPACK)

    def clear(i):
        acc[pl.ds(pl.multiple_of(i * 168, 8), 168)] = jnp.zeros((168, L), F32)

    loop(16, clear)
    copy.wait()
    lane = lanes()
    upper = lane >= 64

    def step(i):
        bx, by = i // 4, i % 4
        (slot_x, ix), (slot_y, iy) = block_of(bx), block_of(by)
        row = slot_x * 24 + slot_y * 8
        rows = [pl.ds(pl.multiple_of(bx * 256 + by * 8, 8) + p * 32, 8) for p in range(8)]
        inner = [a1[r, :] for r in rows]
        outer = [e1[r, :] for r in rows]
        for n in range(3):
            (a, b, c), (wx, wy, wz) = block_numbers(meta, row + n, 0, ix, iy)
            back = [(c + t - 1) & 127 for t in range(4)]
            if n == 1:
                w = [jnp.where(((lane - (c + t - 1)) & -128) == 0, wz[t], 0.0) for t in range(4)]
                values = inner
            else:
                lands = upper if n == 2 else jnp.logical_not(upper)
                w = [jnp.where(lands, wz[t], 0.0) for t in range(4)]
                values = [jnp.where(upper if n == 0 else jnp.logical_not(upper), value, 0.0) for value in outer]
            moved = [sum(w[t] * pltpu.roll(value, back[t], 1) for t in range(4)) for value in values]
            scatter_xy(acc, 56, moved, bx * 8 + 7 + a, by * 8 + 7 + b, wx, wy)


    def finish(x):
        first, second = acc[pl.ds(pl.multiple_of((16 + x) * 56 + 16, 8), 16)], a1[pl.ds(pl.multiple_of((8 + x) * 32 + 8, 8), 16)]
        for c in range(3):
            out[c, x] = reg[c, x] + STEP_SIZE * (g[1, c, x].astype(F32) * second + g[0, c, x].astype(F32) * first)

    copies = []
    for h, (first_block, blocks) in enumerate(((0, 12), (12, 4))):
        loop(blocks, lambda i, first_block=first_block: step(first_block + i), blocks)
        loop(8, lambda x, h=h: finish(8 * h + x), 8)
        half = pl.ds(8 * h, 8)
        done = pltpu.make_async_copy(out.at[:, half], result.at[:, half], out_sem.at[h])
        done.start()
        copies.append(done)
    for done in copies:
        done.wait()


def laplace_kernel(v, zlow, zhigh, ylow, yhigh, xlow, xhigh, out, w):
    lane = lanes(T)
    half = (lane & 4) == 0
    (x_low, x_high), (y_low, y_high), (z_low, z_high) = inside("gx"), inside("gy"), inside("gz")
    sides = [-REG_WEIGHT * t for t in LAPLACE_TAPS]
    for c in range(3):
        rows = pl.ds(Z_V + c * T, T)
        faces = jnp.where(half, z_high * zhigh[rows], z_low * zlow[rows])
        for i in range(4):
            rows = pl.ds(FACE + (c * 4 + i) * T, T)
            w[i, 8:24] = x_low * xlow[rows]
            w[20 + i, 8:24] = x_high * xhigh[rows]
        for x in range(8):
            rows = pl.ds(Y_FACE + (c * 8 + x) * 8, 8)
            a, b = y_low * ylow[rows], y_high * yhigh[rows]
            w[4 + x, 0:8] = a
            w[12 + x, 0:8] = pltpu.roll(a, 4, 0)
            w[4 + x, 24:32] = b
            w[12 + x, 24:32] = pltpu.roll(b, 4, 0)
        for x in range(T):
            w[4 + x, 8:24] = v[c, x]
        for x in range(T):
            here = v[c, x]
            edge = roll(faces, -8 * x)
            total = 3.0 * sides[0] * here
            for k in range(1, 5):
                near = roll(jnp.where(lane < k, edge, here), -k) + roll(jnp.where(lane >= L - k, edge, here), k)
                near = near + w[4 + x - k, 8:24] + w[4 + x + k, 8:24]
                near = near + w[4 + x, 8 - k : 24 - k] + w[4 + x, 8 + k : 24 + k]
                total = total + sides[k] * near
            out[c, x] = total


VMEM = pl.BlockSpec(memory_space=pltpu.VMEM)
HBM = pl.BlockSpec(memory_space=pltpu.HBM)


def call(kernel, args, outs, scratch=(), hbm=(), cost=20000, alias=None, out_space=None):
    specs = [HBM if i in hbm else VMEM for i in range(len(args))]
    shapes = [jax.ShapeDtypeStruct(s, F32) for s in outs]
    return pl.pallas_call(
        kernel,
        out_shape=shapes,
        in_specs=specs,
        out_specs=[out_space or VMEM] * len(shapes),
        input_output_aliases=alias or {},
        scratch_shapes=list(scratch),
        compiler_params=pltpu.CompilerParams(vmem_limit_bytes=24 * 1024 * 1024),
        cost_estimate=pl.CostEstimate(flops=cost, bytes_accessed=cost, transcendentals=0),
    )(*args)


def exchange(up, down, axis):
    n = lax.axis_size(axis)
    rise = [(i, (i + 1) % n) for i in range(n)]
    fall = [(j, i) for i, j in rise]
    return lax.ppermute(up, axis, rise), lax.ppermute(down, axis, fall)


def last_call(args, vm, meta):
    shape = args[-1].shape
    scratch = [vm(32 * 32, L), vm(32 * 32, L), vm(48 * 56, L), vm(*shape)] + meta + [pltpu.SemaphoreType.DMA((2,))]
    return call(last_step_kernel, args, [shape], scratch=scratch, out_space=HBM)


def body(velocity, gradients, shift_x, shift_y, shift_z, fractions):
    v, g = velocity, gradients
    tile = (T, T, L)
    vm = lambda *s: pltpu.VMEM(s, F32)
    shifts = [s.transpose(0, 1, 3, 2) for s in (shift_x, shift_y, shift_z)]
    inputs = [v, g, *shifts, fractions.transpose(0, 2, 3, 4, 1)]
    v, s0, s1, zup, zdown, yup, ydown = call(
        sources_kernel,
        [pltpu.with_memory_space_constraint(a, pltpu.HBM) for a in inputs],
        [v.shape, tile, tile, (Z_ROWS, L), (Z_ROWS, L), (Y_ROWS, L), (Y_ROWS, L)],
        scratch=[pltpu.VMEM(g.shape, g.dtype)]
        + [pltpu.SMEM((2, 2, 1, 2), jnp.int32)] * 3
        + [pltpu.SMEM((2, 2, 2, 1, 3), jnp.int32), pltpu.SemaphoreType.DMA((8,)), pltpu.SemaphoreType.DMA((4,))],
        hbm=range(6),
    )
    zlow, zhigh = exchange(zup, zdown, "gz")
    ylow, yhigh = exchange(yup, ydown, "gy")
    yup, ydown, xup, xdown = call(
        tile_messages_kernel, (s0, s1, v, zup, zlow, zhigh, ylow, yhigh), [(Y_EROWS, L)] * 2 + [(ROWS, L)] * 2
    )
    xlow, xhigh = exchange(xup, xdown, "gx")
    elow, ehigh = exchange(yup, ydown, "gy")
    up, down = call(corner_message_kernel, (ylow, yhigh, elow, ehigh, xlow, xhigh), [(C_ROWS, L)] * 2)
    corner_low, corner_high = exchange(up, down, "gx")
    fields = [(48 * 48, L)] * 2 + [(32 * 32, L)] * 2
    filled = call(assemble_kernel, (xup, xdown, xlow, xhigh, ylow, yhigh, elow, ehigh), fields)
    meta = [pltpu.SMEM((72, L), F32), pltpu.SemaphoreType.DMA]
    up, down, numbers, *_ = call(
        steps_kernel,
        (xup, xlow, xhigh, elow, ehigh, corner_low, corner_high, *filled),
        [(R_ROWS, L), (R_ROWS, L), (72, L)] + fields,
        scratch=[vm(32 * 40, L), vm(32 * 40, L)] + meta,
        alias={7: 3, 8: 4, 9: 5, 10: 6},
    )
    (reg,) = call(
        laplace_kernel, (v, zlow, zhigh, ylow, yhigh, xlow, xhigh), [v.shape], scratch=[vm(24, 32, L)], cost=4000000
    )
    low, high = exchange(up, down, "gy")
    up, down = call(sum_y_kernel, (up, down, low, high), [(R_ROWS, L)] * 2)
    low, high = exchange(up, down, "gx")
    (out,) = last_call((up, down, low, high, numbers, g, reg), vm, meta)
    return out


def solution(mesh):
    in_specs = (
        P(None, "gx", "gy", "gz"),
        P(None, None, "gx", "gy", "gz"),
        P(None, "gx", "gy", "gz"),
        P(None, "gx", "gy", "gz"),
        P(None, "gx", "gy", "gz"),
        P(None, None, "gx", "gy", "gz"),
    )
    out_specs = P(None, "gx", "gy", "gz")
    return jax.shard_map(body, mesh=mesh, in_specs=in_specs, out_specs=out_specs, check_vma=False)
```

```python
import jax
import jax.numpy as jnp
from jax import lax
from jax.experimental import pallas as pl
from jax.experimental.pallas import tpu as pltpu
from jax.sharding import PartitionSpec as P

F32 = jnp.float32
LAPLACE_TAPS = (-205.0 / 72.0, 8.0 / 5.0, -1.0 / 5.0, 8.0 / 315.0, -1.0 / 560.0)
STEP_SIZE = 0.5
REG_WEIGHT = 0.1
T = 16
L = 128
UN_ASM, UN_CORNER, UN_FIRST, UN_SECOND, UN_PACK, UN_UNPACK = 8, 16, 16, 4, 8, 4
META = 15

Z_S0, Z_S1, Z_V, Z_META, Z_ROWS = 0, 128, 256, 304, 312
Y_S0, Y_S1, Y_FACE, Y_ROWS = 0, 256, 384, 576
Y_E0, Y_E1, Y_META, Y_EROWS = 0, 256, 384, 392
A0, E0, A1, E1, FACE, NUMBERS, ROWS = 0, 256, 512, 640, 768, 960, 968
C_LOW, C_HIGH, C_A1, C_E1, C_META, C_ROWS = 0, 512, 1024, 1152, 1280, 1296
R_E, R_ROWS = 512, 640


def lanes(rows=8):
    return lax.broadcasted_iota(jnp.int32, (rows, L), 1)


def subs():
    return lax.broadcasted_iota(jnp.int32, (8, L), 0)


def roll(x, amount):
    amount = amount % L
    return x if amount == 0 else pltpu.roll(x, amount, 1)


def block_numbers(meta, row, step, ix, iy):
    at = ((step * 2 + ix) * 2 + iy) * META
    shift = [meta[row, at + d].astype(jnp.int32) for d in range(3)]
    weights = [[meta[row, at + 3 + 4 * d + t] for t in range(4)] for d in range(3)]
    return shift, weights


def loop(count, body, unroll=1):
    def step(i, _):
        body(i)
        return 0

    lax.fori_loop(0, count, step, 0, unroll=unroll)


def inside(axis):
    i, n = lax.axis_index(axis), lax.axis_size(axis)
    return jnp.where(i > 0, 1.0, 0.0).astype(F32), jnp.where(i < n - 1, 1.0, 0.0).astype(F32)


def is_even(axis):
    return lax.axis_index(axis) % 2 == 0


def sources_kernel(
    v_hbm, g_hbm, sx_hbm, sy_hbm, sz_hbm, fr_hbm, v, s0, s1, swap0, swap1, yup, ydown, g, sx, sy, sz, fr, sem, small_sem
):
    copies = []
    for q in range(4):
        part = pl.ds(4 * q, 4)
        copies.append(pltpu.make_async_copy(v_hbm.at[:, part], v.at[:, part], sem.at[2 * q]))
        copies.append(pltpu.make_async_copy(g_hbm.at[:, :, part], g.at[:, :, part], sem.at[2 * q + 1]))
    small = [
        pltpu.make_async_copy(a, b, small_sem.at[n])
        for n, (a, b) in enumerate(((sx_hbm, sx), (sy_hbm, sy), (sz_hbm, sz), (fr_hbm, fr)))
    ]
    for copy in copies + small:
        copy.start()
    lane = lanes(T)
    for x in range(T):
        if x % 4 == 0:
            copies[x // 2].wait()
            copies[x // 2 + 1].wait()
        vel = [v[c, x] for c in range(3)]
        for k, s in ((0, s0), (1, s1)):
            total = g[k, 0, x].astype(F32) * vel[0]
            for c in (1, 2):
                total = total + g[k, c, x].astype(F32) * vel[c]
            value = STEP_SIZE * total
            s[x] = value
            if k == 0:
                yup[pl.ds(Y_S0 + x * T, T)] = value
                ydown[pl.ds(Y_S0 + x * T, T)] = value
            else:
                yup[pl.ds(Y_S1 + x * 8, 8)] = value[8:16]
                ydown[pl.ds(Y_S1 + x * 8, 8)] = value[0:8]
    first_half = subs() < 4
    for c in range(3):
        for x in range(8):
            rows = pl.ds(Y_FACE + (c * 8 + x) * 8, 8)
            yup[rows] = jnp.where(first_half, pltpu.roll(v[c, x + 8, 8:16], 4, 0), v[c, x, 8:16])
            ydown[rows] = jnp.where(first_half, v[c, x, 0:8], pltpu.roll(v[c, x + 8, 0:8], 4, 0))
    even = is_even("gz")
    upper = lane >= 64
    for start, s in ((Z_S0, s0), (Z_S1, s1)):
        for x in range(8):
            rows = pl.ds(start + x * T, T)
            a, b = s[x], roll(s[x + 8], 64)
            u, d = jnp.where(upper, a, b), jnp.where(upper, b, a)
            swap0[rows] = jnp.where(even, u, d)
            swap1[rows] = jnp.where(even, d, u)
    piece = lane // 8
    for c in range(3):
        u, d = v[c, 0], v[c, 0]
        for x in range(1, T):
            r = roll(v[c, x], 8 * x)
            u = jnp.where(piece == (15 + x) % 16, r, u)
            d = jnp.where(piece == x, r, d)
        swap0[pl.ds(Z_V + c * T, T)] = jnp.where(even, u, d)
        swap1[pl.ds(Z_V + c * T, T)] = jnp.where(even, d, u)
    lane = lanes()
    for copy in small:
        copy.wait()
    shifts, eighths = jnp.zeros((8, L), jnp.int32), jnp.zeros((8, L), jnp.int32)
    for k in range(2):
        for ix in range(2):
            for iy in range(2):
                at = ((k * 2 + ix) * 2 + iy) * META
                for n, ref in enumerate((sx, sy, sz)):
                    shifts = jnp.where(lane == at + n, ref[k, ix, 0, iy], shifts)
                    first = at + 3 + 4 * n
                    eighths = jnp.where((lane >= first) & (lane < first + 4), fr[k, ix, iy, 0, n], eighths)
    e = eighths.astype(F32) / 8.0
    e2 = e * e
    e3 = e2 * e
    weights = [
        0.5 * (2.0 * e2 - e3 - e),
        0.5 * (3.0 * e3 - 5.0 * e2 + 2.0),
        0.5 * (4.0 * e2 - 3.0 * e3 + e),
        0.5 * (e3 - e2),
    ]
    place = lane % META
    tap = (place - 3) % 4
    row = jnp.where(tap == 0, weights[0], jnp.where(tap == 1, weights[1], jnp.where(tap == 2, weights[2], weights[3])))
    row = jnp.where(place < 3, shifts.astype(F32), row)
    swap0[pl.ds(Z_META, 8)] = row
    swap1[pl.ds(Z_META, 8)] = row


def tile_messages_kernel(s0, s1, v, own, swap0, swap1, ylow, yhigh, yup, ydown, xup, xdown):
    del ylow, yhigh
    low_in, high_in = inside("gz")
    even = is_even("gz")
    upper = lanes(T) >= 64
    for start, s in ((Z_S0, s0), (Z_S1, s1)):
        for j in range(8):
            a, b = swap0[pl.ds(start + j * T, T)], swap1[pl.ds(start + j * T, T)]
            a, b = low_in * jnp.where(even, b, a), high_in * jnp.where(even, a, b)
            edges = (jnp.where(upper, a, b), roll(jnp.where(upper, b, a), 64))
            for h, edge in enumerate(edges):
                x = j + 8 * h
                if start == Z_S0:
                    for out in (xup, xdown):
                        out[pl.ds(A0 + x * T, T)] = s[x]
                        out[pl.ds(E0 + x * T, T)] = edge
                    for out in (yup, ydown):
                        out[pl.ds(Y_E0 + x * T, T)] = edge
                else:
                    yup[pl.ds(Y_E1 + x * 8, 8)] = edge[8:16]
                    ydown[pl.ds(Y_E1 + x * 8, 8)] = edge[0:8]
                    out = (xdown, xup)[h]
                    out[pl.ds(A1 + j * T, T)] = s[x]
                    out[pl.ds(E1 + j * T, T)] = edge
    for c in range(3):
        for i in range(4):
            xup[pl.ds(FACE + (c * 4 + i) * T, T)] = v[c, 12 + i]
            xdown[pl.ds(FACE + (c * 4 + i) * T, T)] = v[c, i]
    sub = subs()
    a, b = swap0[pl.ds(Z_META, 8)], swap1[pl.ds(Z_META, 8)]
    a, b = low_in * jnp.where(even, b, a), high_in * jnp.where(even, a, b)
    row = jnp.where(sub == 0, a, jnp.where(sub == 1, own[pl.ds(Z_META, 8)], b))
    for out, at in ((yup, Y_META), (ydown, Y_META), (xup, NUMBERS), (xdown, NUMBERS)):
        out[pl.ds(at, 8)] = row


def corner_message_kernel(low, high, elow, ehigh, xlow, xhigh, up, down):
    del xlow, xhigh
    sides = ((low, elow, C_LOW), (high, ehigh, C_HIGH))
    for y, ((a, e, to), keep) in enumerate(zip(sides, inside("gy"))):
        for x in range(T):
            for at, value in ((0, a[pl.ds(Y_S0 + x * T, T)]), (256, e[pl.ds(Y_E0 + x * T, T)])):
                value = keep * value
                up[pl.ds(to + at + x * T, T)] = value
                down[pl.ds(to + at + x * T, T)] = value
        for ref, start, place in ((a, Y_S1, C_A1), (e, Y_E1, C_E1)):
            for x in range(8):
                down[pl.ds(place + x * T + 8 * y, 8)] = keep * ref[pl.ds(start + x * 8, 8)]
                up[pl.ds(place + x * T + 8 * y, 8)] = keep * ref[pl.ds(start + (8 + x) * 8, 8)]
        value = keep * e[pl.ds(Y_META, 8)]
        up[pl.ds(C_META + 8 * y, 8)] = value
        down[pl.ds(C_META + 8 * y, 8)] = value


def put(low, high, rows, upper, a, e):
    low[rows] = jnp.where(upper, e, a)
    high[rows] = jnp.where(upper, a, e)


def assemble_kernel(own_up, own_down, xlow, xhigh, ylow, yhigh, elow, ehigh, c_low, c_high, d_low, d_high):
    (xl, xh), (yl, yh) = inside("gx"), inside("gy")
    upper, upper8 = lanes(T) >= 64, lanes(8) >= 64

    def first(x):
        at = pl.multiple_of(x * T, 8)
        for ref, keep, dx in ((own_up, None, 16), (xlow, xl, 0), (xhigh, xh, 32)):
            a, e = ref[pl.ds(A0 + at, T)], ref[pl.ds(E0 + at, T)]
            if keep is not None:
                a, e = keep * a, keep * e
            put(c_low, c_high, pl.ds(pl.multiple_of((dx + x) * 48 + 16, 8), T), upper, a, e)
        for ref, eref, keep, dy in ((ylow, elow, yl, 0), (yhigh, ehigh, yh, 32)):
            a, e = keep * ref[pl.ds(Y_S0 + at, T)], keep * eref[pl.ds(Y_E0 + at, T)]
            put(c_low, c_high, pl.ds(pl.multiple_of((16 + x) * 48 + dy, 8), T), upper, a, e)

    loop(T, first, UN_ASM)

    def second(x):
        at = pl.multiple_of(x * T, 8)
        for ref, keep, dx in ((own_down, None, 8), (own_up, None, 16), (xlow, xl, 0), (xhigh, xh, 24)):
            a, e = ref[pl.ds(A1 + at, T)], ref[pl.ds(E1 + at, T)]
            if keep is not None:
                a, e = keep * a, keep * e
            put(d_low, d_high, pl.ds(pl.multiple_of((dx + x) * 32 + 8, 8), T), upper, a, e)
        for h in range(2):
            at = pl.multiple_of((8 * h + x) * 8, 8)
            for ref, eref, keep, dy in ((ylow, elow, yl, 0), (yhigh, ehigh, yh, 24)):
                a, e = keep * ref[pl.ds(Y_S1 + at, 8)], keep * eref[pl.ds(Y_E1 + at, 8)]
                put(d_low, d_high, pl.ds(pl.multiple_of((8 + 8 * h + x) * 32 + dy, 8), 8), upper8, a, e)

    loop(8, second, UN_ASM)


def gather_xy(ref, width, x0, y0, wx, wy):
    base = x0 * width + y0
    planes = []
    for i in range(11):
        plane = wy[0] * ref[pl.ds(base + i * width, 8), :]
        for t in range(1, 4):
            plane = plane + wy[t] * ref[pl.ds(base + (i * width + t), 8), :]
        planes.append(plane)
    out = []
    for i in range(8):
        value = wx[0] * planes[i]
        for t in range(1, 4):
            value = value + wx[t] * planes[i + t]
        out.append(value)
    return out


def scatter_xy(ref, width, vals, x0, y0, wx, wy):
    sub = subs()
    base = x0 * width + y0
    places = [pl.ds(base + (p * width + 8 * half), 8) for p in range(11) for half in range(2)]
    low_w = [jnp.where(sub >= t, wy[t], 0.0) for t in range(4)]
    high_w = [jnp.where(sub < t, wy[t], 0.0) for t in range(4)]
    pairs = []
    for value in vals:
        first, second = wy[0] * value, None
        for t in range(1, 4):
            turned = pltpu.roll(value, t, 0)
            first = first + low_w[t] * turned
            second = high_w[t] * turned if second is None else second + high_w[t] * turned
        pairs.append((first, second))
    sums = []
    for p in range(11):
        for half in range(2):
            total = ref[places[len(sums)], :]
            for t in range(4):
                if 0 <= p - t < 8:
                    total = total + wx[t] * pairs[p - t][half]
            sums.append(total)
    for place, total in zip(places, sums):
        ref[place, :] = total


def block_of(b):
    return (b + 1) // 2, (b + 1) % 2


def steps_kernel(
    own, xlow, xhigh, ylow, yhigh, corner_low, corner_high, c_low_in, c_high_in, d_low_in, d_high_in,
    up, down, numbers, c_low, c_high, d_low, d_high, r_low, r_high, meta, sem,
):
    (xl, xh), (yl, yh) = inside("gx"), inside("gy")
    lane = lanes()
    upper = lane >= 64
    tiles = (
        (0, xl * corner_low[pl.ds(C_META, 8)]),
        (8, xl * xlow[pl.ds(NUMBERS, 8)]),
        (16, xl * corner_low[pl.ds(C_META + 8, 8)]),
        (24, yl * ylow[pl.ds(Y_META, 8)]),
        (32, own[pl.ds(NUMBERS, 8)]),
        (40, yh * yhigh[pl.ds(Y_META, 8)]),
        (48, xh * corner_high[pl.ds(C_META, 8)]),
        (56, xh * xhigh[pl.ds(NUMBERS, 8)]),
        (64, xh * corner_high[pl.ds(C_META + 8, 8)]),
    )
    for at, value in tiles:
        numbers[pl.ds(at, 8)] = value
    copy = pltpu.make_async_copy(numbers, meta, sem)
    copy.start()
    upper16 = lanes(T) >= 64

    def corners(x):
        at = pl.multiple_of(x * T, 8)
        for ref, keep, dx in ((corner_low, xl, 0), (corner_high, xh, 32)):
            for start, dy in ((C_LOW, 0), (C_HIGH, 32)):
                a, e = keep * ref[pl.ds(start + at, T)], keep * ref[pl.ds(start + 256 + at, T)]
                put(c_low, c_high, pl.ds(pl.multiple_of((dx + x) * 48 + dy, 8), T), upper16, a, e)

    loop(T, corners, UN_CORNER)

    def corners_second(x):
        at = pl.multiple_of(x * T, 8)
        for ref, keep, dx in ((corner_low, xl, 0), (corner_high, xh, 24)):
            for half, dy in ((0, 0), (8, 24)):
                a, e = keep * ref[pl.ds(C_A1 + half + at, 8)], keep * ref[pl.ds(C_E1 + half + at, 8)]
                put(d_low, d_high, pl.ds(pl.multiple_of((dx + x) * 32 + dy, 8), 8), upper, a, e)

    loop(8, corners_second, UN_CORNER)

    def clear(i):
        rows = pl.ds(pl.multiple_of(i * 128, 8), 128)
        r_low[rows] = jnp.zeros((128, L), F32)
        r_high[rows] = jnp.zeros((128, L), F32)

    loop(10, clear)
    copy.wait()

    def apply(low, high, width, row, step, ix, iy, bx, by):
        places = []
        values = []
        for n in (1, 0, 2):
            (a, b, c), (wx, wy, wz) = block_numbers(meta, row + n, step, ix, iy)
            x0, y0 = bx * 8 + 7 + a, by * 8 + 7 + b
            turns = [(1 - c - t) & 127 for t in range(4)]
            places.append((x0, y0, c, wx, wy, wz))
            if n == 1:
                masks = [jnp.logical_xor(((lane - (c + t - 1)) & -128) == 0, upper) for t in range(4)]
                lows = gather_xy(low, width, x0, y0, wx, wy)
                highs = gather_xy(high, width, x0, y0, wx, wy)
                values.append(
                    [
                        sum(wz[t] * pltpu.roll(jnp.where(masks[t], lows[p], highs[p]), turns[t], 1) for t in range(4))
                        for p in range(8)
                    ]
                )
            else:
                ins = gather_xy(low if n == 0 else high, width, x0, y0, wx, wy)
                values.append([sum(wz[t] * pltpu.roll(value, turns[t], 1) for t in range(4)) for value in ins])
        return places, values

    def first_step(i):
        bx, by = i // 4, i % 4
        (slot_x, ix), (slot_y, iy) = block_of(bx), block_of(by)
        _, (own_z, below, above) = apply(c_low, c_high, 48, slot_x * 24 + slot_y * 8, 0, ix, iy, bx, by)
        for p in range(8):
            rows = pl.ds(pl.multiple_of(bx * 256 + by * 8, 8) + p * 32, 8)
            d_low[rows, :] = d_low[rows, :] + jnp.where(upper, below[p], own_z[p])
            d_high[rows, :] = d_high[rows, :] + jnp.where(upper, own_z[p], above[p])

    loop(16, first_step, UN_FIRST)

    def second_step(i):
        ix, iy = i // 2, i % 2
        places, (own_z, below, above) = apply(d_low, d_high, 32, 32, 1, ix, iy, ix, iy)
        below = [jnp.where(lane >= 96, value, 0.0) for value in below]
        above = [jnp.where(lane < 32, value, 0.0) for value in above]
        x0, y0, c, wx, wy, wz = places[0]
        back = [(c + t - 1) & 127 for t in range(4)]
        masks = [jnp.logical_xor(((lane - (c + t - 1)) & -128) == 0, upper) for t in range(4)]
        low_w = [jnp.where(masks[t], wz[t], 0.0) for t in range(4)]
        high_w = [jnp.where(masks[t], 0.0, wz[t]) for t in range(4)]
        to_low, to_high = [], []
        for value in own_z:
            turned = [pltpu.roll(value, back[t], 1) for t in range(4)]
            to_low.append(sum(low_w[t] * turned[t] for t in range(4)))
            to_high.append(sum(high_w[t] * turned[t] for t in range(4)))
        scatter_xy(r_low, 40, to_low, x0, y0, wx, wy)
        scatter_xy(r_high, 40, to_high, x0, y0, wx, wy)
        for (x0, y0, c, wx, wy, wz), values, ref in ((places[1], below, r_low), (places[2], above, r_high)):
            back = [(c + t - 1) & 127 for t in range(4)]
            moved = [sum(wz[t] * pltpu.roll(value, back[t], 1) for t in range(4)) for value in values]
            scatter_xy(ref, 40, moved, x0, y0, wx, wy)

    loop(4, second_step, UN_SECOND)

    wide = lanes(32)
    wide_upper = wide >= 64
    quarter = ((wide + 16) & 127) // 32

    def pack(i):
        packed = None
        for g in range(4):
            at = 16 * (i // 4) + 4 * g + i % 4
            rows = pl.ds(pl.multiple_of(at * 40, 8), 32)
            low, high = r_low[rows], r_high[rows]
            a = jnp.where(wide_upper, high, low)
            e = roll(jnp.where(wide_upper, low, high), 32 * g)
            packed = e if g == 0 else jnp.where(quarter == g, e, packed)
            down[pl.ds(pl.multiple_of(at * T, 8), T)] = a[0:16]
            up[pl.ds(pl.multiple_of(at * T, 8), T)] = a[16:32]
        down[pl.ds(pl.multiple_of(R_E + i * T, 8), T)] = packed[0:16]
        up[pl.ds(pl.multiple_of(R_E + i * T, 8), T)] = packed[16:32]

    loop(8, pack, UN_PACK)


def sum_y_kernel(own_up, own_down, low, high, up, down):
    low_in, high_in = inside("gy")
    for h, out in ((0, down), (1, up)):
        for start, planes in ((0, 16), (R_E, 4)):
            for x in range(planes):
                rows = pl.ds(start + (h * planes + x) * T, T)
                out[pl.ds(start + x * 32, T)] = own_down[rows] + low_in * low[rows]
                out[pl.ds(start + x * 32 + T, T)] = own_up[rows] + high_in * high[rows]


def last_step_kernel(own_up, own_down, low, high, numbers, g, reg, result, a1, e1, acc, out, meta, sem, out_sem):
    copy = pltpu.make_async_copy(numbers, meta, sem)
    copy.start()
    low_in, high_in = inside("gx")
    wide = lanes(32)
    valid = (wide < 16) | (wide >= 112)
    for h, (mine, other, keep) in enumerate(((own_down, low, low_in), (own_up, high, high_in))):

        def unpack(x, h=h, mine=mine, other=other, keep=keep):
            rows = pl.ds(pl.multiple_of(R_E + x * 32, 8), 32)
            packed = mine[rows] + keep * other[rows]
            for q in range(4):
                at = pl.multiple_of((4 * q + x) * 32, 8)
                e1[pl.ds(512 * h + at, 32)] = jnp.where(valid, roll(packed, -32 * q), 0.0)
                a1[pl.ds(512 * h + at, 32)] = mine[pl.ds(at, 32)] + keep * other[pl.ds(at, 32)]

        loop(4, unpack, UN_UNPACK)

    def clear(i):
        acc[pl.ds(pl.multiple_of(i * 168, 8), 168)] = jnp.zeros((168, L), F32)

    loop(16, clear)
    copy.wait()
    lane = lanes()
    upper = lane >= 64

    def step(i):
        bx, by = i // 4, i % 4
        (slot_x, ix), (slot_y, iy) = block_of(bx), block_of(by)
        row = slot_x * 24 + slot_y * 8
        rows = [pl.ds(pl.multiple_of(bx * 256 + by * 8, 8) + p * 32, 8) for p in range(8)]
        inner = [a1[r, :] for r in rows]
        outer = [e1[r, :] for r in rows]
        for n in range(3):
            (a, b, c), (wx, wy, wz) = block_numbers(meta, row + n, 0, ix, iy)
            back = [(c + t - 1) & 127 for t in range(4)]
            if n == 1:
                w = [jnp.where(((lane - (c + t - 1)) & -128) == 0, wz[t], 0.0) for t in range(4)]
                values = inner
            else:
                lands = upper if n == 2 else jnp.logical_not(upper)
                w = [jnp.where(lands, wz[t], 0.0) for t in range(4)]
                values = [jnp.where(upper if n == 0 else jnp.logical_not(upper), value, 0.0) for value in outer]
            moved = [sum(w[t] * pltpu.roll(value, back[t], 1) for t in range(4)) for value in values]
            scatter_xy(acc, 56, moved, bx * 8 + 7 + a, by * 8 + 7 + b, wx, wy)


    def finish(x):
        first, second = acc[pl.ds(pl.multiple_of((16 + x) * 56 + 16, 8), 16)], a1[pl.ds(pl.multiple_of((8 + x) * 32 + 8, 8), 16)]
        for c in range(3):
            out[c, x] = reg[c, x] + STEP_SIZE * (g[1, c, x].astype(F32) * second + g[0, c, x].astype(F32) * first)

    copies = []
    for h, (first_block, blocks) in enumerate(((0, 12), (12, 4))):
        loop(blocks, lambda i, first_block=first_block: step(first_block + i), blocks)
        loop(8, lambda x, h=h: finish(8 * h + x), 8)
        half = pl.ds(8 * h, 8)
        done = pltpu.make_async_copy(out.at[:, half], result.at[:, half], out_sem.at[h])
        done.start()
        copies.append(done)
    for done in copies:
        done.wait()


def laplace_kernel(v, swap0, swap1, ylow, yhigh, xlow, xhigh, out, w):
    lane = lanes(T)
    half = (lane & 4) == 0
    even = is_even("gz")
    (x_low, x_high), (y_low, y_high), (z_low, z_high) = inside("gx"), inside("gy"), inside("gz")
    sides = [-REG_WEIGHT * t for t in LAPLACE_TAPS]
    for c in range(3):
        rows = pl.ds(Z_V + c * T, T)
        a, b = swap0[rows], swap1[rows]
        faces = jnp.where(half, z_high * jnp.where(even, a, b), z_low * jnp.where(even, b, a))
        for i in range(4):
            rows = pl.ds(FACE + (c * 4 + i) * T, T)
            w[i, 8:24] = x_low * xlow[rows]
            w[20 + i, 8:24] = x_high * xhigh[rows]
        for x in range(8):
            rows = pl.ds(Y_FACE + (c * 8 + x) * 8, 8)
            a, b = y_low * ylow[rows], y_high * yhigh[rows]
            w[4 + x, 0:8] = a
            w[12 + x, 0:8] = pltpu.roll(a, 4, 0)
            w[4 + x, 24:32] = b
            w[12 + x, 24:32] = pltpu.roll(b, 4, 0)
        for x in range(T):
            w[4 + x, 8:24] = v[c, x]
        for x in range(T):
            here = v[c, x]
            edge = roll(faces, -8 * x)
            total = 3.0 * sides[0] * here
            for k in range(1, 5):
                near = roll(jnp.where(lane < k, edge, here), -k) + roll(jnp.where(lane >= L - k, edge, here), k)
                near = near + w[4 + x - k, 8:24] + w[4 + x + k, 8:24]
                near = near + w[4 + x, 8 - k : 24 - k] + w[4 + x, 8 + k : 24 + k]
                total = total + sides[k] * near
            out[c, x] = total


VMEM = pl.BlockSpec(memory_space=pltpu.VMEM)
HBM = pl.BlockSpec(memory_space=pltpu.HBM)


def call(kernel, args, outs, scratch=(), hbm=(), cost=20000, alias=None, out_space=None):
    specs = [HBM if i in hbm else VMEM for i in range(len(args))]
    shapes = [jax.ShapeDtypeStruct(s, F32) for s in outs]
    return pl.pallas_call(
        kernel,
        out_shape=shapes,
        in_specs=specs,
        out_specs=[out_space or VMEM] * len(shapes),
        input_output_aliases=alias or {},
        scratch_shapes=list(scratch),
        compiler_params=pltpu.CompilerParams(vmem_limit_bytes=24 * 1024 * 1024),
        cost_estimate=pl.CostEstimate(flops=cost, bytes_accessed=cost, transcendentals=0),
    )(*args)


def exchange(up, down, axis):
    n = lax.axis_size(axis)
    rise = [(i, (i + 1) % n) for i in range(n)]
    fall = [(j, i) for i, j in rise]
    return lax.ppermute(up, axis, rise), lax.ppermute(down, axis, fall)


def last_call(args, vm, meta):
    shape = args[-1].shape
    scratch = [vm(32 * 32, L), vm(32 * 32, L), vm(48 * 56, L), vm(*shape)] + meta + [pltpu.SemaphoreType.DMA((2,))]
    return call(last_step_kernel, args, [shape], scratch=scratch, out_space=HBM)


def swap(first, second, axis):
    n = lax.axis_size(axis)
    pairs = [(i, i + 1 if i % 2 == 0 else i - 1) for i in range(n)]
    others = [(i, i if i in (0, n - 1) else i - 1 if i % 2 == 0 else i + 1) for i in range(n)]
    return lax.ppermute(first, axis, pairs), lax.ppermute(second, axis, others)


def body(velocity, gradients, shift_x, shift_y, shift_z, fractions):
    v, g = velocity, gradients
    tile = (T, T, L)
    vm = lambda *s: pltpu.VMEM(s, F32)
    shifts = [s.transpose(0, 1, 3, 2) for s in (shift_x, shift_y, shift_z)]
    inputs = [v, g, *shifts, fractions.transpose(0, 2, 3, 4, 1)]
    v, s0, s1, first, second, yup, ydown = call(
        sources_kernel,
        [pltpu.with_memory_space_constraint(a, pltpu.HBM) for a in inputs],
        [v.shape, tile, tile, (Z_ROWS, L), (Z_ROWS, L), (Y_ROWS, L), (Y_ROWS, L)],
        scratch=[pltpu.VMEM(g.shape, g.dtype)]
        + [pltpu.SMEM((2, 2, 1, 2), jnp.int32)] * 3
        + [pltpu.SMEM((2, 2, 2, 1, 3), jnp.int32), pltpu.SemaphoreType.DMA((8,)), pltpu.SemaphoreType.DMA((4,))],
        hbm=range(6),
    )
    swap0, swap1 = swap(first, second, "gz")
    ylow, yhigh = exchange(yup, ydown, "gy")
    yup, ydown, xup, xdown = call(
        tile_messages_kernel, (s0, s1, v, first, swap0, swap1, ylow, yhigh), [(Y_EROWS, L)] * 2 + [(ROWS, L)] * 2
    )
    xlow, xhigh = exchange(xup, xdown, "gx")
    elow, ehigh = exchange(yup, ydown, "gy")
    up, down = call(corner_message_kernel, (ylow, yhigh, elow, ehigh, xlow, xhigh), [(C_ROWS, L)] * 2)
    corner_low, corner_high = exchange(up, down, "gx")
    fields = [(48 * 48, L)] * 2 + [(32 * 32, L)] * 2
    filled = call(assemble_kernel, (xup, xdown, xlow, xhigh, ylow, yhigh, elow, ehigh), fields)
    meta = [pltpu.SMEM((72, L), F32), pltpu.SemaphoreType.DMA]
    up, down, numbers, *_ = call(
        steps_kernel,
        (xup, xlow, xhigh, elow, ehigh, corner_low, corner_high, *filled),
        [(R_ROWS, L), (R_ROWS, L), (72, L)] + fields,
        scratch=[vm(32 * 40, L), vm(32 * 40, L)] + meta,
        alias={7: 3, 8: 4, 9: 5, 10: 6},
    )
    (reg,) = call(
        laplace_kernel, (v, swap0, swap1, ylow, yhigh, xlow, xhigh), [v.shape], scratch=[vm(24, 32, L)], cost=4000000
    )
    low, high = exchange(up, down, "gy")
    up, down = call(sum_y_kernel, (up, down, low, high), [(R_ROWS, L)] * 2)
    low, high = exchange(up, down, "gx")
    (out,) = last_call((up, down, low, high, numbers, g, reg), vm, meta)
    return out


def solution(mesh):
    in_specs = (
        P(None, "gx", "gy", "gz"),
        P(None, None, "gx", "gy", "gz"),
        P(None, "gx", "gy", "gz"),
        P(None, "gx", "gy", "gz"),
        P(None, "gx", "gy", "gz"),
        P(None, None, "gx", "gy", "gz"),
    )
    out_specs = P(None, "gx", "gy", "gz")
    return jax.shard_map(body, mesh=mesh, in_specs=in_specs, out_specs=out_specs, check_vma=False)
```

```python
import jax
import jax.numpy as jnp
from jax import lax
from jax.experimental import pallas as pl
from jax.experimental.pallas import tpu as pltpu
from jax.sharding import PartitionSpec as P

F32 = jnp.float32
LAPLACE_TAPS = (-205.0 / 72.0, 8.0 / 5.0, -1.0 / 5.0, 8.0 / 315.0, -1.0 / 560.0)
STEP_SIZE = 0.5
REG_WEIGHT = 0.1
T = 16
L = 128
UN_ASM, UN_CORNER, UN_FIRST, UN_SECOND, UN_PACK, UN_UNPACK = 8, 16, 16, 4, 8, 4
META = 15

Z_S0, Z_S1, Z_V, Z_META, Z_ROWS = 0, 128, 256, 304, 312
Y_S0, Y_S1, Y_FACE, Y_ROWS = 0, 256, 384, 576
Y_E0, Y_E1, Y_META, Y_EROWS = 0, 256, 384, 392
A0, E0, A1, E1, FACE, NUMBERS, ROWS = 0, 256, 512, 640, 768, 960, 968
C_LOW, C_HIGH, C_A1, C_E1, C_META, C_ROWS = 0, 512, 1024, 1152, 1280, 1296
R_E, R_ROWS = 512, 640


def lanes(rows=8):
    return lax.broadcasted_iota(jnp.int32, (rows, L), 1)


def subs():
    return lax.broadcasted_iota(jnp.int32, (8, L), 0)


def roll(x, amount):
    amount = amount % L
    return x if amount == 0 else pltpu.roll(x, amount, 1)


def block_numbers(meta, row, step, ix, iy):
    at = ((step * 2 + ix) * 2 + iy) * META
    shift = [meta[row, at + d].astype(jnp.int32) for d in range(3)]
    weights = [[meta[row, at + 3 + 4 * d + t] for t in range(4)] for d in range(3)]
    return shift, weights


def loop(count, body, unroll=1):
    def step(i, _):
        body(i)
        return 0

    lax.fori_loop(0, count, step, 0, unroll=unroll)


def inside(axis):
    i, n = lax.axis_index(axis), lax.axis_size(axis)
    return jnp.where(i > 0, 1.0, 0.0).astype(F32), jnp.where(i < n - 1, 1.0, 0.0).astype(F32)


def is_even(axis):
    return lax.axis_index(axis) % 2 == 0


class Side:
    def __init__(self, axis, refs, up):
        self.even, self.refs = is_even(axis), refs if up else refs[::-1]

    def __getitem__(self, rows):
        return jnp.where(self.even, self.refs[0][rows], self.refs[1][rows])


def sides(axis, refs):
    return Side(axis, refs, False), Side(axis, refs, True)


class Swap:
    def __init__(self, axis, refs):
        self.even, self.refs = is_even(axis), refs

    def write(self, rows, up, down):
        if up is down:
            self.refs[0][rows] = up
            self.refs[1][rows] = up
        else:
            self.refs[0][rows] = jnp.where(self.even, up, down)
            self.refs[1][rows] = jnp.where(self.even, down, up)


def sources_kernel(
    v_hbm, g_hbm, sx_hbm, sy_hbm, sz_hbm, fr_hbm, v, s0, s1, swap0, swap1, y0, y1, g, sx, sy, sz, fr, sem, small_sem
):
    copies = []
    for q in range(4):
        part = pl.ds(4 * q, 4)
        copies.append(pltpu.make_async_copy(v_hbm.at[:, part], v.at[:, part], sem.at[2 * q]))
        copies.append(pltpu.make_async_copy(g_hbm.at[:, :, part], g.at[:, :, part], sem.at[2 * q + 1]))
    small = [
        pltpu.make_async_copy(a, b, small_sem.at[n])
        for n, (a, b) in enumerate(((sx_hbm, sx), (sy_hbm, sy), (sz_hbm, sz), (fr_hbm, fr)))
    ]
    for copy in copies + small:
        copy.start()
    y_swap = Swap("gy", (y0, y1))
    lane = lanes(T)
    for x in range(T):
        if x % 4 == 0:
            copies[x // 2].wait()
            copies[x // 2 + 1].wait()
        vel = [v[c, x] for c in range(3)]
        for k, s in ((0, s0), (1, s1)):
            total = g[k, 0, x].astype(F32) * vel[0]
            for c in (1, 2):
                total = total + g[k, c, x].astype(F32) * vel[c]
            value = STEP_SIZE * total
            s[x] = value
            if k == 0:
                y_swap.write(pl.ds(Y_S0 + x * T, T), value, value)
            else:
                y_swap.write(pl.ds(Y_S1 + x * 8, 8), value[8:16], value[0:8])
    first_half = subs() < 4
    for c in range(3):
        for x in range(8):
            rows = pl.ds(Y_FACE + (c * 8 + x) * 8, 8)
            u = jnp.where(first_half, pltpu.roll(v[c, x + 8, 8:16], 4, 0), v[c, x, 8:16])
            d = jnp.where(first_half, v[c, x, 0:8], pltpu.roll(v[c, x + 8, 0:8], 4, 0))
            y_swap.write(rows, u, d)
    even = is_even("gz")
    upper = lane >= 64
    for start, s in ((Z_S0, s0), (Z_S1, s1)):
        for x in range(8):
            rows = pl.ds(start + x * T, T)
            a, b = s[x], roll(s[x + 8], 64)
            u, d = jnp.where(upper, a, b), jnp.where(upper, b, a)
            swap0[rows] = jnp.where(even, u, d)
            swap1[rows] = jnp.where(even, d, u)
    piece = lane // 8
    for c in range(3):
        u, d = v[c, 0], v[c, 0]
        for x in range(1, T):
            r = roll(v[c, x], 8 * x)
            u = jnp.where(piece == (15 + x) % 16, r, u)
            d = jnp.where(piece == x, r, d)
        swap0[pl.ds(Z_V + c * T, T)] = jnp.where(even, u, d)
        swap1[pl.ds(Z_V + c * T, T)] = jnp.where(even, d, u)
    lane = lanes()
    for copy in small:
        copy.wait()
    shifts, eighths = jnp.zeros((8, L), jnp.int32), jnp.zeros((8, L), jnp.int32)
    for k in range(2):
        for ix in range(2):
            for iy in range(2):
                at = ((k * 2 + ix) * 2 + iy) * META
                for n, ref in enumerate((sx, sy, sz)):
                    shifts = jnp.where(lane == at + n, ref[k, ix, 0, iy], shifts)
                    first = at + 3 + 4 * n
                    eighths = jnp.where((lane >= first) & (lane < first + 4), fr[k, ix, iy, 0, n], eighths)
    e = eighths.astype(F32) / 8.0
    e2 = e * e
    e3 = e2 * e
    weights = [
        0.5 * (2.0 * e2 - e3 - e),
        0.5 * (3.0 * e3 - 5.0 * e2 + 2.0),
        0.5 * (4.0 * e2 - 3.0 * e3 + e),
        0.5 * (e3 - e2),
    ]
    place = lane % META
    tap = (place - 3) % 4
    row = jnp.where(tap == 0, weights[0], jnp.where(tap == 1, weights[1], jnp.where(tap == 2, weights[2], weights[3])))
    row = jnp.where(place < 3, shifts.astype(F32), row)
    swap0[pl.ds(Z_META, 8)] = row
    swap1[pl.ds(Z_META, 8)] = row


def tile_messages_kernel(s0, s1, v, own, swap0, swap1, ylow, yhigh, y0, y1, x0, x1):
    del ylow, yhigh
    y_swap, x_swap = Swap("gy", (y0, y1)), Swap("gx", (x0, x1))
    low_in, high_in = inside("gz")
    even = is_even("gz")
    upper = lanes(T) >= 64
    for start, s in ((Z_S0, s0), (Z_S1, s1)):
        for j in range(8):
            a, b = swap0[pl.ds(start + j * T, T)], swap1[pl.ds(start + j * T, T)]
            a, b = low_in * jnp.where(even, b, a), high_in * jnp.where(even, a, b)
            edges = (jnp.where(upper, a, b), roll(jnp.where(upper, b, a), 64))
            for h, edge in enumerate(edges):
                x = j + 8 * h
                if start == Z_S0:
                    inner = s[x]
                    x_swap.write(pl.ds(A0 + x * T, T), inner, inner)
                    x_swap.write(pl.ds(E0 + x * T, T), edge, edge)
                    y_swap.write(pl.ds(Y_E0 + x * T, T), edge, edge)
                else:
                    y_swap.write(pl.ds(Y_E1 + x * 8, 8), edge[8:16], edge[0:8])
            if start == Z_S1:
                x_swap.write(pl.ds(A1 + j * T, T), s[j + 8], s[j])
                x_swap.write(pl.ds(E1 + j * T, T), edges[1], edges[0])
    for c in range(3):
        for i in range(4):
            x_swap.write(pl.ds(FACE + (c * 4 + i) * T, T), v[c, 12 + i], v[c, i])
    sub = subs()
    a, b = swap0[pl.ds(Z_META, 8)], swap1[pl.ds(Z_META, 8)]
    a, b = low_in * jnp.where(even, b, a), high_in * jnp.where(even, a, b)
    row = jnp.where(sub == 0, a, jnp.where(sub == 1, own[pl.ds(Z_META, 8)], b))
    y_swap.write(pl.ds(Y_META, 8), row, row)
    x_swap.write(pl.ds(NUMBERS, 8), row, row)


def corner_message_kernel(y0, y1, e0, e1, from_x0, from_x1, x0, x1):
    del from_x0, from_x1
    x_swap = Swap("gx", (x0, x1))
    places = zip(sides("gy", (y0, y1)), sides("gy", (e0, e1)), inside("gy"), (C_LOW, C_HIGH))
    for y, (a, e, keep, to) in enumerate(places):
        for x in range(T):
            for at, value in ((0, a[pl.ds(Y_S0 + x * T, T)]), (256, e[pl.ds(Y_E0 + x * T, T)])):
                value = keep * value
                x_swap.write(pl.ds(to + at + x * T, T), value, value)
        for ref, start, place in ((a, Y_S1, C_A1), (e, Y_E1, C_E1)):
            for x in range(8):
                u, d = keep * ref[pl.ds(start + (8 + x) * 8, 8)], keep * ref[pl.ds(start + x * 8, 8)]
                x_swap.write(pl.ds(place + x * T + 8 * y, 8), u, d)
        value = keep * e[pl.ds(Y_META, 8)]
        x_swap.write(pl.ds(C_META + 8 * y, 8), value, value)


def put(low, high, rows, upper, a, e):
    low[rows] = jnp.where(upper, e, a)
    high[rows] = jnp.where(upper, a, e)


def assemble_kernel(own0, own1, x0, x1, y0, y1, e0, e1, c_low, c_high, d_low, d_high):
    own_down, own_up = sides("gx", (own0, own1))
    (xlow, xhigh), (ylow, yhigh), (elow, ehigh) = sides("gx", (x0, x1)), sides("gy", (y0, y1)), sides("gy", (e0, e1))
    (xl, xh), (yl, yh) = inside("gx"), inside("gy")
    upper, upper8 = lanes(T) >= 64, lanes(8) >= 64

    def first(x):
        at = pl.multiple_of(x * T, 8)
        for ref, keep, dx in ((own0, None, 16), (xlow, xl, 0), (xhigh, xh, 32)):
            a, e = ref[pl.ds(A0 + at, T)], ref[pl.ds(E0 + at, T)]
            if keep is not None:
                a, e = keep * a, keep * e
            put(c_low, c_high, pl.ds(pl.multiple_of((dx + x) * 48 + 16, 8), T), upper, a, e)
        for ref, eref, keep, dy in ((ylow, elow, yl, 0), (yhigh, ehigh, yh, 32)):
            a, e = keep * ref[pl.ds(Y_S0 + at, T)], keep * eref[pl.ds(Y_E0 + at, T)]
            put(c_low, c_high, pl.ds(pl.multiple_of((16 + x) * 48 + dy, 8), T), upper, a, e)

    loop(T, first, UN_ASM)

    def second(x):
        at = pl.multiple_of(x * T, 8)
        for ref, keep, dx in ((own_down, None, 8), (own_up, None, 16), (xlow, xl, 0), (xhigh, xh, 24)):
            a, e = ref[pl.ds(A1 + at, T)], ref[pl.ds(E1 + at, T)]
            if keep is not None:
                a, e = keep * a, keep * e
            put(d_low, d_high, pl.ds(pl.multiple_of((dx + x) * 32 + 8, 8), T), upper, a, e)
        for h in range(2):
            at = pl.multiple_of((8 * h + x) * 8, 8)
            for ref, eref, keep, dy in ((ylow, elow, yl, 0), (yhigh, ehigh, yh, 24)):
                a, e = keep * ref[pl.ds(Y_S1 + at, 8)], keep * eref[pl.ds(Y_E1 + at, 8)]
                put(d_low, d_high, pl.ds(pl.multiple_of((8 + 8 * h + x) * 32 + dy, 8), 8), upper8, a, e)

    loop(8, second, UN_ASM)


def gather_xy(ref, width, x0, y0, wx, wy):
    base = x0 * width + y0
    planes = []
    for i in range(11):
        plane = wy[0] * ref[pl.ds(base + i * width, 8), :]
        for t in range(1, 4):
            plane = plane + wy[t] * ref[pl.ds(base + (i * width + t), 8), :]
        planes.append(plane)
    out = []
    for i in range(8):
        value = wx[0] * planes[i]
        for t in range(1, 4):
            value = value + wx[t] * planes[i + t]
        out.append(value)
    return out


def scatter_xy(ref, width, vals, x0, y0, wx, wy):
    sub = subs()
    base = x0 * width + y0
    places = [pl.ds(base + (p * width + 8 * half), 8) for p in range(11) for half in range(2)]
    low_w = [jnp.where(sub >= t, wy[t], 0.0) for t in range(4)]
    high_w = [jnp.where(sub < t, wy[t], 0.0) for t in range(4)]
    pairs = []
    for value in vals:
        first, second = wy[0] * value, None
        for t in range(1, 4):
            turned = pltpu.roll(value, t, 0)
            first = first + low_w[t] * turned
            second = high_w[t] * turned if second is None else second + high_w[t] * turned
        pairs.append((first, second))
    sums = []
    for p in range(11):
        for half in range(2):
            total = ref[places[len(sums)], :]
            for t in range(4):
                if 0 <= p - t < 8:
                    total = total + wx[t] * pairs[p - t][half]
            sums.append(total)
    for place, total in zip(places, sums):
        ref[place, :] = total


def block_of(b):
    return (b + 1) // 2, (b + 1) % 2


def steps_kernel(
    own, x0, x1, e0, e1, corner0, corner1, c_low_in, c_high_in, d_low_in, d_high_in,
    out0, out1, numbers, c_low, c_high, d_low, d_high, r_low, r_high, meta, sem,
):
    (xl, xh), (yl, yh) = inside("gx"), inside("gy")
    (xlow, xhigh), (ylow, yhigh) = sides("gx", (x0, x1)), sides("gy", (e0, e1))
    corner_low, corner_high = sides("gx", (corner0, corner1))
    y_swap = Swap("gy", (out0, out1))
    lane = lanes()
    upper = lane >= 64
    tiles = (
        (0, xl * corner_low[pl.ds(C_META, 8)]),
        (8, xl * xlow[pl.ds(NUMBERS, 8)]),
        (16, xl * corner_low[pl.ds(C_META + 8, 8)]),
        (24, yl * ylow[pl.ds(Y_META, 8)]),
        (32, own[pl.ds(NUMBERS, 8)]),
        (40, yh * yhigh[pl.ds(Y_META, 8)]),
        (48, xh * corner_high[pl.ds(C_META, 8)]),
        (56, xh * xhigh[pl.ds(NUMBERS, 8)]),
        (64, xh * corner_high[pl.ds(C_META + 8, 8)]),
    )
    for at, value in tiles:
        numbers[pl.ds(at, 8)] = value
    copy = pltpu.make_async_copy(numbers, meta, sem)
    copy.start()
    upper16 = lanes(T) >= 64

    def corners(x):
        at = pl.multiple_of(x * T, 8)
        for ref, keep, dx in ((corner_low, xl, 0), (corner_high, xh, 32)):
            for start, dy in ((C_LOW, 0), (C_HIGH, 32)):
                a, e = keep * ref[pl.ds(start + at, T)], keep * ref[pl.ds(start + 256 + at, T)]
                put(c_low, c_high, pl.ds(pl.multiple_of((dx + x) * 48 + dy, 8), T), upper16, a, e)

    loop(T, corners, UN_CORNER)

    def corners_second(x):
        at = pl.multiple_of(x * T, 8)
        for ref, keep, dx in ((corner_low, xl, 0), (corner_high, xh, 24)):
            for half, dy in ((0, 0), (8, 24)):
                a, e = keep * ref[pl.ds(C_A1 + half + at, 8)], keep * ref[pl.ds(C_E1 + half + at, 8)]
                put(d_low, d_high, pl.ds(pl.multiple_of((dx + x) * 32 + dy, 8), 8), upper, a, e)

    loop(8, corners_second, UN_CORNER)

    def clear(i):
        rows = pl.ds(pl.multiple_of(i * 128, 8), 128)
        r_low[rows] = jnp.zeros((128, L), F32)
        r_high[rows] = jnp.zeros((128, L), F32)

    loop(10, clear)
    copy.wait()

    def apply(low, high, width, row, step, ix, iy, bx, by):
        places = []
        values = []
        for n in (1, 0, 2):
            (a, b, c), (wx, wy, wz) = block_numbers(meta, row + n, step, ix, iy)
            x0, y0 = bx * 8 + 7 + a, by * 8 + 7 + b
            turns = [(1 - c - t) & 127 for t in range(4)]
            places.append((x0, y0, c, wx, wy, wz))
            if n == 1:
                masks = [jnp.logical_xor(((lane - (c + t - 1)) & -128) == 0, upper) for t in range(4)]
                lows = gather_xy(low, width, x0, y0, wx, wy)
                highs = gather_xy(high, width, x0, y0, wx, wy)
                values.append(
                    [
                        sum(wz[t] * pltpu.roll(jnp.where(masks[t], lows[p], highs[p]), turns[t], 1) for t in range(4))
                        for p in range(8)
                    ]
                )
            else:
                ins = gather_xy(low if n == 0 else high, width, x0, y0, wx, wy)
                values.append([sum(wz[t] * pltpu.roll(value, turns[t], 1) for t in range(4)) for value in ins])
        return places, values

    def first_step(i):
        bx, by = i // 4, i % 4
        (slot_x, ix), (slot_y, iy) = block_of(bx), block_of(by)
        _, (own_z, below, above) = apply(c_low, c_high, 48, slot_x * 24 + slot_y * 8, 0, ix, iy, bx, by)
        for p in range(8):
            rows = pl.ds(pl.multiple_of(bx * 256 + by * 8, 8) + p * 32, 8)
            d_low[rows, :] = d_low[rows, :] + jnp.where(upper, below[p], own_z[p])
            d_high[rows, :] = d_high[rows, :] + jnp.where(upper, own_z[p], above[p])

    loop(16, first_step, UN_FIRST)

    def second_step(i):
        ix, iy = i // 2, i % 2
        places, (own_z, below, above) = apply(d_low, d_high, 32, 32, 1, ix, iy, ix, iy)
        below = [jnp.where(lane >= 96, value, 0.0) for value in below]
        above = [jnp.where(lane < 32, value, 0.0) for value in above]
        x0, y0, c, wx, wy, wz = places[0]
        back = [(c + t - 1) & 127 for t in range(4)]
        masks = [jnp.logical_xor(((lane - (c + t - 1)) & -128) == 0, upper) for t in range(4)]
        low_w = [jnp.where(masks[t], wz[t], 0.0) for t in range(4)]
        high_w = [jnp.where(masks[t], 0.0, wz[t]) for t in range(4)]
        to_low, to_high = [], []
        for value in own_z:
            turned = [pltpu.roll(value, back[t], 1) for t in range(4)]
            to_low.append(sum(low_w[t] * turned[t] for t in range(4)))
            to_high.append(sum(high_w[t] * turned[t] for t in range(4)))
        scatter_xy(r_low, 40, to_low, x0, y0, wx, wy)
        scatter_xy(r_high, 40, to_high, x0, y0, wx, wy)
        for (x0, y0, c, wx, wy, wz), values, ref in ((places[1], below, r_low), (places[2], above, r_high)):
            back = [(c + t - 1) & 127 for t in range(4)]
            moved = [sum(wz[t] * pltpu.roll(value, back[t], 1) for t in range(4)) for value in values]
            scatter_xy(ref, 40, moved, x0, y0, wx, wy)

    loop(4, second_step, UN_SECOND)

    wide = lanes(32)
    wide_upper = wide >= 64
    quarter = ((wide + 16) & 127) // 32

    def pack(i):
        packed = None
        for g in range(4):
            at = 16 * (i // 4) + 4 * g + i % 4
            rows = pl.ds(pl.multiple_of(at * 40, 8), 32)
            low, high = r_low[rows], r_high[rows]
            a = jnp.where(wide_upper, high, low)
            e = roll(jnp.where(wide_upper, low, high), 32 * g)
            packed = e if g == 0 else jnp.where(quarter == g, e, packed)
            y_swap.write(pl.ds(pl.multiple_of(at * T, 8), T), a[16:32], a[0:16])
        y_swap.write(pl.ds(pl.multiple_of(R_E + i * T, 8), T), packed[16:32], packed[0:16])

    loop(8, pack, UN_PACK)


def sum_y_kernel(own0, own1, y0, y1, x0, x1):
    low_in, high_in = inside("gy")
    (own_down, own_up), (low, high) = sides("gy", (own0, own1)), sides("gy", (y0, y1))
    x_swap = Swap("gx", (x0, x1))
    for start, planes in ((0, 16), (R_E, 4)):
        for x in range(planes):
            rows = [pl.ds(start + (h * planes + x) * T, T) for h in range(2)]
            lows = [own_down[r] + low_in * low[r] for r in rows]
            highs = [own_up[r] + high_in * high[r] for r in rows]
            x_swap.write(pl.ds(start + x * 32, T), lows[1], lows[0])
            x_swap.write(pl.ds(start + x * 32 + T, T), highs[1], highs[0])


def last_step_kernel(own0, own1, x0, x1, numbers, g, reg, result, a1, e1, acc, out, meta, sem, out_sem):
    copy = pltpu.make_async_copy(numbers, meta, sem)
    copy.start()
    low_in, high_in = inside("gx")
    (own_down, own_up), (low, high) = sides("gx", (own0, own1)), sides("gx", (x0, x1))
    wide = lanes(32)
    valid = (wide < 16) | (wide >= 112)
    for h, (mine, other, keep) in enumerate(((own_down, low, low_in), (own_up, high, high_in))):

        def unpack(x, h=h, mine=mine, other=other, keep=keep):
            rows = pl.ds(pl.multiple_of(R_E + x * 32, 8), 32)
            packed = mine[rows] + keep * other[rows]
            for q in range(4):
                at = pl.multiple_of((4 * q + x) * 32, 8)
                e1[pl.ds(512 * h + at, 32)] = jnp.where(valid, roll(packed, -32 * q), 0.0)
                a1[pl.ds(512 * h + at, 32)] = mine[pl.ds(at, 32)] + keep * other[pl.ds(at, 32)]

        loop(4, unpack, UN_UNPACK)

    def clear(i):
        acc[pl.ds(pl.multiple_of(i * 168, 8), 168)] = jnp.zeros((168, L), F32)

    loop(16, clear)
    copy.wait()
    lane = lanes()
    upper = lane >= 64

    def step(i):
        bx, by = i // 4, i % 4
        (slot_x, ix), (slot_y, iy) = block_of(bx), block_of(by)
        row = slot_x * 24 + slot_y * 8
        rows = [pl.ds(pl.multiple_of(bx * 256 + by * 8, 8) + p * 32, 8) for p in range(8)]
        inner = [a1[r, :] for r in rows]
        outer = [e1[r, :] for r in rows]
        for n in range(3):
            (a, b, c), (wx, wy, wz) = block_numbers(meta, row + n, 0, ix, iy)
            back = [(c + t - 1) & 127 for t in range(4)]
            if n == 1:
                w = [jnp.where(((lane - (c + t - 1)) & -128) == 0, wz[t], 0.0) for t in range(4)]
                values = inner
            else:
                lands = upper if n == 2 else jnp.logical_not(upper)
                w = [jnp.where(lands, wz[t], 0.0) for t in range(4)]
                values = [jnp.where(upper if n == 0 else jnp.logical_not(upper), value, 0.0) for value in outer]
            moved = [sum(w[t] * pltpu.roll(value, back[t], 1) for t in range(4)) for value in values]
            scatter_xy(acc, 56, moved, bx * 8 + 7 + a, by * 8 + 7 + b, wx, wy)


    def finish(x):
        first, second = acc[pl.ds(pl.multiple_of((16 + x) * 56 + 16, 8), 16)], a1[pl.ds(pl.multiple_of((8 + x) * 32 + 8, 8), 16)]
        for c in range(3):
            out[c, x] = reg[c, x] + STEP_SIZE * (g[1, c, x].astype(F32) * second + g[0, c, x].astype(F32) * first)

    copies = []
    for h, (first_block, blocks) in enumerate(((0, 12), (12, 4))):
        loop(blocks, lambda i, first_block=first_block: step(first_block + i), blocks)
        loop(8, lambda x, h=h: finish(8 * h + x), 8)
        half = pl.ds(8 * h, 8)
        done = pltpu.make_async_copy(out.at[:, half], result.at[:, half], out_sem.at[h])
        done.start()
        copies.append(done)
    for done in copies:
        done.wait()


def laplace_kernel(v, swap0, swap1, y0, y1, x0, x1, out, w):
    (ylow, yhigh), (xlow, xhigh) = sides("gy", (y0, y1)), sides("gx", (x0, x1))
    lane = lanes(T)
    half = (lane & 4) == 0
    even = is_even("gz")
    (x_low, x_high), (y_low, y_high), (z_low, z_high) = inside("gx"), inside("gy"), inside("gz")
    taps = [-REG_WEIGHT * t for t in LAPLACE_TAPS]
    for c in range(3):
        rows = pl.ds(Z_V + c * T, T)
        a, b = swap0[rows], swap1[rows]
        faces = jnp.where(half, z_high * jnp.where(even, a, b), z_low * jnp.where(even, b, a))
        for i in range(4):
            rows = pl.ds(FACE + (c * 4 + i) * T, T)
            w[i, 8:24] = x_low * xlow[rows]
            w[20 + i, 8:24] = x_high * xhigh[rows]
        for x in range(8):
            rows = pl.ds(Y_FACE + (c * 8 + x) * 8, 8)
            a, b = y_low * ylow[rows], y_high * yhigh[rows]
            w[4 + x, 0:8] = a
            w[12 + x, 0:8] = pltpu.roll(a, 4, 0)
            w[4 + x, 24:32] = b
            w[12 + x, 24:32] = pltpu.roll(b, 4, 0)
        for x in range(T):
            w[4 + x, 8:24] = v[c, x]
        for x in range(T):
            here = v[c, x]
            edge = roll(faces, -8 * x)
            total = 3.0 * taps[0] * here
            for k in range(1, 5):
                near = roll(jnp.where(lane < k, edge, here), -k) + roll(jnp.where(lane >= L - k, edge, here), k)
                near = near + w[4 + x - k, 8:24] + w[4 + x + k, 8:24]
                near = near + w[4 + x, 8 - k : 24 - k] + w[4 + x, 8 + k : 24 + k]
                total = total + taps[k] * near
            out[c, x] = total


VMEM = pl.BlockSpec(memory_space=pltpu.VMEM)
HBM = pl.BlockSpec(memory_space=pltpu.HBM)


def call(kernel, args, outs, scratch=(), hbm=(), cost=20000, alias=None, out_space=None):
    specs = [HBM if i in hbm else VMEM for i in range(len(args))]
    shapes = [jax.ShapeDtypeStruct(s, F32) for s in outs]
    return pl.pallas_call(
        kernel,
        out_shape=shapes,
        in_specs=specs,
        out_specs=[out_space or VMEM] * len(shapes),
        input_output_aliases=alias or {},
        scratch_shapes=list(scratch),
        compiler_params=pltpu.CompilerParams(vmem_limit_bytes=24 * 1024 * 1024),
        cost_estimate=pl.CostEstimate(flops=cost, bytes_accessed=cost, transcendentals=0),
    )(*args)


def last_call(args, vm, meta):
    shape = args[-1].shape
    scratch = [vm(32 * 32, L), vm(32 * 32, L), vm(48 * 56, L), vm(*shape)] + meta + [pltpu.SemaphoreType.DMA((2,))]
    return call(last_step_kernel, args, [shape], scratch=scratch, out_space=HBM)


def swap(first, second, axis):
    n = lax.axis_size(axis)
    pairs = [(i, i + 1 if i % 2 == 0 else i - 1) for i in range(n)]
    others = [(i, i if i in (0, n - 1) else i - 1 if i % 2 == 0 else i + 1) for i in range(n)]
    return lax.ppermute(first, axis, pairs), lax.ppermute(second, axis, others)


def body(velocity, gradients, shift_x, shift_y, shift_z, fractions):
    v, g = velocity, gradients
    tile = (T, T, L)
    vm = lambda *s: pltpu.VMEM(s, F32)
    shifts = [s.transpose(0, 1, 3, 2) for s in (shift_x, shift_y, shift_z)]
    inputs = [v, g, *shifts, fractions.transpose(0, 2, 3, 4, 1)]
    v, s0, s1, z0, z1, *ys = call(
        sources_kernel,
        [pltpu.with_memory_space_constraint(a, pltpu.HBM) for a in inputs],
        [v.shape, tile, tile, (Z_ROWS, L), (Z_ROWS, L), (Y_ROWS, L), (Y_ROWS, L)],
        scratch=[pltpu.VMEM(g.shape, g.dtype)]
        + [pltpu.SMEM((2, 2, 1, 2), jnp.int32)] * 3
        + [pltpu.SMEM((2, 2, 2, 1, 3), jnp.int32), pltpu.SemaphoreType.DMA((8,)), pltpu.SemaphoreType.DMA((4,))],
        hbm=range(6),
    )
    zs = swap(z0, z1, "gz")
    from_y = swap(*ys, "gy")
    *es, x0, x1 = call(
        tile_messages_kernel, (s0, s1, v, z0, *zs, *from_y), [(Y_EROWS, L)] * 2 + [(ROWS, L)] * 2
    )
    from_x = swap(x0, x1, "gx")
    from_e = swap(*es, "gy")
    corners = call(corner_message_kernel, (*from_y, *from_e, *from_x), [(C_ROWS, L)] * 2)
    from_corner = swap(*corners, "gx")
    fields = [(48 * 48, L)] * 2 + [(32 * 32, L)] * 2
    filled = call(assemble_kernel, (x0, x1, *from_x, *from_y, *from_e), fields)
    meta = [pltpu.SMEM((72, L), F32), pltpu.SemaphoreType.DMA]
    sum0, sum1, numbers, *_ = call(
        steps_kernel,
        (x0, *from_x, *from_e, *from_corner, *filled),
        [(R_ROWS, L), (R_ROWS, L), (72, L)] + fields,
        scratch=[vm(32 * 40, L), vm(32 * 40, L)] + meta,
        alias={7: 3, 8: 4, 9: 5, 10: 6},
    )
    (reg,) = call(
        laplace_kernel, (v, *zs, *from_y, *from_x), [v.shape], scratch=[vm(24, 32, L)], cost=4000000
    )
    from_y = swap(sum0, sum1, "gy")
    sums = call(sum_y_kernel, (sum0, sum1, *from_y), [(R_ROWS, L)] * 2)
    from_x = swap(*sums, "gx")
    (out,) = last_call((*sums, *from_x, numbers, g, reg), vm, meta)
    return out


def solution(mesh):
    in_specs = (
        P(None, "gx", "gy", "gz"),
        P(None, None, "gx", "gy", "gz"),
        P(None, "gx", "gy", "gz"),
        P(None, "gx", "gy", "gz"),
        P(None, "gx", "gy", "gz"),
        P(None, None, "gx", "gy", "gz"),
    )
    out_specs = P(None, "gx", "gy", "gz")
    return jax.shard_map(body, mesh=mesh, in_specs=in_specs, out_specs=out_specs, check_vma=False)
```

```python
import jax
import jax.numpy as jnp
from jax import lax
from jax.experimental import pallas as pl
from jax.experimental.pallas import tpu as pltpu
from jax.sharding import PartitionSpec as P

F32 = jnp.float32
LAPLACE_TAPS = (-205.0 / 72.0, 8.0 / 5.0, -1.0 / 5.0, 8.0 / 315.0, -1.0 / 560.0)
STEP_SIZE = 0.5
REG_WEIGHT = 0.1
T = 16
L = 128
UN_ASM, UN_CORNER, UN_FIRST, UN_SECOND, UN_PACK, UN_UNPACK = 8, 16, 16, 4, 8, 4
META = 15

Z_S0, Z_S1, Z_V, Z_META, Z_ROWS = 0, 128, 256, 304, 312
Y_S0, Y_S1, Y_FACE, Y_ROWS = 0, 256, 384, 576
Y_E0, Y_E1, Y_META, Y_EROWS = 0, 256, 384, 392
A0, E0, A1, E1, FACE, NUMBERS, ROWS = 0, 256, 512, 640, 768, 960, 968
C_LOW, C_HIGH, C_A1, C_E1, C_META, C_ROWS = 0, 512, 1024, 1152, 1280, 1296
R_E, R_ROWS = 512, 640


def lanes(rows=8):
    return lax.broadcasted_iota(jnp.int32, (rows, L), 1)


def subs():
    return lax.broadcasted_iota(jnp.int32, (8, L), 0)


def roll(x, amount):
    amount = amount % L
    return x if amount == 0 else pltpu.roll(x, amount, 1)


def block_numbers(meta, row, step, ix, iy):
    at = ((step * 2 + ix) * 2 + iy) * META
    shift = [meta[row, at + d].astype(jnp.int32) for d in range(3)]
    weights = [[meta[row, at + 3 + 4 * d + t] for t in range(4)] for d in range(3)]
    return shift, weights


def loop(count, body, unroll=1):
    def step(i, _):
        body(i)
        return 0

    lax.fori_loop(0, count, step, 0, unroll=unroll)


def inside(axis):
    i, n = lax.axis_index(axis), lax.axis_size(axis)
    return jnp.where(i > 0, 1.0, 0.0).astype(F32), jnp.where(i < n - 1, 1.0, 0.0).astype(F32)


def is_even(axis):
    return lax.axis_index(axis) % 2 == 0


def sources_kernel(
    v_hbm, g_hbm, sx_hbm, sy_hbm, sz_hbm, fr_hbm, v, s0, s1, swap0, swap1, yup, ydown, g, sx, sy, sz, fr, sem, small_sem
):
    copies = []
    for q in range(4):
        part = pl.ds(4 * q, 4)
        copies.append(pltpu.make_async_copy(v_hbm.at[:, part], v.at[:, part], sem.at[2 * q]))
        copies.append(pltpu.make_async_copy(g_hbm.at[:, :, part], g.at[:, :, part], sem.at[2 * q + 1]))
    small = [
        pltpu.make_async_copy(a, b, small_sem.at[n])
        for n, (a, b) in enumerate(((sx_hbm, sx), (sy_hbm, sy), (sz_hbm, sz), (fr_hbm, fr)))
    ]
    for copy in copies + small:
        copy.start()
    lane = lanes(T)
    for x in range(T):
        if x % 4 == 0:
            copies[x // 2].wait()
            copies[x // 2 + 1].wait()
        vel = [v[c, x] for c in range(3)]
        for k, s in ((0, s0), (1, s1)):
            total = g[k, 0, x].astype(F32) * vel[0]
            for c in (1, 2):
                total = total + g[k, c, x].astype(F32) * vel[c]
            value = STEP_SIZE * total
            s[x] = value
            if k == 0:
                yup[pl.ds(Y_S0 + x * T, T)] = value
                ydown[pl.ds(Y_S0 + x * T, T)] = value
            else:
                yup[pl.ds(Y_S1 + x * 8, 8)] = value[8:16]
                ydown[pl.ds(Y_S1 + x * 8, 8)] = value[0:8]
    first_half = subs() < 4
    for c in range(3):
        for x in range(8):
            rows = pl.ds(Y_FACE + (c * 8 + x) * 8, 8)
            yup[rows] = jnp.where(first_half, pltpu.roll(v[c, x + 8, 8:16], 4, 0), v[c, x, 8:16])
            ydown[rows] = jnp.where(first_half, v[c, x, 0:8], pltpu.roll(v[c, x + 8, 0:8], 4, 0))
    even = is_even("gz")
    upper = lane >= 64
    for start, s in ((Z_S0, s0), (Z_S1, s1)):
        for x in range(8):
            rows = pl.ds(start + x * T, T)
            a, b = s[x], roll(s[x + 8], 64)
            u, d = jnp.where(upper, a, b), jnp.where(upper, b, a)
            swap0[rows] = jnp.where(even, u, d)
            swap1[rows] = jnp.where(even, d, u)
    piece = lane // 8
    for c in range(3):
        u, d = v[c, 0], v[c, 0]
        for x in range(1, T):
            r = roll(v[c, x], 8 * x)
            u = jnp.where(piece == (15 + x) % 16, r, u)
            d = jnp.where(piece == x, r, d)
        swap0[pl.ds(Z_V + c * T, T)] = jnp.where(even, u, d)
        swap1[pl.ds(Z_V + c * T, T)] = jnp.where(even, d, u)
    lane = lanes()
    for copy in small:
        copy.wait()
    shifts, eighths = jnp.zeros((8, L), jnp.int32), jnp.zeros((8, L), jnp.int32)
    for k in range(2):
        for ix in range(2):
            for iy in range(2):
                at = ((k * 2 + ix) * 2 + iy) * META
                for n, ref in enumerate((sx, sy, sz)):
                    shifts = jnp.where(lane == at + n, ref[k, ix, 0, iy], shifts)
                    first = at + 3 + 4 * n
                    eighths = jnp.where((lane >= first) & (lane < first + 4), fr[k, ix, iy, 0, n], eighths)
    e = eighths.astype(F32) / 8.0
    e2 = e * e
    e3 = e2 * e
    weights = [
        0.5 * (2.0 * e2 - e3 - e),
        0.5 * (3.0 * e3 - 5.0 * e2 + 2.0),
        0.5 * (4.0 * e2 - 3.0 * e3 + e),
        0.5 * (e3 - e2),
    ]
    place = lane % META
    tap = (place - 3) % 4
    row = jnp.where(tap == 0, weights[0], jnp.where(tap == 1, weights[1], jnp.where(tap == 2, weights[2], weights[3])))
    row = jnp.where(place < 3, shifts.astype(F32), row)
    swap0[pl.ds(Z_META, 8)] = row
    swap1[pl.ds(Z_META, 8)] = row


def tile_messages_kernel(s0, s1, v, own, swap0, swap1, ylow, yhigh, yup, ydown, xup, xdown):
    del ylow, yhigh
    low_in, high_in = inside("gz")
    even = is_even("gz")
    upper = lanes(T) >= 64
    for start, s in ((Z_S0, s0), (Z_S1, s1)):
        for j in range(8):
            a, b = swap0[pl.ds(start + j * T, T)], swap1[pl.ds(start + j * T, T)]
            a, b = low_in * jnp.where(even, b, a), high_in * jnp.where(even, a, b)
            edges = (jnp.where(upper, a, b), roll(jnp.where(upper, b, a), 64))
            for h, edge in enumerate(edges):
                x = j + 8 * h
                if start == Z_S0:
                    for out in (xup, xdown):
                        out[pl.ds(A0 + x * T, T)] = s[x]
                        out[pl.ds(E0 + x * T, T)] = edge
                    for out in (yup, ydown):
                        out[pl.ds(Y_E0 + x * T, T)] = edge
                else:
                    yup[pl.ds(Y_E1 + x * 8, 8)] = edge[8:16]
                    ydown[pl.ds(Y_E1 + x * 8, 8)] = edge[0:8]
                    out = (xdown, xup)[h]
                    out[pl.ds(A1 + j * T, T)] = s[x]
                    out[pl.ds(E1 + j * T, T)] = edge
    for c in range(3):
        for i in range(4):
            xup[pl.ds(FACE + (c * 4 + i) * T, T)] = v[c, 12 + i]
            xdown[pl.ds(FACE + (c * 4 + i) * T, T)] = v[c, i]
    sub = subs()
    a, b = swap0[pl.ds(Z_META, 8)], swap1[pl.ds(Z_META, 8)]
    a, b = low_in * jnp.where(even, b, a), high_in * jnp.where(even, a, b)
    row = jnp.where(sub == 0, a, jnp.where(sub == 1, own[pl.ds(Z_META, 8)], b))
    for out, at in ((yup, Y_META), (ydown, Y_META), (xup, NUMBERS), (xdown, NUMBERS)):
        out[pl.ds(at, 8)] = row


def corner_message_kernel(low, high, elow, ehigh, xlow, xhigh, up, down):
    del xlow, xhigh
    sides = ((low, elow, C_LOW), (high, ehigh, C_HIGH))
    for y, ((a, e, to), keep) in enumerate(zip(sides, inside("gy"))):
        for x in range(T):
            for at, value in ((0, a[pl.ds(Y_S0 + x * T, T)]), (256, e[pl.ds(Y_E0 + x * T, T)])):
                value = keep * value
                up[pl.ds(to + at + x * T, T)] = value
                down[pl.ds(to + at + x * T, T)] = value
        for ref, start, place in ((a, Y_S1, C_A1), (e, Y_E1, C_E1)):
            for x in range(8):
                down[pl.ds(place + x * T + 8 * y, 8)] = keep * ref[pl.ds(start + x * 8, 8)]
                up[pl.ds(place + x * T + 8 * y, 8)] = keep * ref[pl.ds(start + (8 + x) * 8, 8)]
        value = keep * e[pl.ds(Y_META, 8)]
        up[pl.ds(C_META + 8 * y, 8)] = value
        down[pl.ds(C_META + 8 * y, 8)] = value


def put(low, high, rows, upper, a, e):
    low[rows] = jnp.where(upper, e, a)
    high[rows] = jnp.where(upper, a, e)


def assemble_kernel(own_up, own_down, xlow, xhigh, ylow, yhigh, elow, ehigh, c_low, c_high, d_low, d_high):
    (xl, xh), (yl, yh) = inside("gx"), inside("gy")
    upper, upper8 = lanes(T) >= 64, lanes(8) >= 64

    def first(x):
        at = pl.multiple_of(x * T, 8)
        for ref, keep, dx in ((own_up, None, 16), (xlow, xl, 0), (xhigh, xh, 32)):
            a, e = ref[pl.ds(A0 + at, T)], ref[pl.ds(E0 + at, T)]
            if keep is not None:
                a, e = keep * a, keep * e
            put(c_low, c_high, pl.ds(pl.multiple_of((dx + x) * 48 + 16, 8), T), upper, a, e)
        for ref, eref, keep, dy in ((ylow, elow, yl, 0), (yhigh, ehigh, yh, 32)):
            a, e = keep * ref[pl.ds(Y_S0 + at, T)], keep * eref[pl.ds(Y_E0 + at, T)]
            put(c_low, c_high, pl.ds(pl.multiple_of((16 + x) * 48 + dy, 8), T), upper, a, e)

    loop(T, first, UN_ASM)

    def second(x):
        at = pl.multiple_of(x * T, 8)
        for ref, keep, dx in ((own_down, None, 8), (own_up, None, 16), (xlow, xl, 0), (xhigh, xh, 24)):
            a, e = ref[pl.ds(A1 + at, T)], ref[pl.ds(E1 + at, T)]
            if keep is not None:
                a, e = keep * a, keep * e
            put(d_low, d_high, pl.ds(pl.multiple_of((dx + x) * 32 + 8, 8), T), upper, a, e)
        for h in range(2):
            at = pl.multiple_of((8 * h + x) * 8, 8)
            for ref, eref, keep, dy in ((ylow, elow, yl, 0), (yhigh, ehigh, yh, 24)):
                a, e = keep * ref[pl.ds(Y_S1 + at, 8)], keep * eref[pl.ds(Y_E1 + at, 8)]
                put(d_low, d_high, pl.ds(pl.multiple_of((8 + 8 * h + x) * 32 + dy, 8), 8), upper8, a, e)

    loop(8, second, UN_ASM)


def gather_xy(ref, width, x0, y0, wx, wy):
    base = x0 * width + y0
    planes = []
    for i in range(11):
        plane = wy[0] * ref[pl.ds(base + i * width, 8), :]
        for t in range(1, 4):
            plane = plane + wy[t] * ref[pl.ds(base + (i * width + t), 8), :]
        planes.append(plane)
    out = []
    for i in range(8):
        value = wx[0] * planes[i]
        for t in range(1, 4):
            value = value + wx[t] * planes[i + t]
        out.append(value)
    return out


def scatter_xy(ref, width, vals, x0, y0, wx, wy):
    sub = subs()
    base = x0 * width + y0
    places = [pl.ds(base + (p * width + 8 * half), 8) for p in range(11) for half in range(2)]
    low_w = [jnp.where(sub >= t, wy[t], 0.0) for t in range(4)]
    high_w = [jnp.where(sub < t, wy[t], 0.0) for t in range(4)]
    pairs = []
    for value in vals:
        first, second = wy[0] * value, None
        for t in range(1, 4):
            turned = pltpu.roll(value, t, 0)
            first = first + low_w[t] * turned
            second = high_w[t] * turned if second is None else second + high_w[t] * turned
        pairs.append((first, second))
    sums = []
    for p in range(11):
        for half in range(2):
            total = ref[places[len(sums)], :]
            for t in range(4):
                if 0 <= p - t < 8:
                    total = total + wx[t] * pairs[p - t][half]
            sums.append(total)
    for place, total in zip(places, sums):
        ref[place, :] = total


def block_of(b):
    return (b + 1) // 2, (b + 1) % 2


def steps_kernel(
    own, xlow, xhigh, ylow, yhigh, corner_low, corner_high, c_low_in, c_high_in, d_low_in, d_high_in,
    up, down, numbers, c_low, c_high, d_low, d_high, r_low, r_high, meta, sem,
):
    (xl, xh), (yl, yh) = inside("gx"), inside("gy")
    lane = lanes()
    upper = lane >= 64
    tiles = (
        (0, xl * corner_low[pl.ds(C_META, 8)]),
        (8, xl * xlow[pl.ds(NUMBERS, 8)]),
        (16, xl * corner_low[pl.ds(C_META + 8, 8)]),
        (24, yl * ylow[pl.ds(Y_META, 8)]),
        (32, own[pl.ds(NUMBERS, 8)]),
        (40, yh * yhigh[pl.ds(Y_META, 8)]),
        (48, xh * corner_high[pl.ds(C_META, 8)]),
        (56, xh * xhigh[pl.ds(NUMBERS, 8)]),
        (64, xh * corner_high[pl.ds(C_META + 8, 8)]),
    )
    for at, value in tiles:
        numbers[pl.ds(at, 8)] = value
    copy = pltpu.make_async_copy(numbers, meta, sem)
    copy.start()
    upper16 = lanes(T) >= 64

    def corners(x):
        at = pl.multiple_of(x * T, 8)
        for ref, keep, dx in ((corner_low, xl, 0), (corner_high, xh, 32)):
            for start, dy in ((C_LOW, 0), (C_HIGH, 32)):
                a, e = keep * ref[pl.ds(start + at, T)], keep * ref[pl.ds(start + 256 + at, T)]
                put(c_low, c_high, pl.ds(pl.multiple_of((dx + x) * 48 + dy, 8), T), upper16, a, e)

    loop(T, corners, UN_CORNER)

    def corners_second(x):
        at = pl.multiple_of(x * T, 8)
        for ref, keep, dx in ((corner_low, xl, 0), (corner_high, xh, 24)):
            for half, dy in ((0, 0), (8, 24)):
                a, e = keep * ref[pl.ds(C_A1 + half + at, 8)], keep * ref[pl.ds(C_E1 + half + at, 8)]
                put(d_low, d_high, pl.ds(pl.multiple_of((dx + x) * 32 + dy, 8), 8), upper, a, e)

    loop(8, corners_second, UN_CORNER)

    def clear(i):
        rows = pl.ds(pl.multiple_of(i * 128, 8), 128)
        r_low[rows] = jnp.zeros((128, L), F32)
        r_high[rows] = jnp.zeros((128, L), F32)

    loop(10, clear)
    copy.wait()

    def apply(low, high, width, row, step, ix, iy, bx, by):
        places = []
        values = []
        for n in (1, 0, 2):
            (a, b, c), (wx, wy, wz) = block_numbers(meta, row + n, step, ix, iy)
            x0, y0 = bx * 8 + 7 + a, by * 8 + 7 + b
            turns = [(1 - c - t) & 127 for t in range(4)]
            places.append((x0, y0, c, wx, wy, wz))
            if n == 1:
                masks = [jnp.logical_xor(((lane - (c + t - 1)) & -128) == 0, upper) for t in range(4)]
                lows = gather_xy(low, width, x0, y0, wx, wy)
                highs = gather_xy(high, width, x0, y0, wx, wy)
                values.append(
                    [
                        sum(wz[t] * pltpu.roll(jnp.where(masks[t], lows[p], highs[p]), turns[t], 1) for t in range(4))
                        for p in range(8)
                    ]
                )
            else:
                ins = gather_xy(low if n == 0 else high, width, x0, y0, wx, wy)
                values.append([sum(wz[t] * pltpu.roll(value, turns[t], 1) for t in range(4)) for value in ins])
        return places, values

    def first_step(i):
        bx, by = i // 4, i % 4
        (slot_x, ix), (slot_y, iy) = block_of(bx), block_of(by)
        _, (own_z, below, above) = apply(c_low, c_high, 48, slot_x * 24 + slot_y * 8, 0, ix, iy, bx, by)
        for p in range(8):
            rows = pl.ds(pl.multiple_of(bx * 256 + by * 8, 8) + p * 32, 8)
            d_low[rows, :] = d_low[rows, :] + jnp.where(upper, below[p], own_z[p])
            d_high[rows, :] = d_high[rows, :] + jnp.where(upper, own_z[p], above[p])

    loop(16, first_step, UN_FIRST)

    def second_step(i):
        ix, iy = i // 2, i % 2
        places, (own_z, below, above) = apply(d_low, d_high, 32, 32, 1, ix, iy, ix, iy)
        below = [jnp.where(lane >= 96, value, 0.0) for value in below]
        above = [jnp.where(lane < 32, value, 0.0) for value in above]
        x0, y0, c, wx, wy, wz = places[0]
        back = [(c + t - 1) & 127 for t in range(4)]
        masks = [jnp.logical_xor(((lane - (c + t - 1)) & -128) == 0, upper) for t in range(4)]
        low_w = [jnp.where(masks[t], wz[t], 0.0) for t in range(4)]
        high_w = [jnp.where(masks[t], 0.0, wz[t]) for t in range(4)]
        to_low, to_high = [], []
        for value in own_z:
            turned = [pltpu.roll(value, back[t], 1) for t in range(4)]
            to_low.append(sum(low_w[t] * turned[t] for t in range(4)))
            to_high.append(sum(high_w[t] * turned[t] for t in range(4)))
        scatter_xy(r_low, 40, to_low, x0, y0, wx, wy)
        scatter_xy(r_high, 40, to_high, x0, y0, wx, wy)
        for (x0, y0, c, wx, wy, wz), values, ref in ((places[1], below, r_low), (places[2], above, r_high)):
            back = [(c + t - 1) & 127 for t in range(4)]
            moved = [sum(wz[t] * pltpu.roll(value, back[t], 1) for t in range(4)) for value in values]
            scatter_xy(ref, 40, moved, x0, y0, wx, wy)

    loop(4, second_step, UN_SECOND)

    wide = lanes(32)
    wide_upper = wide >= 64
    quarter = ((wide + 16) & 127) // 32

    for h, out in ((0, down), (1, up)):

        def pack(x, h=h, out=out):
            packed = None
            for g in range(4):
                rows = pl.ds(pl.multiple_of((16 * h + 4 * g + x) * 40, 8), 32)
                low, high = r_low[rows], r_high[rows]
                e = roll(jnp.where(wide_upper, low, high), 32 * g)
                packed = e if g == 0 else jnp.where(quarter == g, e, packed)
                out[pl.ds(pl.multiple_of((4 * g + x) * 32, 8), 32)] = jnp.where(wide_upper, high, low)
            out[pl.ds(pl.multiple_of(R_E + x * 32, 8), 32)] = packed

        loop(4, pack, UN_PACK)


def sum_x_kernel(own_up, own_down, low, high, up, down):
    low_in, high_in = inside("gx")
    for h, (mine, other, keep) in enumerate(((own_down, low, low_in), (own_up, high, high_in))):
        for start, planes in ((0, 16), (R_E, 4)):
            for x in range(planes):
                value = mine[pl.ds(start + x * 32, 32)] + keep * other[pl.ds(start + x * 32, 32)]
                rows = pl.ds(start + (h * planes + x) * T, T)
                down[rows] = value[0:16]
                up[rows] = value[16:32]


def last_step_kernel(own_up, own_down, low, high, numbers, g, reg, result, a1, e1, acc, out, meta, sem, out_sem):
    copy = pltpu.make_async_copy(numbers, meta, sem)
    copy.start()
    low_in, high_in = inside("gy")
    wide = lanes(T)
    valid = (wide < 16) | (wide >= 112)

    def unpack(i):
        for mine, other, keep, y in ((own_down, low, low_in, 0), (own_up, high, high_in, T)):
            rows = pl.ds(pl.multiple_of(R_E + i * T, 8), T)
            packed = mine[rows] + keep * other[rows]
            for q in range(4):
                x = 16 * (i // 4) + 4 * q + i % 4
                rows, to = pl.ds(pl.multiple_of(x * T, 8), T), pl.ds(pl.multiple_of(x * 32 + y, 8), T)
                e1[to] = jnp.where(valid, roll(packed, -32 * q), 0.0)
                a1[to] = mine[rows] + keep * other[rows]

    loop(8, unpack, 2 * UN_UNPACK)

    def clear(i):
        acc[pl.ds(pl.multiple_of(i * 168, 8), 168)] = jnp.zeros((168, L), F32)

    loop(16, clear)
    copy.wait()
    lane = lanes()
    upper = lane >= 64

    def step(i):
        bx, by = i // 4, i % 4
        (slot_x, ix), (slot_y, iy) = block_of(bx), block_of(by)
        row = slot_x * 24 + slot_y * 8
        rows = [pl.ds(pl.multiple_of(bx * 256 + by * 8, 8) + p * 32, 8) for p in range(8)]
        inner = [a1[r, :] for r in rows]
        outer = [e1[r, :] for r in rows]
        for n in range(3):
            (a, b, c), (wx, wy, wz) = block_numbers(meta, row + n, 0, ix, iy)
            back = [(c + t - 1) & 127 for t in range(4)]
            if n == 1:
                w = [jnp.where(((lane - (c + t - 1)) & -128) == 0, wz[t], 0.0) for t in range(4)]
                values = inner
            else:
                lands = upper if n == 2 else jnp.logical_not(upper)
                w = [jnp.where(lands, wz[t], 0.0) for t in range(4)]
                values = [jnp.where(upper if n == 0 else jnp.logical_not(upper), value, 0.0) for value in outer]
            moved = [sum(w[t] * pltpu.roll(value, back[t], 1) for t in range(4)) for value in values]
            scatter_xy(acc, 56, moved, bx * 8 + 7 + a, by * 8 + 7 + b, wx, wy)


    def finish(x):
        first, second = acc[pl.ds(pl.multiple_of((16 + x) * 56 + 16, 8), 16)], a1[pl.ds(pl.multiple_of((8 + x) * 32 + 8, 8), 16)]
        for c in range(3):
            out[c, x] = reg[c, x] + STEP_SIZE * (g[1, c, x].astype(F32) * second + g[0, c, x].astype(F32) * first)

    copies = []
    for h, (first_block, blocks) in enumerate(((0, 12), (12, 4))):
        loop(blocks, lambda i, first_block=first_block: step(first_block + i), blocks)
        loop(8, lambda x, h=h: finish(8 * h + x), 8)
        half = pl.ds(8 * h, 8)
        done = pltpu.make_async_copy(out.at[:, half], result.at[:, half], out_sem.at[h])
        done.start()
        copies.append(done)
    for done in copies:
        done.wait()


def laplace_kernel(v, swap0, swap1, ylow, yhigh, xlow, xhigh, out, w):
    lane = lanes(T)
    half = (lane & 4) == 0
    even = is_even("gz")
    (x_low, x_high), (y_low, y_high), (z_low, z_high) = inside("gx"), inside("gy"), inside("gz")
    sides = [-REG_WEIGHT * t for t in LAPLACE_TAPS]
    for c in range(3):
        rows = pl.ds(Z_V + c * T, T)
        a, b = swap0[rows], swap1[rows]
        faces = jnp.where(half, z_high * jnp.where(even, a, b), z_low * jnp.where(even, b, a))
        for i in range(4):
            rows = pl.ds(FACE + (c * 4 + i) * T, T)
            w[i, 8:24] = x_low * xlow[rows]
            w[20 + i, 8:24] = x_high * xhigh[rows]
        for x in range(8):
            rows = pl.ds(Y_FACE + (c * 8 + x) * 8, 8)
            a, b = y_low * ylow[rows], y_high * yhigh[rows]
            w[4 + x, 0:8] = a
            w[12 + x, 0:8] = pltpu.roll(a, 4, 0)
            w[4 + x, 24:32] = b
            w[12 + x, 24:32] = pltpu.roll(b, 4, 0)
        for x in range(T):
            w[4 + x, 8:24] = v[c, x]
        for x in range(T):
            here = v[c, x]
            edge = roll(faces, -8 * x)
            total = 3.0 * sides[0] * here
            for k in range(1, 5):
                near = roll(jnp.where(lane < k, edge, here), -k) + roll(jnp.where(lane >= L - k, edge, here), k)
                near = near + w[4 + x - k, 8:24] + w[4 + x + k, 8:24]
                near = near + w[4 + x, 8 - k : 24 - k] + w[4 + x, 8 + k : 24 + k]
                total = total + sides[k] * near
            out[c, x] = total


VMEM = pl.BlockSpec(memory_space=pltpu.VMEM)
HBM = pl.BlockSpec(memory_space=pltpu.HBM)


def call(kernel, args, outs, scratch=(), hbm=(), cost=20000, alias=None, out_space=None):
    specs = [HBM if i in hbm else VMEM for i in range(len(args))]
    shapes = [jax.ShapeDtypeStruct(s, F32) for s in outs]
    return pl.pallas_call(
        kernel,
        out_shape=shapes,
        in_specs=specs,
        out_specs=[out_space or VMEM] * len(shapes),
        input_output_aliases=alias or {},
        scratch_shapes=list(scratch),
        compiler_params=pltpu.CompilerParams(vmem_limit_bytes=24 * 1024 * 1024),
        cost_estimate=pl.CostEstimate(flops=cost, bytes_accessed=cost, transcendentals=0),
    )(*args)


def exchange(up, down, axis):
    n = lax.axis_size(axis)
    rise = [(i, (i + 1) % n) for i in range(n)]
    fall = [(j, i) for i, j in rise]
    return lax.ppermute(up, axis, rise), lax.ppermute(down, axis, fall)


def last_call(args, vm, meta):
    shape = args[-1].shape
    scratch = [vm(32 * 32, L), vm(32 * 32, L), vm(48 * 56, L), vm(*shape)] + meta + [pltpu.SemaphoreType.DMA((2,))]
    return call(last_step_kernel, args, [shape], scratch=scratch, out_space=HBM)


def swap(first, second, axis):
    n = lax.axis_size(axis)
    pairs = [(i, i + 1 if i % 2 == 0 else i - 1) for i in range(n)]
    others = [(i, i if i in (0, n - 1) else i - 1 if i % 2 == 0 else i + 1) for i in range(n)]
    return lax.ppermute(first, axis, pairs), lax.ppermute(second, axis, others)


def body(velocity, gradients, shift_x, shift_y, shift_z, fractions):
    v, g = velocity, gradients
    tile = (T, T, L)
    vm = lambda *s: pltpu.VMEM(s, F32)
    shifts = [s.transpose(0, 1, 3, 2) for s in (shift_x, shift_y, shift_z)]
    inputs = [v, g, *shifts, fractions.transpose(0, 2, 3, 4, 1)]
    v, s0, s1, first, second, yup, ydown = call(
        sources_kernel,
        [pltpu.with_memory_space_constraint(a, pltpu.HBM) for a in inputs],
        [v.shape, tile, tile, (Z_ROWS, L), (Z_ROWS, L), (Y_ROWS, L), (Y_ROWS, L)],
        scratch=[pltpu.VMEM(g.shape, g.dtype)]
        + [pltpu.SMEM((2, 2, 1, 2), jnp.int32)] * 3
        + [pltpu.SMEM((2, 2, 2, 1, 3), jnp.int32), pltpu.SemaphoreType.DMA((8,)), pltpu.SemaphoreType.DMA((4,))],
        hbm=range(6),
    )
    swap0, swap1 = swap(first, second, "gz")
    ylow, yhigh = exchange(yup, ydown, "gy")
    yup, ydown, xup, xdown = call(
        tile_messages_kernel, (s0, s1, v, first, swap0, swap1, ylow, yhigh), [(Y_EROWS, L)] * 2 + [(ROWS, L)] * 2
    )
    xlow, xhigh = exchange(xup, xdown, "gx")
    elow, ehigh = exchange(yup, ydown, "gy")
    up, down = call(corner_message_kernel, (ylow, yhigh, elow, ehigh, xlow, xhigh), [(C_ROWS, L)] * 2)
    corner_low, corner_high = exchange(up, down, "gx")
    fields = [(48 * 48, L)] * 2 + [(32 * 32, L)] * 2
    filled = call(assemble_kernel, (xup, xdown, xlow, xhigh, ylow, yhigh, elow, ehigh), fields)
    meta = [pltpu.SMEM((72, L), F32), pltpu.SemaphoreType.DMA]
    up, down, numbers, *_ = call(
        steps_kernel,
        (xup, xlow, xhigh, elow, ehigh, corner_low, corner_high, *filled),
        [(R_ROWS, L), (R_ROWS, L), (72, L)] + fields,
        scratch=[vm(32 * 40, L), vm(32 * 40, L)] + meta,
        alias={7: 3, 8: 4, 9: 5, 10: 6},
    )
    (reg,) = call(
        laplace_kernel, (v, swap0, swap1, ylow, yhigh, xlow, xhigh), [v.shape], scratch=[vm(24, 32, L)], cost=4000000
    )
    low, high = exchange(up, down, "gx")
    up, down = call(sum_x_kernel, (up, down, low, high), [(R_ROWS, L)] * 2)
    low, high = exchange(up, down, "gy")
    (out,) = last_call((up, down, low, high, numbers, g, reg), vm, meta)
    return out


def solution(mesh):
    in_specs = (
        P(None, "gx", "gy", "gz"),
        P(None, None, "gx", "gy", "gz"),
        P(None, "gx", "gy", "gz"),
        P(None, "gx", "gy", "gz"),
        P(None, "gx", "gy", "gz"),
        P(None, None, "gx", "gy", "gz"),
    )
    out_specs = P(None, "gx", "gy", "gz")
    return jax.shard_map(body, mesh=mesh, in_specs=in_specs, out_specs=out_specs, check_vma=False)
```

```python
import jax
import jax.numpy as jnp
from jax import lax
from jax.experimental import pallas as pl
from jax.experimental.pallas import tpu as pltpu
from jax.sharding import PartitionSpec as P

F32 = jnp.float32
LAPLACE_TAPS = (-205.0 / 72.0, 8.0 / 5.0, -1.0 / 5.0, 8.0 / 315.0, -1.0 / 560.0)
STEP_SIZE = 0.5
REG_WEIGHT = 0.1
T = 16
L = 128
UN_ASM, UN_CORNER, UN_FIRST, UN_SECOND, UN_PACK, UN_UNPACK = 8, 4, 16, 4, 4, 2
META = 15

Z_S0, Z_S1, Z_V, Z_META, Z_ROWS = 0, 128, 256, 304, 312
Y_S0, Y_S1, Y_FACE, Y_ROWS = 0, 256, 384, 576
Y_E0, Y_E1, Y_META, Y_EROWS = 0, 256, 384, 392
A0, E0, A1, E1, FACE, NUMBERS, ROWS = 0, 256, 512, 640, 768, 960, 968
C_LOW, C_HIGH, C_A1, C_E1, C_META, C_ROWS = 0, 512, 1024, 1152, 1280, 1296
R_E, R_ROWS = 512, 640


def lanes(rows=8):
    return lax.broadcasted_iota(jnp.int32, (rows, L), 1)


def subs():
    return lax.broadcasted_iota(jnp.int32, (8, L), 0)


def roll(x, amount):
    amount = amount % L
    return x if amount == 0 else pltpu.roll(x, amount, 1)


def block_numbers(meta, row, step, ix, iy):
    at = ((step * 2 + ix) * 2 + iy) * META
    shift = [meta[row, at + d].astype(jnp.int32) for d in range(3)]
    weights = [[meta[row, at + 3 + 4 * d + t] for t in range(4)] for d in range(3)]
    return shift, weights


def loop(count, body, unroll=1):
    def step(i, _):
        body(i)
        return 0

    lax.fori_loop(0, count, step, 0, unroll=unroll)


def inside(axis):
    i, n = lax.axis_index(axis), lax.axis_size(axis)
    return jnp.where(i > 0, 1.0, 0.0).astype(F32), jnp.where(i < n - 1, 1.0, 0.0).astype(F32)


def is_even(axis):
    return lax.axis_index(axis) % 2 == 0


def sources_kernel(
    v_hbm, g_hbm, sx_hbm, sy_hbm, sz_hbm, fr_hbm, v, s0, s1, swap0, swap1, yup, ydown, g, sx, sy, sz, fr, sem, small_sem
):
    copies = []
    for q in range(4):
        part = pl.ds(4 * q, 4)
        copies.append(pltpu.make_async_copy(v_hbm.at[:, part], v.at[:, part], sem.at[2 * q]))
        copies.append(pltpu.make_async_copy(g_hbm.at[:, :, part], g.at[:, :, part], sem.at[2 * q + 1]))
    small = [
        pltpu.make_async_copy(a, b, small_sem.at[n])
        for n, (a, b) in enumerate(((sx_hbm, sx), (sy_hbm, sy), (sz_hbm, sz), (fr_hbm, fr)))
    ]
    for copy in copies + small:
        copy.start()
    lane = lanes(T)
    for x in range(T):
        if x % 4 == 0:
            copies[x // 2].wait()
            copies[x // 2 + 1].wait()
        vel = [v[c, x] for c in range(3)]
        for k, s in ((0, s0), (1, s1)):
            total = g[k, 0, x].astype(F32) * vel[0]
            for c in (1, 2):
                total = total + g[k, c, x].astype(F32) * vel[c]
            value = STEP_SIZE * total
            s[x] = value
            if k == 0:
                yup[pl.ds(Y_S0 + x * T, T)] = value
                ydown[pl.ds(Y_S0 + x * T, T)] = value
            else:
                yup[pl.ds(Y_S1 + x * 8, 8)] = value[8:16]
                ydown[pl.ds(Y_S1 + x * 8, 8)] = value[0:8]
    first_half = subs() < 4
    for c in range(3):
        for x in range(8):
            rows = pl.ds(Y_FACE + (c * 8 + x) * 8, 8)
            yup[rows] = jnp.where(first_half, pltpu.roll(v[c, x + 8, 8:16], 4, 0), v[c, x, 8:16])
            ydown[rows] = jnp.where(first_half, v[c, x, 0:8], pltpu.roll(v[c, x + 8, 0:8], 4, 0))
    even = is_even("gz")
    upper = lane >= 64
    for start, s in ((Z_S0, s0), (Z_S1, s1)):
        for x in range(8):
            rows = pl.ds(start + x * T, T)
            a, b = s[x], roll(s[x + 8], 64)
            u, d = jnp.where(upper, a, b), jnp.where(upper, b, a)
            swap0[rows] = jnp.where(even, u, d)
            swap1[rows] = jnp.where(even, d, u)
    piece = lane // 8
    for c in range(3):
        u, d = v[c, 0], v[c, 0]
        for x in range(1, T):
            r = roll(v[c, x], 8 * x)
            u = jnp.where(piece == (15 + x) % 16, r, u)
            d = jnp.where(piece == x, r, d)
        swap0[pl.ds(Z_V + c * T, T)] = jnp.where(even, u, d)
        swap1[pl.ds(Z_V + c * T, T)] = jnp.where(even, d, u)
    lane = lanes()
    for copy in small:
        copy.wait()
    shifts, eighths = jnp.zeros((8, L), jnp.int32), jnp.zeros((8, L), jnp.int32)
    for k in range(2):
        for ix in range(2):
            for iy in range(2):
                at = ((k * 2 + ix) * 2 + iy) * META
                for n, ref in enumerate((sx, sy, sz)):
                    shifts = jnp.where(lane == at + n, ref[k, ix, 0, iy], shifts)
                    first = at + 3 + 4 * n
                    eighths = jnp.where((lane >= first) & (lane < first + 4), fr[k, ix, iy, 0, n], eighths)
    e = eighths.astype(F32) / 8.0
    e2 = e * e
    e3 = e2 * e
    weights = [
        0.5 * (2.0 * e2 - e3 - e),
        0.5 * (3.0 * e3 - 5.0 * e2 + 2.0),
        0.5 * (4.0 * e2 - 3.0 * e3 + e),
        0.5 * (e3 - e2),
    ]
    place = lane % META
    tap = (place - 3) % 4
    row = jnp.where(tap == 0, weights[0], jnp.where(tap == 1, weights[1], jnp.where(tap == 2, weights[2], weights[3])))
    row = jnp.where(place < 3, shifts.astype(F32), row)
    swap0[pl.ds(Z_META, 8)] = row
    swap1[pl.ds(Z_META, 8)] = row


def tile_messages_kernel(s0, s1, v, own, swap0, swap1, ylow, yhigh, yup, ydown, xup, xdown):
    del ylow, yhigh
    low_in, high_in = inside("gz")
    even = is_even("gz")
    upper = lanes(T) >= 64
    for start, s in ((Z_S0, s0), (Z_S1, s1)):
        for j in range(8):
            a, b = swap0[pl.ds(start + j * T, T)], swap1[pl.ds(start + j * T, T)]
            a, b = low_in * jnp.where(even, b, a), high_in * jnp.where(even, a, b)
            edges = (jnp.where(upper, a, b), roll(jnp.where(upper, b, a), 64))
            for h, edge in enumerate(edges):
                x = j + 8 * h
                if start == Z_S0:
                    for out in (xup, xdown):
                        out[pl.ds(A0 + x * T, T)] = s[x]
                        out[pl.ds(E0 + x * T, T)] = edge
                    for out in (yup, ydown):
                        out[pl.ds(Y_E0 + x * T, T)] = edge
                else:
                    yup[pl.ds(Y_E1 + x * 8, 8)] = edge[8:16]
                    ydown[pl.ds(Y_E1 + x * 8, 8)] = edge[0:8]
                    out = (xdown, xup)[h]
                    out[pl.ds(A1 + j * T, T)] = s[x]
                    out[pl.ds(E1 + j * T, T)] = edge
    for c in range(3):
        for i in range(4):
            xup[pl.ds(FACE + (c * 4 + i) * T, T)] = v[c, 12 + i]
            xdown[pl.ds(FACE + (c * 4 + i) * T, T)] = v[c, i]
    sub = subs()
    a, b = swap0[pl.ds(Z_META, 8)], swap1[pl.ds(Z_META, 8)]
    a, b = low_in * jnp.where(even, b, a), high_in * jnp.where(even, a, b)
    row = jnp.where(sub == 0, a, jnp.where(sub == 1, own[pl.ds(Z_META, 8)], b))
    for out, at in ((yup, Y_META), (ydown, Y_META), (xup, NUMBERS), (xdown, NUMBERS)):
        out[pl.ds(at, 8)] = row


def corner_message_kernel(low, high, elow, ehigh, xlow, xhigh, up, down):
    del xlow, xhigh
    sides = ((low, elow, C_LOW), (high, ehigh, C_HIGH))
    for y, ((a, e, to), keep) in enumerate(zip(sides, inside("gy"))):
        for x in range(T):
            for at, value in ((0, a[pl.ds(Y_S0 + x * T, T)]), (256, e[pl.ds(Y_E0 + x * T, T)])):
                value = keep * value
                up[pl.ds(to + at + x * T, T)] = value
                down[pl.ds(to + at + x * T, T)] = value
        for ref, start, place in ((a, Y_S1, C_A1), (e, Y_E1, C_E1)):
            for x in range(8):
                down[pl.ds(place + x * T + 8 * y, 8)] = keep * ref[pl.ds(start + x * 8, 8)]
                up[pl.ds(place + x * T + 8 * y, 8)] = keep * ref[pl.ds(start + (8 + x) * 8, 8)]
        value = keep * e[pl.ds(Y_META, 8)]
        up[pl.ds(C_META + 8 * y, 8)] = value
        down[pl.ds(C_META + 8 * y, 8)] = value


def put(low, high, rows, upper, a, e):
    low[rows] = jnp.where(upper, e, a)
    high[rows] = jnp.where(upper, a, e)


def assemble_kernel(own_up, own_down, xlow, xhigh, ylow, yhigh, elow, ehigh, c_low, c_high, d_low, d_high):
    (xl, xh), (yl, yh) = inside("gx"), inside("gy")
    upper, upper8 = lanes(T) >= 64, lanes(8) >= 64

    def first(x):
        at = pl.multiple_of(x * T, 8)
        for ref, keep, dx in ((own_up, None, 16), (xlow, xl, 0), (xhigh, xh, 32)):
            a, e = ref[pl.ds(A0 + at, T)], ref[pl.ds(E0 + at, T)]
            if keep is not None:
                a, e = keep * a, keep * e
            put(c_low, c_high, pl.ds(pl.multiple_of((dx + x) * 48 + 16, 8), T), upper, a, e)
        for ref, eref, keep, dy in ((ylow, elow, yl, 0), (yhigh, ehigh, yh, 32)):
            a, e = keep * ref[pl.ds(Y_S0 + at, T)], keep * eref[pl.ds(Y_E0 + at, T)]
            put(c_low, c_high, pl.ds(pl.multiple_of((16 + x) * 48 + dy, 8), T), upper, a, e)

    loop(T, first, UN_ASM)

    def second(x):
        at = pl.multiple_of(x * T, 8)
        for ref, keep, dx in ((own_down, None, 8), (own_up, None, 16), (xlow, xl, 0), (xhigh, xh, 24)):
            a, e = ref[pl.ds(A1 + at, T)], ref[pl.ds(E1 + at, T)]
            if keep is not None:
                a, e = keep * a, keep * e
            put(d_low, d_high, pl.ds(pl.multiple_of((dx + x) * 32 + 8, 8), T), upper, a, e)
        for h in range(2):
            at = pl.multiple_of((8 * h + x) * 8, 8)
            for ref, eref, keep, dy in ((ylow, elow, yl, 0), (yhigh, ehigh, yh, 24)):
                a, e = keep * ref[pl.ds(Y_S1 + at, 8)], keep * eref[pl.ds(Y_E1 + at, 8)]
                put(d_low, d_high, pl.ds(pl.multiple_of((8 + 8 * h + x) * 32 + dy, 8), 8), upper8, a, e)

    loop(8, second, UN_ASM)


def gather_xy(ref, width, x0, y0, wx, wy):
    base = x0 * width + y0
    planes = []
    for i in range(11):
        plane = wy[0] * ref[pl.ds(base + i * width, 8), :]
        for t in range(1, 4):
            plane = plane + wy[t] * ref[pl.ds(base + (i * width + t), 8), :]
        planes.append(plane)
    out = []
    for i in range(8):
        value = wx[0] * planes[i]
        for t in range(1, 4):
            value = value + wx[t] * planes[i + t]
        out.append(value)
    return out


def scatter_xy(ref, width, vals, x0, y0, wx, wy):
    sub = subs()
    base = x0 * width + y0
    places = [pl.ds(base + (p * width + 8 * half), 8) for p in range(11) for half in range(2)]
    low_w = [jnp.where(sub >= t, wy[t], 0.0) for t in range(4)]
    high_w = [jnp.where(sub < t, wy[t], 0.0) for t in range(4)]
    pairs = []
    for value in vals:
        first, second = wy[0] * value, None
        for t in range(1, 4):
            turned = pltpu.roll(value, t, 0)
            first = first + low_w[t] * turned
            second = high_w[t] * turned if second is None else second + high_w[t] * turned
        pairs.append((first, second))
    sums = []
    for p in range(11):
        for half in range(2):
            total = ref[places[len(sums)], :]
            for t in range(4):
                if 0 <= p - t < 8:
                    total = total + wx[t] * pairs[p - t][half]
            sums.append(total)
    for place, total in zip(places, sums):
        ref[place, :] = total


def block_of(b):
    return (b + 1) // 2, (b + 1) % 2


def steps_kernel(
    own, xlow, xhigh, ylow, yhigh, corner_low, corner_high, c_low_in, c_high_in, d_low_in, d_high_in,
    up, down, numbers, c_low, c_high, d_low, d_high, r_low, r_high, meta, sem,
):
    (xl, xh), (yl, yh) = inside("gx"), inside("gy")
    lane = lanes()
    upper = lane >= 64
    tiles = (
        (0, xl * corner_low[pl.ds(C_META, 8)]),
        (8, xl * xlow[pl.ds(NUMBERS, 8)]),
        (16, xl * corner_low[pl.ds(C_META + 8, 8)]),
        (24, yl * ylow[pl.ds(Y_META, 8)]),
        (32, own[pl.ds(NUMBERS, 8)]),
        (40, yh * yhigh[pl.ds(Y_META, 8)]),
        (48, xh * corner_high[pl.ds(C_META, 8)]),
        (56, xh * xhigh[pl.ds(NUMBERS, 8)]),
        (64, xh * corner_high[pl.ds(C_META + 8, 8)]),
    )
    for at, value in tiles:
        numbers[pl.ds(at, 8)] = value
    copy = pltpu.make_async_copy(numbers, meta, sem)
    copy.start()
    upper16 = lanes(T) >= 64

    def corners(x):
        at = pl.multiple_of(x * T, 8)
        for ref, keep, dx in ((corner_low, xl, 0), (corner_high, xh, 32)):
            for start, dy in ((C_LOW, 0), (C_HIGH, 32)):
                a, e = keep * ref[pl.ds(start + at, T)], keep * ref[pl.ds(start + 256 + at, T)]
                put(c_low, c_high, pl.ds(pl.multiple_of((dx + x) * 48 + dy, 8), T), upper16, a, e)

    loop(T, corners, UN_CORNER)

    def corners_second(x):
        at = pl.multiple_of(x * T, 8)
        for ref, keep, dx in ((corner_low, xl, 0), (corner_high, xh, 24)):
            for half, dy in ((0, 0), (8, 24)):
                a, e = keep * ref[pl.ds(C_A1 + half + at, 8)], keep * ref[pl.ds(C_E1 + half + at, 8)]
                put(d_low, d_high, pl.ds(pl.multiple_of((dx + x) * 32 + dy, 8), 8), upper, a, e)

    loop(8, corners_second, UN_CORNER)

    def clear(i):
        rows = pl.ds(pl.multiple_of(i * 128, 8), 128)
        r_low[rows] = jnp.zeros((128, L), F32)
        r_high[rows] = jnp.zeros((128, L), F32)

    loop(10, clear)
    copy.wait()

    def apply(low, high, width, row, step, ix, iy, bx, by):
        places = []
        values = []
        for n in (1, 0, 2):
            (a, b, c), (wx, wy, wz) = block_numbers(meta, row + n, step, ix, iy)
            x0, y0 = bx * 8 + 7 + a, by * 8 + 7 + b
            turns = [(1 - c - t) & 127 for t in range(4)]
            places.append((x0, y0, c, wx, wy, wz))
            if n == 1:
                masks = [jnp.logical_xor(((lane - (c + t - 1)) & -128) == 0, upper) for t in range(4)]
                lows = gather_xy(low, width, x0, y0, wx, wy)
                highs = gather_xy(high, width, x0, y0, wx, wy)
                values.append(
                    [
                        sum(wz[t] * pltpu.roll(jnp.where(masks[t], lows[p], highs[p]), turns[t], 1) for t in range(4))
                        for p in range(8)
                    ]
                )
            else:
                ins = gather_xy(low if n == 0 else high, width, x0, y0, wx, wy)
                values.append([sum(wz[t] * pltpu.roll(value, turns[t], 1) for t in range(4)) for value in ins])
        return places, values

    def first_step(i):
        bx, by = i // 4, i % 4
        (slot_x, ix), (slot_y, iy) = block_of(bx), block_of(by)
        _, (own_z, below, above) = apply(c_low, c_high, 48, slot_x * 24 + slot_y * 8, 0, ix, iy, bx, by)
        for p in range(8):
            rows = pl.ds(pl.multiple_of(bx * 256 + by * 8, 8) + p * 32, 8)
            d_low[rows, :] = d_low[rows, :] + jnp.where(upper, below[p], own_z[p])
            d_high[rows, :] = d_high[rows, :] + jnp.where(upper, own_z[p], above[p])

    loop(16, first_step, UN_FIRST)

    def second_step(i):
        ix, iy = i // 2, i % 2
        places, (own_z, below, above) = apply(d_low, d_high, 32, 32, 1, ix, iy, ix, iy)
        below = [jnp.where(lane >= 96, value, 0.0) for value in below]
        above = [jnp.where(lane < 32, value, 0.0) for value in above]
        x0, y0, c, wx, wy, wz = places[0]
        back = [(c + t - 1) & 127 for t in range(4)]
        masks = [jnp.logical_xor(((lane - (c + t - 1)) & -128) == 0, upper) for t in range(4)]
        low_w = [jnp.where(masks[t], wz[t], 0.0) for t in range(4)]
        high_w = [jnp.where(masks[t], 0.0, wz[t]) for t in range(4)]
        to_low, to_high = [], []
        for value in own_z:
            turned = [pltpu.roll(value, back[t], 1) for t in range(4)]
            to_low.append(sum(low_w[t] * turned[t] for t in range(4)))
            to_high.append(sum(high_w[t] * turned[t] for t in range(4)))
        scatter_xy(r_low, 40, to_low, x0, y0, wx, wy)
        scatter_xy(r_high, 40, to_high, x0, y0, wx, wy)
        for (x0, y0, c, wx, wy, wz), values, ref in ((places[1], below, r_low), (places[2], above, r_high)):
            back = [(c + t - 1) & 127 for t in range(4)]
            moved = [sum(wz[t] * pltpu.roll(value, back[t], 1) for t in range(4)) for value in values]
            scatter_xy(ref, 40, moved, x0, y0, wx, wy)

    loop(4, second_step, UN_SECOND)

    wide = lanes(32)
    wide_upper = wide >= 64
    quarter = ((wide + 16) & 127) // 32

    for h, out in ((0, down), (1, up)):

        def pack(x, h=h, out=out):
            packed = None
            for g in range(4):
                rows = pl.ds(pl.multiple_of((16 * h + 4 * g + x) * 40, 8), 32)
                low, high = r_low[rows], r_high[rows]
                e = roll(jnp.where(wide_upper, low, high), 32 * g)
                packed = e if g == 0 else jnp.where(quarter == g, e, packed)
                out[pl.ds(pl.multiple_of((4 * g + x) * 32, 8), 32)] = jnp.where(wide_upper, high, low)
            out[pl.ds(pl.multiple_of(R_E + x * 32, 8), 32)] = packed

        loop(4, pack, UN_PACK)


def sum_x_kernel(own_up, own_down, low, high, up, down):
    low_in, high_in = inside("gx")
    for h, (mine, other, keep) in enumerate(((own_down, low, low_in), (own_up, high, high_in))):
        for start, planes in ((0, 16), (R_E, 4)):
            for x in range(planes):
                value = mine[pl.ds(start + x * 32, 32)] + keep * other[pl.ds(start + x * 32, 32)]
                rows = pl.ds(start + (h * planes + x) * T, T)
                down[rows] = value[0:16]
                up[rows] = value[16:32]


def last_step_kernel(own_up, own_down, low, high, numbers, g, reg, result, a1, e1, acc, out, meta, sem, out_sem):
    copy = pltpu.make_async_copy(numbers, meta, sem)
    copy.start()
    low_in, high_in = inside("gy")
    wide = lanes(T)
    valid = (wide < 16) | (wide >= 112)

    def unpack(i):
        for mine, other, keep, y in ((own_down, low, low_in, 0), (own_up, high, high_in, T)):
            rows = pl.ds(pl.multiple_of(R_E + i * T, 8), T)
            packed = mine[rows] + keep * other[rows]
            for q in range(4):
                x = 16 * (i // 4) + 4 * q + i % 4
                rows, to = pl.ds(pl.multiple_of(x * T, 8), T), pl.ds(pl.multiple_of(x * 32 + y, 8), T)
                e1[to] = jnp.where(valid, roll(packed, -32 * q), 0.0)
                a1[to] = mine[rows] + keep * other[rows]

    loop(8, unpack, 2 * UN_UNPACK)

    def clear(i):
        acc[pl.ds(pl.multiple_of(i * 168, 8), 168)] = jnp.zeros((168, L), F32)

    loop(16, clear)
    copy.wait()
    lane = lanes()
    upper = lane >= 64

    def step(i):
        bx, by = i // 4, i % 4
        (slot_x, ix), (slot_y, iy) = block_of(bx), block_of(by)
        row = slot_x * 24 + slot_y * 8
        rows = [pl.ds(pl.multiple_of(bx * 256 + by * 8, 8) + p * 32, 8) for p in range(8)]
        inner = [a1[r, :] for r in rows]
        outer = [e1[r, :] for r in rows]
        for n in range(3):
            (a, b, c), (wx, wy, wz) = block_numbers(meta, row + n, 0, ix, iy)
            back = [(c + t - 1) & 127 for t in range(4)]
            if n == 1:
                w = [jnp.where(((lane - (c + t - 1)) & -128) == 0, wz[t], 0.0) for t in range(4)]
                values = inner
            else:
                lands = upper if n == 2 else jnp.logical_not(upper)
                w = [jnp.where(lands, wz[t], 0.0) for t in range(4)]
                values = [jnp.where(upper if n == 0 else jnp.logical_not(upper), value, 0.0) for value in outer]
            moved = [sum(w[t] * pltpu.roll(value, back[t], 1) for t in range(4)) for value in values]
            scatter_xy(acc, 56, moved, bx * 8 + 7 + a, by * 8 + 7 + b, wx, wy)


    def finish(x):
        first, second = acc[pl.ds(pl.multiple_of((16 + x) * 56 + 16, 8), 16)], a1[pl.ds(pl.multiple_of((8 + x) * 32 + 8, 8), 16)]
        for c in range(3):
            out[c, x] = reg[c, x] + STEP_SIZE * (g[1, c, x].astype(F32) * second + g[0, c, x].astype(F32) * first)

    copies = []
    for h, (first_block, blocks) in enumerate(((0, 12), (12, 4))):
        loop(blocks, lambda i, first_block=first_block: step(first_block + i), blocks)
        loop(8, lambda x, h=h: finish(8 * h + x), 8)
        half = pl.ds(8 * h, 8)
        done = pltpu.make_async_copy(out.at[:, half], result.at[:, half], out_sem.at[h])
        done.start()
        copies.append(done)
    for done in copies:
        done.wait()


def laplace_kernel(v, swap0, swap1, ylow, yhigh, xlow, xhigh, out, w):
    lane = lanes(T)
    half = (lane & 4) == 0
    even = is_even("gz")
    (x_low, x_high), (y_low, y_high), (z_low, z_high) = inside("gx"), inside("gy"), inside("gz")
    sides = [-REG_WEIGHT * t for t in LAPLACE_TAPS]
    for c in range(3):
        rows = pl.ds(Z_V + c * T, T)
        a, b = swap0[rows], swap1[rows]
        faces = jnp.where(half, z_high * jnp.where(even, a, b), z_low * jnp.where(even, b, a))
        for i in range(4):
            rows = pl.ds(FACE + (c * 4 + i) * T, T)
            w[i, 8:24] = x_low * xlow[rows]
            w[20 + i, 8:24] = x_high * xhigh[rows]
        for x in range(8):
            rows = pl.ds(Y_FACE + (c * 8 + x) * 8, 8)
            a, b = y_low * ylow[rows], y_high * yhigh[rows]
            w[4 + x, 0:8] = a
            w[12 + x, 0:8] = pltpu.roll(a, 4, 0)
            w[4 + x, 24:32] = b
            w[12 + x, 24:32] = pltpu.roll(b, 4, 0)
        for x in range(T):
            w[4 + x, 8:24] = v[c, x]
        for x in range(T):
            here = v[c, x]
            edge = roll(faces, -8 * x)
            total = 3.0 * sides[0] * here
            for k in range(1, 5):
                near = roll(jnp.where(lane < k, edge, here), -k) + roll(jnp.where(lane >= L - k, edge, here), k)
                near = near + w[4 + x - k, 8:24] + w[4 + x + k, 8:24]
                near = near + w[4 + x, 8 - k : 24 - k] + w[4 + x, 8 + k : 24 + k]
                total = total + sides[k] * near
            out[c, x] = total


VMEM = pl.BlockSpec(memory_space=pltpu.VMEM)
HBM = pl.BlockSpec(memory_space=pltpu.HBM)


def call(kernel, args, outs, scratch=(), hbm=(), cost=20000, alias=None, out_space=None):
    specs = [HBM if i in hbm else VMEM for i in range(len(args))]
    shapes = [jax.ShapeDtypeStruct(s, F32) for s in outs]
    return pl.pallas_call(
        kernel,
        out_shape=shapes,
        in_specs=specs,
        out_specs=[out_space or VMEM] * len(shapes),
        input_output_aliases=alias or {},
        scratch_shapes=list(scratch),
        compiler_params=pltpu.CompilerParams(vmem_limit_bytes=24 * 1024 * 1024),
        cost_estimate=pl.CostEstimate(flops=cost, bytes_accessed=cost, transcendentals=0),
    )(*args)


def exchange(up, down, axis):
    n = lax.axis_size(axis)
    rise = [(i, (i + 1) % n) for i in range(n)]
    fall = [(j, i) for i, j in rise]
    return lax.ppermute(up, axis, rise), lax.ppermute(down, axis, fall)


def last_call(args, vm, meta):
    shape = args[-1].shape
    scratch = [vm(32 * 32, L), vm(32 * 32, L), vm(48 * 56, L), vm(*shape)] + meta + [pltpu.SemaphoreType.DMA((2,))]
    return call(last_step_kernel, args, [shape], scratch=scratch, out_space=HBM)


def swap(first, second, axis):
    n = lax.axis_size(axis)
    pairs = [(i, i + 1 if i % 2 == 0 else i - 1) for i in range(n)]
    others = [(i, i if i in (0, n - 1) else i - 1 if i % 2 == 0 else i + 1) for i in range(n)]
    from_other = lax.ppermute(second, axis, others)
    return lax.ppermute(first, axis, pairs), from_other


def body(velocity, gradients, shift_x, shift_y, shift_z, fractions):
    v, g = velocity, gradients
    tile = (T, T, L)
    vm = lambda *s: pltpu.VMEM(s, F32)
    shifts = [s.transpose(0, 1, 3, 2) for s in (shift_x, shift_y, shift_z)]
    inputs = [v, g, *shifts, fractions.transpose(0, 2, 3, 4, 1)]
    v, s0, s1, first, second, yup, ydown = call(
        sources_kernel,
        [pltpu.with_memory_space_constraint(a, pltpu.HBM) for a in inputs],
        [v.shape, tile, tile, (Z_ROWS, L), (Z_ROWS, L), (Y_ROWS, L), (Y_ROWS, L)],
        scratch=[pltpu.VMEM(g.shape, g.dtype)]
        + [pltpu.SMEM((2, 2, 1, 2), jnp.int32)] * 3
        + [pltpu.SMEM((2, 2, 2, 1, 3), jnp.int32), pltpu.SemaphoreType.DMA((8,)), pltpu.SemaphoreType.DMA((4,))],
        hbm=range(6),
    )
    swap0, swap1 = swap(first, second, "gz")
    ylow, yhigh = exchange(yup, ydown, "gy")
    yup, ydown, xup, xdown = call(
        tile_messages_kernel, (s0, s1, v, first, swap0, swap1, ylow, yhigh), [(Y_EROWS, L)] * 2 + [(ROWS, L)] * 2
    )
    xlow, xhigh = exchange(xup, xdown, "gx")
    elow, ehigh = exchange(yup, ydown, "gy")
    up, down = call(corner_message_kernel, (ylow, yhigh, elow, ehigh, xlow, xhigh), [(C_ROWS, L)] * 2)
    corner_low, corner_high = exchange(up, down, "gx")
    fields = [(48 * 48, L)] * 2 + [(32 * 32, L)] * 2
    filled = call(assemble_kernel, (xup, xdown, xlow, xhigh, ylow, yhigh, elow, ehigh), fields)
    meta = [pltpu.SMEM((72, L), F32), pltpu.SemaphoreType.DMA]
    up, down, numbers, *_ = call(
        steps_kernel,
        (xup, xlow, xhigh, elow, ehigh, corner_low, corner_high, *filled),
        [(R_ROWS, L), (R_ROWS, L), (72, L)] + fields,
        scratch=[vm(32 * 40, L), vm(32 * 40, L)] + meta,
        alias={7: 3, 8: 4, 9: 5, 10: 6},
    )
    (reg,) = call(
        laplace_kernel, (v, swap0, swap1, ylow, yhigh, xlow, xhigh), [v.shape], scratch=[vm(24, 32, L)], cost=4000000
    )
    low, high = exchange(up, down, "gx")
    up, down = call(sum_x_kernel, (up, down, low, high), [(R_ROWS, L)] * 2)
    low, high = exchange(up, down, "gy")
    (out,) = last_call((up, down, low, high, numbers, g, reg), vm, meta)
    return out


def solution(mesh):
    in_specs = (
        P(None, "gx", "gy", "gz"),
        P(None, None, "gx", "gy", "gz"),
        P(None, "gx", "gy", "gz"),
        P(None, "gx", "gy", "gz"),
        P(None, "gx", "gy", "gz"),
        P(None, None, "gx", "gy", "gz"),
    )
    out_specs = P(None, "gx", "gy", "gz")
    return jax.shard_map(body, mesh=mesh, in_specs=in_specs, out_specs=out_specs, check_vma=False)
```
